32 devices in a mesh: group: 2 (over y), tile: 16 (over z, x, core).
Axes of the slice: x: 2, y: 2, z: 4, core: 2. Of those that a mesh axis runs over, the one named last changes fastest.
Arguments:
- increment: float32 [32, 221184], P(None, ('group', 'tile')), parts along dimension 1, may hold values from -6 to 6
- send_slots: int32 [110592, 4], P('tile'), may hold values from 0 to 2047, all different within a row; in each aligned block of 6912 rows (0 to 6911, 6912 to 13823, ...) at most 64 rows name the same one
- tent_weight: float32 [4, 110592], P(None, 'tile'), may hold values from 0.05 to 0.5
- coarse_cell: int32 [32768], P('tile'), may hold values from 0 to 3455
- diffusivity: float32 [288, 192], P('tile'), may hold values from 0.04 to 0.24
Outputs:
- result: float32 [32, 221184], P(None, ('group', 'tile')), parts along dimension 1
- coarse_field: float32 [32, 576, 192], P(None, ('group', 'tile')), parts along dimension 1
The draws below stay inside these ranges and needn't reach their ends.
There are 2 independent parts, one for each index of `group`. The reference program is written for one: setup_inputs(seed, part) draws one part's arguments, and reference() takes and returns one part's arrays. A program takes and returns all parts, laid end to end along the dimension named above; an argument that names none is the same for every part. Nothing has to cross between parts.
Inputs may be any that keep to these rules, and one draw needn't show every extreme that they name: `send_slots`: each row names four different slots; among the rows of one device no slot is named by more than 64 rows, a bound that some block reaches; every slot is named by some row.
All inputs are finite; a program needn't handle non-finite values.
Results may differ from the reference program's by a relative error of at most 0.00002.
Values sent between devices are 32-bit elements; how exact they have to be, the bound alone decides.
No kernel may reach another device: no remote copies, remote signals or barrier semaphores. Data moves between devices by JAX's collectives and lax.ppermute only.
A program may use at most 64 MiB of HBM per device.

```python
import math
import jax
import jax.numpy as jnp
import numpy as np

CH = 32
FINE_DEV = 6912
SLOTS = 2048
SLOT_MOST = 64
CAP = 128
NX = 192
STEPS = 5
COARSE_DEV = 3456
NF = 110592
NY = 288
N_TILE = 16


def with_ends(array, own_key, smallest, top_value):
    place = [jax.random.randint(jax.random.fold_in(own_key, axis), (), 0, length) for axis, length in enumerate(array.shape)]
    widest = array.shape.index(max(array.shape))
    neighbour = place[:widest] + [(place[widest] + 1) % array.shape[widest]] + place[widest + 1:]
    return array.at[tuple(place)].set(smallest).at[tuple(neighbour)].set(top_value)


def levels(rng, dims, split, least, top_value):
    loudness = 1.0
    for dim, parts in split:
        heights = jax.random.uniform(jax.random.fold_in(jax.random.fold_in(rng, 6), dim), (parts,), jnp.float32, least / len(split), top_value / len(split))
        loudness = loudness * jnp.repeat(jnp.exp(heights), dims[dim] // parts).reshape((-1,) + (1,) * (len(dims) - 1 - dim))
    return loudness


def shared_out(own_key, own, number, rows, number_of, top, bound, lean):
    order = jax.random.permutation(own_key, number_of)
    packed, common = portions_of(number_of, rows * top, bound, lean, True), portions_of(number_of, rows * top, bound, lean, False)
    places = jnp.arange(number_of)

    def named(sizes, turn):
        used = int((sizes > 0).sum())
        fixed = max(1, used // 4)
        passed = fixed + (places - fixed + turn * (used - fixed)) % max(1, number_of - fixed)
        return jnp.zeros((number_of,), jnp.int32).at[order[jnp.where(places < fixed, places, passed)]].set(jnp.asarray(sizes, jnp.int32))

    sizes = jnp.where(number % 4 == 0, named(packed, number // 4), named(common, number - number // 4 - 1))
    mixed = jax.random.permutation(jax.random.fold_in(own, 3), number_of)
    source_of, receiver = mixed[0:number_of // 2 * 2:2], mixed[1:number_of // 2 * 2:2]
    margin = jnp.minimum(sizes[source_of] - 1, bound - sizes[receiver]) // 2
    margin = jnp.where((source_of == order[0]) | (receiver == order[0]) | (sizes[receiver] == 0), 0, jnp.maximum(margin, 0))
    passed = jax.random.randint(jax.random.fold_in(own, 4), (number_of // 2,), 0, 1 << 20) % (margin + 1)
    sizes = sizes.at[source_of].add(-passed).at[receiver].add(passed)
    labels = jnp.searchsorted(jnp.cumsum(sizes), jnp.arange(rows * top), side="right").astype(jnp.int32)
    table = labels.reshape(top, rows).T
    table = table[jax.random.permutation(jax.random.fold_in(own, 1), rows)]
    turn = jax.random.randint(jax.random.fold_in(own, 2), (rows, 1), 0, top)
    return jnp.take_along_axis(table, (jnp.arange(top)[None, :] + turn) % top, axis=1)


def portions_of(count, total, reach, skew, full):
    loads = [(1 << 20) // math.isqrt(standing ** skew) + 1 for standing in range(1, count + 1)]
    largest = reach if full else min(reach, max(-(-total // count), total * loads[0] // sum(loads)))
    least = 1 if total - largest >= count - 1 else 0
    given, spare = [largest] + [least] * (count - 1), total - largest - least * (count - 1)
    while spare > 0:
        free = [i for i in range(1, count) if given[i] < largest] or [i for i in range(1, count) if given[i] < reach]
        pool, left = sum([loads[i] for i in free]), spare
        for i in free:
            more = min(reach - given[i], max(1, left * loads[i] // pool), spare)
            given[i] = given[i] + more
            spare = spare - more
    return np.array(given)


def normal_values(key, extent, scale, limit, pieces=(), held_as=jnp.bfloat16):
    values = jax.random.normal(key, extent, jnp.float32) * scale
    if len(pieces) > 0:
        values = levels(key, extent, pieces, -0.22, 0.18) * values
    return jnp.clip(values, min=-limit, max=limit).astype(held_as)


def setup_inputs(seed: int = 0, part: int = 0) -> dict:
    streams_of = jax.random.split(jax.random.key(seed), 6)
    part_splits = jax.random.split(jax.random.fold_in(streams_of[5], part), 6)
    increment = normal_values(part_splits[0], (CH, NF), 1.0, 6.0, ((1, 16),), jnp.float32)
    send_slots_keys = jax.random.split(jax.random.fold_in(streams_of[1], 1), NF // FINE_DEV)
    send_slots_turns = jax.random.permutation(jax.random.fold_in(streams_of[1], 3), NF // FINE_DEV)
    send_slots = jax.vmap(lambda own, number: shared_out(jax.random.fold_in(streams_of[1], 2), own, number, FINE_DEV, SLOTS, 4, SLOT_MOST, 2))(send_slots_keys, send_slots_turns).reshape((NF, 4))
    tent_weight = jnp.clip(0.05 + 0.45 * jax.random.uniform(streams_of[2], (4, NF), jnp.float32) ** levels(streams_of[2], (4, NF), ((1, 16),), -0.2, 0.2), 0.05, 0.5)
    coarse_cell = with_ends(jax.random.randint(streams_of[3], (N_TILE * SLOTS,), 0, COARSE_DEV), jax.random.fold_in(streams_of[3], 1), 0, COARSE_DEV - 1).astype(jnp.int32)
    diffusivity = jnp.clip(0.04 + 0.19999999552965164 * jax.random.uniform(streams_of[4], (NY, NX), jnp.float32) ** levels(streams_of[4], (NY, NX), ((0, 16),), -0.2, 0.2), 0.04, 0.24)
    return dict(increment=increment, send_slots=send_slots, tent_weight=tent_weight, coarse_cell=coarse_cell, diffusivity=diffusivity)


def reference(increment, send_slots, tent_weight, coarse_cell, diffusivity):
    nfine = increment.shape[1]
    sender = jnp.arange(nfine, dtype=jnp.int32) // FINE_DEV
    sent = jnp.zeros((CH, N_TILE * SLOTS), jnp.float32)
    for corner in range(4):
        target = (sender * SLOTS + send_slots[:, corner]).astype(jnp.int32)
        sent = sent.at[:, target].add(tent_weight[corner][None, :] * increment)
    received = sent.reshape(CH, N_TILE, N_TILE, CAP).transpose(0, 2, 1, 3).reshape(CH, -1)
    owner = jnp.arange(N_TILE * SLOTS, dtype=jnp.int32) // SLOTS
    cells = (owner * COARSE_DEV + coarse_cell).astype(jnp.int32)
    coarse = jnp.zeros((CH, NY * NX), jnp.float32).at[:, cells].add(received).reshape(CH, NY, NX)
    for turn in range(STEPS):
        spread = jnp.roll(coarse, -1, 1) + jnp.roll(coarse, 1, 1) + jnp.roll(coarse, 1, 2) + jnp.roll(coarse, -1, 2)
        coarse = coarse + diffusivity[None] * (spread - 4.0 * coarse)
    values = coarse.reshape(CH, -1)[:, cells]
    returned = values.reshape(CH, N_TILE, N_TILE, CAP).transpose(0, 2, 1, 3).reshape(CH, -1)
    result = jnp.zeros_like(increment)
    for corner in range(4):
        target = (sender * SLOTS + send_slots[:, corner]).astype(jnp.int32)
        result = result + tent_weight[corner][None, :] * returned[:, target]
    return result, coarse
```

```python
import functools

import jax
import jax.numpy as jnp
from jax import lax
from jax.experimental import pallas as pl
from jax.experimental.pallas import tpu as pltpu
from jax.sharding import PartitionSpec as P

STEPS = 5
CORNERS = 4
LANES = 128
PLACES = 256
BF16 = jnp.bfloat16
F32 = jnp.float32
VMEM = pl.BlockSpec(memory_space=pltpu.VMEM)


def halves(values):
    high = values.astype(BF16)
    return high, (values - high.astype(F32)).astype(BF16)


def one_hot(places, length):
    rows = lax.broadcasted_iota(jnp.int32, (length, places.shape[1]), 0)
    return jnp.where(rows == places, 1.0, 0.0).astype(BF16)


def masked(values, marks, count):
    marks = jnp.broadcast_to(marks, values.shape)
    zero = jnp.zeros((), values.dtype)
    return jnp.concatenate([jnp.where(marks == k, values, zero) for k in range(count)], 0)


def dot_last(left, right):
    return lax.dot_general(left, right, (((1,), (1,)), ((), ())), preferred_element_type=F32)


def sum_to_slots(inc_ref, slot_ref, weight_ref, sent_ref, *, chunk):
    channels, fine = inc_ref.shape
    count = sent_ref.shape[0] * LANES // PLACES
    sent_ref[...] = jnp.zeros_like(sent_ref)

    def step(turn, carry):
        columns = pl.ds(pl.multiple_of(turn * chunk, LANES), chunk)
        inc = inc_ref[:, columns]
        left, right = [], []
        for corner in range(CORNERS):
            slots = slot_ref[corner : corner + 1, columns]
            parts = jnp.concatenate(halves(weight_ref[corner : corner + 1, columns] * inc), 0)
            left.append(masked(parts, slots // PLACES, count))
            right.append(one_hot(slots % PLACES, PLACES))
        sums = dot_last(jnp.concatenate(left, 1), jnp.concatenate(right, 1))
        for k in range(count):
            both = sums[2 * channels * k : 2 * channels * (k + 1)]
            both = both[:channels] + both[channels:]
            for part in range(PLACES // LANES):
                sent_ref[k * (PLACES // LANES) + part] += both[:, LANES * part : LANES * (part + 1)]
        return carry

    lax.fori_loop(0, fine // chunk, step, 0)


def wide_column(width):
    lanes = lax.broadcasted_iota(jnp.int32, (2 * LANES, 1), 0)
    extra = (2 * LANES - width) // 2
    return jnp.where(lanes < width, lanes, jnp.where(lanes < width + extra, lanes - width, lanes - 2 * LANES + width))


def add_to_cells(rec_ref, cell_ref, coarse_ref, head_ref, tail_ref, *, width):
    rows, channels, wide = coarse_ref.shape
    senders = rec_ref.shape[0]
    cells = jnp.concatenate([cell_ref[s : s + 1, :] for s in range(senders)], 1)
    values = jnp.concatenate([rec_ref[s] for s in range(senders)], 1)
    y = cells // width
    right = jnp.where(wide_column(width) == cells - y * width, 1.0, 0.0).astype(BF16)
    left = masked(jnp.concatenate(halves(values), 0), y, rows)
    sums = dot_last(left, right)
    for k in range(rows):
        both = sums[2 * channels * k : 2 * channels * (k + 1)]
        both = both[:channels] + both[channels:]
        coarse_ref[k] = both
        if k < STEPS:
            head_ref[k] = both
        if k >= rows - STEPS:
            tail_ref[k - rows + STEPS] = both


def diffuse_and_read(coarse_ref, before_ref, after_ref, coef_ref, cell_ref, field_ref, values_ref, one_ref, two_ref, *, width):
    rows, channels, wide = coarse_ref.shape
    senders = values_ref.shape[0]
    total = rows + 2 * STEPS
    one_ref[0:STEPS] = before_ref[...]
    one_ref[STEPS : STEPS + rows] = coarse_ref[...]
    one_ref[STEPS + rows : total] = after_ref[...]
    held, other = one_ref, two_ref
    for turn in range(1, STEPS + 1):
        for y in range(turn, total - turn):
            here = held[y]
            spread = held[y + 1] + held[y - 1] + pltpu.roll(here, 1, 1) + pltpu.roll(here, wide - 1, 1)
            other[y] = here + coef_ref[y : y + 1, :] * (spread - 4.0 * here)
        held, other = other, held
    final = held[STEPS : STEPS + rows]
    field_ref[...] = final[:, :, :width]
    left = jnp.concatenate(halves(final.reshape(rows * channels, wide)), 1)
    for s in range(0, senders, 2):
        cells = jnp.concatenate([cell_ref[s : s + 1, :], cell_ref[s + 1 : s + 2, :]], 1)
        y = cells // width
        right = one_hot(cells - y * width, wide)
        found = jnp.dot(left, jnp.concatenate([right, right], 0), preferred_element_type=F32)
        out = jnp.zeros((channels, 2 * LANES), F32)
        marks = jnp.broadcast_to(y, out.shape)
        for k in range(rows):
            out = jnp.where(marks == k, found[channels * k : channels * (k + 1)], out)
        values_ref[s] = out[:, :LANES]
        values_ref[s + 1] = out[:, LANES:]


def sum_from_slots(ret_ref, slot_ref, weight_ref, result_ref, table_ref, *, chunk):
    channels, fine = result_ref.shape
    count = ret_ref.shape[0] * LANES // PLACES
    group = PLACES // LANES
    for k in range(count):
        high, low = halves(jnp.concatenate([ret_ref[group * k + part] for part in range(group)], 1))
        table_ref[channels * k : channels * (k + 1), :PLACES] = high
        table_ref[channels * k : channels * (k + 1), PLACES:] = low

    def step(turn, carry):
        columns = pl.ds(pl.multiple_of(turn * chunk, LANES), chunk)
        total = jnp.zeros((channels, chunk), F32)
        for corner in range(CORNERS):
            slots = slot_ref[corner : corner + 1, columns]
            right = one_hot(slots % PLACES, PLACES)
            found = jnp.dot(table_ref[...], jnp.concatenate([right, right], 0), preferred_element_type=F32)
            marks = jnp.broadcast_to(slots // PLACES, total.shape)
            out = found[:channels]
            for k in range(1, count):
                out = jnp.where(marks == k, found[channels * k : channels * (k + 1)], out)
            total = total + weight_ref[corner : corner + 1, columns] * out
        result_ref[:, columns] = total
        return carry

    lax.fori_loop(0, fine // chunk, step, 0)


def chunk_of(fine, most):
    return max(c for c in range(LANES, most + 1, LANES) if fine % c == 0)


def call(kernel, out, scratch=()):
    return pl.pallas_call(
        kernel,
        out_shape=out,
        scratch_shapes=list(scratch),
        compiler_params=pltpu.CompilerParams(vmem_limit_bytes=48 << 20),
    )


def body(increment, send_slots, tent_weight, coarse_cell, diffusivity):
    channels, fine = increment.shape
    slot_count = coarse_cell.shape[0]
    rows, width = diffusivity.shape
    tiles = lax.axis_size("tile")
    share = slot_count // tiles
    blocks = slot_count // LANES
    wide = 2 * LANES
    ahead = [(i, (i + 1) % tiles) for i in range(tiles)]
    back = [((i + 1) % tiles, i) for i in range(tiles)]
    shape = jax.ShapeDtypeStruct
    slots = send_slots.T
    cells = coarse_cell.reshape(blocks, LANES)

    extra = (wide - width) // 2
    coef = jnp.concatenate([diffusivity, diffusivity[:, :extra], diffusivity[:, width - extra :]], 1)
    coef = jnp.concatenate(
        [lax.ppermute(coef[rows - STEPS :], "tile", ahead), coef, lax.ppermute(coef[:STEPS], "tile", back)], 0
    )

    sent = call(functools.partial(sum_to_slots, chunk=chunk_of(fine, 2304)), shape((blocks, channels, LANES), F32))(
        increment, slots, tent_weight
    )
    received = exchange(sent, tiles, share)
    coarse, head, tail = call(
        functools.partial(add_to_cells, width=width),
        [
            shape((rows, channels, wide), F32),
            shape((STEPS, channels, wide), F32),
            shape((STEPS, channels, wide), F32),
        ],
    )(received, cells)
    before = lax.ppermute(tail, "tile", ahead)
    after = lax.ppermute(head, "tile", back)
    padded = pltpu.VMEM((rows + 2 * STEPS, channels, wide), F32)
    field, values = call(
        functools.partial(diffuse_and_read, width=width),
        [shape((rows, channels, width), F32), shape((blocks, channels, LANES), F32)],
        [padded, padded],
    )(coarse, before, after, coef, cells)
    returned = exchange(values, tiles, share)
    result = call(
        functools.partial(sum_from_slots, chunk=chunk_of(fine, 768)),
        shape((channels, fine), F32),
        [pltpu.VMEM((channels * slot_count // PLACES, 2 * PLACES), BF16)],
    )(returned, slots, tent_weight)
    return (result, field.transpose(1, 0, 2))


def exchange(blocks, tiles, share):
    count, channels, lanes = blocks.shape
    if share == lanes:
        return lax.all_to_all(blocks, "tile", split_axis=0, concat_axis=0, tiled=True)
    flat = blocks.transpose(1, 0, 2).reshape(channels, count * lanes)
    flat = lax.all_to_all(flat, "tile", split_axis=1, concat_axis=1, tiled=True)
    return flat.reshape(channels, count, lanes).transpose(1, 0, 2)


def solution(mesh):
    in_specs = (
        P(None, ("group", "tile")),
        P("tile", None),
        P(None, "tile"),
        P("tile"),
        P("tile", None),
    )
    out_specs = (P(None, ("group", "tile")), P(None, ("group", "tile"), None))
    return jax.shard_map(body, mesh=mesh, in_specs=in_specs, out_specs=out_specs, check_vma=False)
```

```python
import functools

import jax
import jax.numpy as jnp
from jax import lax
from jax.experimental import pallas as pl
from jax.experimental.pallas import tpu as pltpu
from jax.sharding import PartitionSpec as P

STEPS = 5
CORNERS = 4
LANES = 128
PLACES = 256
EDGE = STEPS + (STEPS + 1) // 2
BF16 = jnp.bfloat16
F32 = jnp.float32
VMEM = pl.BlockSpec(memory_space=pltpu.VMEM)


def halves(values):
    high = values.astype(BF16)
    return high, (values - high.astype(F32)).astype(BF16)


def one_hot(places, length):
    rows = lax.broadcasted_iota(jnp.int32, (length, places.shape[1]), 0)
    return jnp.where(rows == places, 1.0, 0.0).astype(BF16)


def masked(values, marks, count):
    marks = jnp.broadcast_to(marks, values.shape)
    zero = jnp.zeros((), values.dtype)
    return jnp.concatenate([jnp.where(marks == k, values, zero) for k in range(count)], 0)


def dot_last(left, right):
    return lax.dot_general(left, right, (((1,), (1,)), ((), ())), preferred_element_type=F32)


def sum_to_slots(inc_ref, slot_ref, weight_ref, sent_ref):
    channels = inc_ref.shape[0]
    count = sent_ref.shape[0] * LANES // PLACES
    inc = inc_ref[...]
    left, right = [], []
    for corner in range(CORNERS):
        slots = slot_ref[corner : corner + 1, :]
        parts = jnp.concatenate(halves(weight_ref[corner : corner + 1, :] * inc), 0)
        left.append(masked(parts, slots // PLACES, count))
        right.append(one_hot(slots % PLACES, PLACES))
    sums = dot_last(jnp.concatenate(left, 1), jnp.concatenate(right, 1))

    @pl.when(pl.program_id(0) == 0)
    def _():
        sent_ref[...] = jnp.zeros_like(sent_ref)

    for k in range(count):
        both = sums[2 * channels * k : 2 * channels * (k + 1)]
        both = both[:channels] + both[channels:]
        for part in range(PLACES // LANES):
            sent_ref[k * (PLACES // LANES) + part] += both[:, LANES * part : LANES * (part + 1)]


def wide_column(width):
    lanes = lax.broadcasted_iota(jnp.int32, (2 * LANES, 1), 0)
    extra = (2 * LANES - width) // 2
    return jnp.where(lanes < width, lanes, jnp.where(lanes < width + extra, lanes - width, lanes - 2 * LANES + width))


def place_edge(edge_ref, rows, coefs, width):
    half = width - LANES
    for k, row in enumerate(rows):
        edge_ref[k] = row[:, :LANES]
    ends = [row[:, LANES:width] for row in rows]
    for k in range(0, STEPS - 1, 2):
        edge_ref[STEPS + k // 2] = jnp.concatenate([ends[k], ends[k + 1]], 1)
    edge_ref[EDGE - 1] = jnp.concatenate([ends[-1], jnp.zeros_like(ends[-1])], 1)
    for k, coef in enumerate(coefs):
        for part in range(3):
            edge_ref[EDGE - 1, 3 * k + part : 3 * k + part + 1, half:] = coef[:, half * part : half * (part + 1)]


def read_edge(edge_ref, k, width):
    half = width - LANES
    start = edge_ref[k]
    end = edge_ref[STEPS + k // 2, :, half * (k % 2) : half * (k % 2) + half]
    return widened([start, end], start, end, width)


def read_coef(edge_ref, k, width):
    half = width - LANES
    parts = [edge_ref[EDGE - 1, 3 * k + part : 3 * k + part + 1, half:] for part in range(3)]
    return widened(parts, parts[0], parts[2], width)


def widened(parts, start, end, width):
    extra = (2 * LANES - width) // 2
    return jnp.concatenate(parts + [start[:, :extra], end[:, end.shape[1] - extra :]], 1)


def add_to_cells(rec_ref, cell_ref, coef_ref, coarse_ref, head_ref, tail_ref, *, width):
    rows, channels, wide = coarse_ref.shape
    senders = rec_ref.shape[0]
    cells = jnp.concatenate([cell_ref[s : s + 1, :] for s in range(senders)], 1)
    values = jnp.concatenate([rec_ref[s] for s in range(senders)], 1)
    y = cells // width
    right = jnp.where(wide_column(width) == cells - y * width, 1.0, 0.0).astype(BF16)
    left = masked(jnp.concatenate(halves(values), 0), y, rows)
    sums = dot_last(left, right)
    full = []
    for k in range(rows):
        both = sums[2 * channels * k : 2 * channels * (k + 1)]
        both = both[:channels] + both[channels:]
        coarse_ref[k] = both
        full.append(both)
    coefs = [coef_ref[k : k + 1, :] for k in range(rows)]
    place_edge(head_ref, full[:STEPS], coefs[:STEPS], width)
    place_edge(tail_ref, full[rows - STEPS :], coefs[rows - STEPS :], width)


def diffuse_and_read(
    coarse_ref, before_ref, after_ref, own_ref, cell_ref, field_ref, values_ref, one_ref, two_ref, coef_ref, *, width
):
    rows, channels, wide = coarse_ref.shape
    senders = values_ref.shape[0]
    total = rows + 2 * STEPS
    own = own_ref[...]
    coef_ref[STEPS : STEPS + rows, :] = widened([own], own, own, width)
    one_ref[STEPS : STEPS + rows] = coarse_ref[...]
    for k in range(STEPS):
        one_ref[k] = read_edge(before_ref, k, width)
        one_ref[STEPS + rows + k] = read_edge(after_ref, k, width)
        coef_ref[k : k + 1, :] = read_coef(before_ref, k, width)
        coef_ref[STEPS + rows + k : STEPS + rows + k + 1, :] = read_coef(after_ref, k, width)
    held, other = one_ref, two_ref
    for turn in range(1, STEPS + 1):
        for y in range(turn, total - turn):
            here = held[y]
            spread = held[y + 1] + held[y - 1] + pltpu.roll(here, 1, 1) + pltpu.roll(here, wide - 1, 1)
            other[y] = here + coef_ref[y : y + 1, :] * (spread - 4.0 * here)
        held, other = other, held
    final = held[STEPS : STEPS + rows]
    field_ref[...] = final[:, :, :width]
    left = jnp.concatenate(halves(final.reshape(rows * channels, wide)), 1)
    for s in range(0, senders, 2):
        cells = jnp.concatenate([cell_ref[s : s + 1, :], cell_ref[s + 1 : s + 2, :]], 1)
        y = cells // width
        right = one_hot(cells - y * width, wide)
        found = jnp.dot(left, jnp.concatenate([right, right], 0), preferred_element_type=F32)
        out = jnp.zeros((channels, 2 * LANES), F32)
        marks = jnp.broadcast_to(y, out.shape)
        for k in range(rows):
            out = jnp.where(marks == k, found[channels * k : channels * (k + 1)], out)
        values_ref[s] = out[:, :LANES]
        values_ref[s + 1] = out[:, LANES:]


def by_product(table_ref, slot_ref, weight_ref, columns, channels):
    count = table_ref.shape[0] // (2 * channels)
    total = 0.0
    for corner in range(CORNERS):
        slots = slot_ref[corner : corner + 1, columns]
        found = jnp.dot(table_ref[...], one_hot(slots % PLACES, PLACES), preferred_element_type=F32)
        marks = jnp.broadcast_to(slots // PLACES, (channels, slots.shape[1]))
        out = None
        for k in range(count):
            both = found[2 * channels * k : 2 * channels * (k + 1)]
            both = both[:channels] + both[channels:]
            out = both if out is None else jnp.where(marks == k, both, out)
        total = total + weight_ref[corner : corner + 1, columns] * out
    return total


def by_lanes(ret_ref, slot_ref, weight_ref, columns):
    blocks, channels, _ = ret_ref.shape
    group = 8
    totals = [0.0] * (channels // group)
    for corner in range(CORNERS):
        slots = slot_ref[corner : corner + 1, columns]
        weight = weight_ref[corner : corner + 1, columns]
        lanes = jnp.broadcast_to(slots % LANES, (group, LANES))
        block = jnp.broadcast_to(slots // LANES, (group, LANES))
        marks = [block == k for k in range(blocks)]
        for c in range(channels // group):
            out = None
            for k in range(blocks):
                found = jnp.take_along_axis(ret_ref[k, group * c : group * (c + 1), :], lanes, axis=1)
                out = found if out is None else jnp.where(marks[k], found, out)
            totals[c] = totals[c] + weight * out
    return jnp.concatenate(totals, 0)


def sum_from_slots(ret_ref, slot_ref, weight_ref, result_ref, table_ref, *, plan):
    blocks, channels, _ = ret_ref.shape
    group = PLACES // LANES

    @pl.when(pl.program_id(0) == 0)
    def _():
        for k in range(blocks // group):
            both = halves(jnp.concatenate([ret_ref[group * k + part] for part in range(group)], 1))
            table_ref[2 * channels * k : 2 * channels * (k + 1), :] = jnp.concatenate(both, 0)

    at = 0
    for product, single in plan:
        columns = slice(at, at + product * LANES)
        result_ref[:, columns] = by_product(table_ref, slot_ref, weight_ref, columns, channels)
        for k in range(product, product + single):
            columns = slice(at + k * LANES, at + (k + 1) * LANES)
            result_ref[:, columns] = by_lanes(ret_ref, slot_ref, weight_ref, columns)
        at += (product + single) * LANES


def plan_of(blocks):
    turns = max(t for t in (3, 2, 1) if blocks % t == 0)
    size = blocks // turns
    return [(size - size // 3, size // 3)] * turns


def chunk_of(fine, most):
    return max(c for c in range(LANES, most + 1, LANES) if fine % c == 0)


def call(kernel, ins, out, scratch=(), grid=(), in_specs=VMEM, out_specs=VMEM):
    single = isinstance(in_specs, pl.BlockSpec)
    return pl.pallas_call(
        kernel,
        grid=grid,
        out_shape=out,
        in_specs=[in_specs] * len(ins) if single else in_specs,
        out_specs=[out_specs] * len(out) if isinstance(out, list) else out_specs,
        scratch_shapes=list(scratch),
        compiler_params=pltpu.CompilerParams(vmem_limit_bytes=56 << 20),
    )(*ins)


def body(increment, send_slots, tent_weight, coarse_cell, diffusivity):
    channels, fine = increment.shape
    slot_count = coarse_cell.shape[0]
    rows, width = diffusivity.shape
    tiles = lax.axis_size("tile")
    share = slot_count // tiles
    blocks = slot_count // LANES
    wide = 2 * LANES
    ahead = [(i, (i + 1) % tiles) for i in range(tiles)]
    back = [((i + 1) % tiles, i) for i in range(tiles)]
    shape = jax.ShapeDtypeStruct
    slots = send_slots.T
    cells = coarse_cell.reshape(blocks, LANES)
    chunk = chunk_of(fine, 2304)
    grid = (fine // chunk,)
    part = lambda n: pl.BlockSpec((n, chunk), lambda i: (0, i))
    whole = pl.BlockSpec((blocks, channels, LANES), lambda i: (0, 0, 0))

    sent = call(
        sum_to_slots,
        (increment, slots, tent_weight),
        shape((blocks, channels, LANES), F32),
        grid=grid,
        in_specs=[part(channels), part(CORNERS), part(CORNERS)],
        out_specs=whole,
    )
    received = exchange(sent, tiles, share)
    edge = shape((EDGE, channels, LANES), F32)
    coarse, head, tail = call(
        functools.partial(add_to_cells, width=width),
        (received, cells, diffusivity),
        [shape((rows, channels, wide), F32), edge, edge],
    )
    before = lax.ppermute(tail, "tile", ahead)
    after = lax.ppermute(head, "tile", back)
    padded = pltpu.VMEM((rows + 2 * STEPS, channels, wide), F32)
    field, values = call(
        functools.partial(diffuse_and_read, width=width),
        (coarse, before, after, diffusivity, cells),
        [shape((rows, channels, width), F32), shape((blocks, channels, LANES), F32)],
        [padded, padded, pltpu.VMEM((rows + 2 * STEPS, wide), F32)],
    )
    returned = exchange(values, tiles, share)
    result = call(
        functools.partial(sum_from_slots, plan=plan_of(chunk // LANES)),
        (returned, slots, tent_weight),
        shape((channels, fine), F32),
        [pltpu.VMEM((2 * channels * slot_count // PLACES, PLACES), BF16)],
        grid=grid,
        in_specs=[whole, part(CORNERS), part(CORNERS)],
        out_specs=part(channels),
    )
    return (result, field.transpose(1, 0, 2))


def exchange(blocks, tiles, share):
    count, channels, lanes = blocks.shape
    if share == lanes:
        return lax.all_to_all(blocks, "tile", split_axis=0, concat_axis=0, tiled=True)
    flat = blocks.transpose(1, 0, 2).reshape(channels, count * lanes)
    flat = lax.all_to_all(flat, "tile", split_axis=1, concat_axis=1, tiled=True)
    return flat.reshape(channels, count, lanes).transpose(1, 0, 2)


def solution(mesh):
    in_specs = (
        P(None, ("group", "tile")),
        P("tile", None),
        P(None, "tile"),
        P("tile"),
        P("tile", None),
    )
    out_specs = (P(None, ("group", "tile")), P(None, ("group", "tile"), None))
    return jax.shard_map(body, mesh=mesh, in_specs=in_specs, out_specs=out_specs, check_vma=False)
```

```python
import functools

import jax
import jax.numpy as jnp
from jax import lax
from jax.experimental import pallas as pl
from jax.experimental.pallas import tpu as pltpu
from jax.sharding import PartitionSpec as P

STEPS = 5
CORNERS = 4
LANES = 128
PLACES = 256
EDGE = STEPS + (STEPS + 1) // 2
BF16 = jnp.bfloat16
F32 = jnp.float32
VMEM = pl.BlockSpec(memory_space=pltpu.VMEM)


def halves(values):
    high = values.astype(BF16)
    return high, (values - high.astype(F32)).astype(BF16)


def one_hot(places, length):
    rows = lax.broadcasted_iota(jnp.int32, (length, places.shape[1]), 0)
    return jnp.where(rows == places, 1.0, 0.0).astype(BF16)


def masked(values, marks, count):
    marks = jnp.broadcast_to(marks, values.shape)
    zero = jnp.zeros((), values.dtype)
    return jnp.concatenate([jnp.where(marks == k, values, zero) for k in range(count)], 0)


def dot_last(left, right):
    return lax.dot_general(left, right, (((1,), (1,)), ((), ())), preferred_element_type=F32)


def sum_to_slots(inc_ref, slot_ref, weight_ref, sent_ref):
    channels = inc_ref.shape[0]
    count = sent_ref.shape[0] * LANES // PLACES
    inc = inc_ref[...]
    left, right = [], []
    for corner in range(CORNERS):
        slots = slot_ref[corner : corner + 1, :]
        parts = jnp.concatenate(halves(weight_ref[corner : corner + 1, :] * inc), 0)
        left.append(masked(parts, slots // PLACES, count))
        right.append(one_hot(slots % PLACES, PLACES))
    sums = dot_last(jnp.concatenate(left, 1), jnp.concatenate(right, 1))

    @pl.when(pl.program_id(0) == 0)
    def _():
        sent_ref[...] = jnp.zeros_like(sent_ref)

    for k in range(count):
        both = sums[2 * channels * k : 2 * channels * (k + 1)]
        both = both[:channels] + both[channels:]
        for part in range(PLACES // LANES):
            sent_ref[k * (PLACES // LANES) + part] += both[:, LANES * part : LANES * (part + 1)]


def wide_column(width):
    lanes = lax.broadcasted_iota(jnp.int32, (2 * LANES, 1), 0)
    extra = (2 * LANES - width) // 2
    return jnp.where(lanes < width, lanes, jnp.where(lanes < width + extra, lanes - width, lanes - 2 * LANES + width))


def place_edge(edge_ref, rows, coefs, width):
    half = width - LANES
    for k, row in enumerate(rows):
        edge_ref[k] = row[:, :LANES]
    ends = [row[:, LANES:width] for row in rows]
    for k in range(0, STEPS - 1, 2):
        edge_ref[STEPS + k // 2] = jnp.concatenate([ends[k], ends[k + 1]], 1)
    edge_ref[EDGE - 1] = jnp.concatenate([ends[-1], jnp.zeros_like(ends[-1])], 1)
    for k, coef in enumerate(coefs):
        for part in range(3):
            edge_ref[EDGE - 1, 3 * k + part : 3 * k + part + 1, half:] = coef[:, half * part : half * (part + 1)]


def read_edge(edge_ref, k, width):
    half = width - LANES
    start = edge_ref[k]
    end = edge_ref[STEPS + k // 2, :, half * (k % 2) : half * (k % 2) + half]
    return widened([start, end], start, end, width)


def read_coef(edge_ref, k, width):
    half = width - LANES
    parts = [edge_ref[EDGE - 1, 3 * k + part : 3 * k + part + 1, half:] for part in range(3)]
    return widened(parts, parts[0], parts[2], width)


def widened(parts, start, end, width):
    extra = (2 * LANES - width) // 2
    return jnp.concatenate(parts + [start[:, :extra], end[:, end.shape[1] - extra :]], 1)


def add_to_cells(rec_ref, cell_ref, coef_ref, coarse_ref, head_ref, tail_ref, *, width):
    rows, channels, wide = coarse_ref.shape
    senders = rec_ref.shape[0]
    cells = jnp.concatenate([cell_ref[s : s + 1, :] for s in range(senders)], 1)
    values = jnp.concatenate([rec_ref[s] for s in range(senders)], 1)
    y = cells // width
    right = jnp.where(wide_column(width) == cells - y * width, 1.0, 0.0).astype(BF16)
    left = masked(jnp.concatenate(halves(values), 0), y, rows)
    sums = dot_last(left, right)
    full = []
    for k in range(rows):
        both = sums[2 * channels * k : 2 * channels * (k + 1)]
        both = both[:channels] + both[channels:]
        coarse_ref[k] = both
        full.append(both)
    coefs = [coef_ref[k : k + 1, :] for k in range(rows)]
    place_edge(head_ref, full[:STEPS], coefs[:STEPS], width)
    place_edge(tail_ref, full[rows - STEPS :], coefs[rows - STEPS :], width)


def diffuse_and_read(
    coarse_ref, before_ref, after_ref, own_ref, cell_ref, field_ref, values_ref, one_ref, two_ref, coef_ref, *, width
):
    rows, channels, wide = coarse_ref.shape
    senders = values_ref.shape[0]
    total = rows + 2 * STEPS
    own = own_ref[...]
    coef_ref[STEPS : STEPS + rows, :] = widened([own], own, own, width)
    one_ref[STEPS : STEPS + rows] = coarse_ref[...]
    for k in range(STEPS):
        one_ref[k] = read_edge(before_ref, k, width)
        one_ref[STEPS + rows + k] = read_edge(after_ref, k, width)
        coef_ref[k : k + 1, :] = read_coef(before_ref, k, width)
        coef_ref[STEPS + rows + k : STEPS + rows + k + 1, :] = read_coef(after_ref, k, width)
    held, other = one_ref, two_ref
    for turn in range(1, STEPS + 1):
        for y in range(turn, total - turn):
            here = held[y]
            spread = held[y + 1] + held[y - 1] + pltpu.roll(here, 1, 1) + pltpu.roll(here, wide - 1, 1)
            other[y] = here + coef_ref[y : y + 1, :] * (spread - 4.0 * here)
        held, other = other, held
    final = held[STEPS : STEPS + rows]
    field_ref[...] = final[:, :, :width]
    left = jnp.concatenate(halves(final.reshape(rows * channels, wide)), 1)
    for s in range(0, senders, 2):
        cells = jnp.concatenate([cell_ref[s : s + 1, :], cell_ref[s + 1 : s + 2, :]], 1)
        y = cells // width
        right = one_hot(cells - y * width, wide)
        found = jnp.dot(left, jnp.concatenate([right, right], 0), preferred_element_type=F32)
        out = jnp.zeros((channels, 2 * LANES), F32)
        marks = jnp.broadcast_to(y, out.shape)
        for k in range(rows):
            out = jnp.where(marks == k, found[channels * k : channels * (k + 1)], out)
        values_ref[s] = out[:, :LANES]
        values_ref[s + 1] = out[:, LANES:]


def by_product(table_ref, slot_ref, weight_ref, columns, channels):
    count = table_ref.shape[0] // (2 * channels)
    total = 0.0
    for corner in range(CORNERS):
        slots = slot_ref[corner : corner + 1, columns]
        found = jnp.dot(table_ref[...], one_hot(slots % PLACES, PLACES), preferred_element_type=F32)
        marks = jnp.broadcast_to(slots // PLACES, (channels, slots.shape[1]))
        out = None
        for k in range(count):
            both = found[2 * channels * k : 2 * channels * (k + 1)]
            both = both[:channels] + both[channels:]
            out = both if out is None else jnp.where(marks == k, both, out)
        total = total + weight_ref[corner : corner + 1, columns] * out
    return total


def by_lanes(ret_ref, slot_ref, weight_ref, columns):
    blocks, channels, _ = ret_ref.shape
    group = 8
    totals = [0.0] * (channels // group)
    for corner in range(CORNERS):
        slots = slot_ref[corner : corner + 1, columns]
        weight = weight_ref[corner : corner + 1, columns]
        lanes = jnp.broadcast_to(slots % LANES, (group, LANES))
        block = jnp.broadcast_to(slots // LANES, (group, LANES))
        marks = [block == k for k in range(blocks)]
        for c in range(channels // group):
            out = None
            for k in range(blocks):
                found = jnp.take_along_axis(ret_ref[k, group * c : group * (c + 1), :], lanes, axis=1)
                out = found if out is None else jnp.where(marks[k], found, out)
            totals[c] = totals[c] + weight * out
    return jnp.concatenate(totals, 0)


def sum_from_slots(ret_ref, slot_ref, weight_ref, result_ref, table_ref, *, plan):
    blocks, channels, _ = ret_ref.shape
    group = PLACES // LANES

    @pl.when(pl.program_id(0) == 0)
    def _():
        for k in range(blocks // group):
            both = halves(jnp.concatenate([ret_ref[group * k + part] for part in range(group)], 1))
            table_ref[2 * channels * k : 2 * channels * (k + 1), :] = jnp.concatenate(both, 0)

    at = 0
    for product, single in plan:
        columns = slice(at, at + product * LANES)
        result_ref[:, columns] = by_product(table_ref, slot_ref, weight_ref, columns, channels)
        for k in range(product, product + single):
            columns = slice(at + k * LANES, at + (k + 1) * LANES)
            result_ref[:, columns] = by_lanes(ret_ref, slot_ref, weight_ref, columns)
        at += (product + single) * LANES


def plan_of(blocks):
    turns = max(t for t in (3, 2, 1) if blocks % t == 0)
    size = blocks // turns
    return [(size - size // 3, size // 3)] * turns


def chunk_of(fine, most):
    return max(c for c in range(LANES, most + 1, LANES) if fine % c == 0)


def call(kernel, ins, out, scratch=(), grid=(), in_specs=VMEM, out_specs=VMEM, memory=16):
    single = isinstance(in_specs, pl.BlockSpec)
    return pl.pallas_call(
        kernel,
        grid=grid,
        out_shape=out,
        in_specs=[in_specs] * len(ins) if single else in_specs,
        out_specs=[out_specs] * len(out) if isinstance(out, list) else out_specs,
        scratch_shapes=list(scratch),
        compiler_params=pltpu.CompilerParams(vmem_limit_bytes=memory << 20),
    )(*ins)


def body(increment, send_slots, tent_weight, coarse_cell, diffusivity):
    channels, fine = increment.shape
    slot_count = coarse_cell.shape[0]
    rows, width = diffusivity.shape
    tiles = lax.axis_size("tile")
    share = slot_count // tiles
    blocks = slot_count // LANES
    wide = 2 * LANES
    ahead = [(i, (i + 1) % tiles) for i in range(tiles)]
    back = [((i + 1) % tiles, i) for i in range(tiles)]
    shape = jax.ShapeDtypeStruct
    slots = send_slots.T
    cells = coarse_cell.reshape(blocks, LANES)
    chunk = chunk_of(fine, 2304)
    grid = (fine // chunk,)
    part = lambda n: pl.BlockSpec((n, chunk), lambda i: (0, i))
    whole = pl.BlockSpec((blocks, channels, LANES), lambda i: (0, 0, 0))

    sent = call(
        sum_to_slots,
        (increment, slots, tent_weight),
        shape((blocks, channels, LANES), F32),
        grid=grid,
        in_specs=[part(channels), part(CORNERS), part(CORNERS)],
        out_specs=whole,
        memory=56,
    )
    received = exchange(sent, tiles, share)
    edge = shape((EDGE, channels, LANES), F32)
    coarse, head, tail = call(
        functools.partial(add_to_cells, width=width),
        (received, cells, diffusivity),
        [shape((rows, channels, wide), F32), edge, edge],
    )
    before = lax.ppermute(tail, "tile", ahead)
    after = lax.ppermute(head, "tile", back)
    padded = pltpu.VMEM((rows + 2 * STEPS, channels, wide), F32)
    field, values = call(
        functools.partial(diffuse_and_read, width=width),
        (coarse, before, after, diffusivity, cells),
        [shape((rows, channels, width), F32), shape((blocks, channels, LANES), F32)],
        [padded, padded, pltpu.VMEM((rows + 2 * STEPS, wide), F32)],
    )
    returned = exchange(values, tiles, share)
    result = call(
        functools.partial(sum_from_slots, plan=plan_of(chunk // LANES)),
        (returned, slots, tent_weight),
        shape((channels, fine), F32),
        [pltpu.VMEM((2 * channels * slot_count // PLACES, PLACES), BF16)],
        grid=grid,
        in_specs=[whole, part(CORNERS), part(CORNERS)],
        out_specs=part(channels),
        memory=32,
    )
    return (result, field.transpose(1, 0, 2))


def exchange(blocks, tiles, share):
    count, channels, lanes = blocks.shape
    if share == lanes:
        return lax.all_to_all(blocks, "tile", split_axis=0, concat_axis=0, tiled=True)
    flat = blocks.transpose(1, 0, 2).reshape(channels, count * lanes)
    flat = lax.all_to_all(flat, "tile", split_axis=1, concat_axis=1, tiled=True)
    return flat.reshape(channels, count, lanes).transpose(1, 0, 2)


def solution(mesh):
    in_specs = (
        P(None, ("group", "tile")),
        P("tile", None),
        P(None, "tile"),
        P("tile"),
        P("tile", None),
    )
    out_specs = (P(None, ("group", "tile")), P(None, ("group", "tile"), None))
    return jax.shard_map(body, mesh=mesh, in_specs=in_specs, out_specs=out_specs, check_vma=False)
```

```python
import functools

import jax
import jax.numpy as jnp
from jax import lax
from jax.experimental import pallas as pl
from jax.experimental.pallas import tpu as pltpu
from jax.sharding import PartitionSpec as P

STEPS = 5
CORNERS = 4
LANES = 128
PLACES = 256
EDGE = STEPS + (STEPS + 1) // 2
BF16 = jnp.bfloat16
F32 = jnp.float32
VMEM = pl.BlockSpec(memory_space=pltpu.VMEM)


def halves(values):
    high = values.astype(BF16)
    return high, (values - high.astype(F32)).astype(BF16)


def one_hot(places, length):
    rows = lax.broadcasted_iota(jnp.int32, (length, places.shape[1]), 0)
    return jnp.where(rows == places, 1.0, 0.0).astype(BF16)


def masked(values, marks, count):
    marks = jnp.broadcast_to(marks, values.shape)
    zero = jnp.zeros((), values.dtype)
    return jnp.concatenate([jnp.where(marks == k, values, zero) for k in range(count)], 0)


def dot_last(left, right):
    return lax.dot_general(left, right, (((1,), (1,)), ((), ())), preferred_element_type=F32)


def sum_to_slots(inc_ref, slot_ref, weight_ref, sent_ref):
    channels = inc_ref.shape[0]
    count = sent_ref.shape[0] * LANES // PLACES
    inc = inc_ref[...]
    left, right = [], []
    for corner in range(CORNERS):
        slots = slot_ref[corner : corner + 1, :]
        parts = jnp.concatenate(halves(weight_ref[corner : corner + 1, :] * inc), 0)
        left.append(masked(parts, slots // PLACES, count))
        right.append(one_hot(slots % PLACES, PLACES))
    sums = dot_last(jnp.concatenate(left, 1), jnp.concatenate(right, 1))

    @pl.when(pl.program_id(0) == 0)
    def _():
        sent_ref[...] = jnp.zeros_like(sent_ref)

    for k in range(count):
        both = sums[2 * channels * k : 2 * channels * (k + 1)]
        both = both[:channels] + both[channels:]
        for part in range(PLACES // LANES):
            sent_ref[k * (PLACES // LANES) + part] += both[:, LANES * part : LANES * (part + 1)]


def wide_column(width):
    lanes = lax.broadcasted_iota(jnp.int32, (2 * LANES, 1), 0)
    extra = (2 * LANES - width) // 2
    return jnp.where(lanes < width, lanes, jnp.where(lanes < width + extra, lanes - width, lanes - 2 * LANES + width))


def place_edge(edge_ref, rows, coefs, width):
    half = width - LANES
    for k, row in enumerate(rows):
        edge_ref[k] = row[:, :LANES]
    ends = [row[:, LANES:width] for row in rows]
    for k in range(0, STEPS - 1, 2):
        edge_ref[STEPS + k // 2] = jnp.concatenate([ends[k], ends[k + 1]], 1)
    edge_ref[EDGE - 1] = jnp.concatenate([ends[-1], jnp.zeros_like(ends[-1])], 1)
    for k, coef in enumerate(coefs):
        for part in range(3):
            edge_ref[EDGE - 1, 3 * k + part : 3 * k + part + 1, half:] = coef[:, half * part : half * (part + 1)]


def read_edge(edge_ref, k, width):
    half = width - LANES
    start = edge_ref[k]
    end = edge_ref[STEPS + k // 2, :, half * (k % 2) : half * (k % 2) + half]
    return widened([start, end], start, end, width)


def read_coef(edge_ref, k, width):
    half = width - LANES
    parts = [edge_ref[EDGE - 1, 3 * k + part : 3 * k + part + 1, half:] for part in range(3)]
    return widened(parts, parts[0], parts[2], width)


def widened(parts, start, end, width):
    extra = (2 * LANES - width) // 2
    return jnp.concatenate(parts + [start[:, :extra], end[:, end.shape[1] - extra :]], 1)


def add_to_cells(rec_ref, cell_ref, coef_ref, coarse_ref, near_ref, far_ref, *, width):
    rows, channels, wide = coarse_ref.shape
    senders = rec_ref.shape[0]
    cells = jnp.concatenate([cell_ref[s : s + 1, :] for s in range(senders)], 1)
    values = jnp.concatenate([rec_ref[s] for s in range(senders)], 1)
    y = cells // width
    right = jnp.where(wide_column(width) == cells - y * width, 1.0, 0.0).astype(BF16)
    left = masked(jnp.concatenate(halves(values), 0), y, rows)
    sums = dot_last(left, right)
    full = []
    for k in range(rows):
        both = sums[2 * channels * k : 2 * channels * (k + 1)]
        both = both[:channels] + both[channels:]
        coarse_ref[k] = both
        full.append(both)
    coefs = [coef_ref[k : k + 1, :] for k in range(rows)]
    even = lax.axis_index("tile") % 2 == 0

    def place(head_ref, tail_ref):
        place_edge(head_ref, full[:STEPS], coefs[:STEPS], width)
        place_edge(tail_ref, full[rows - STEPS :], coefs[rows - STEPS :], width)

    pl.when(even)(lambda: place(far_ref, near_ref))
    pl.when(jnp.logical_not(even))(lambda: place(near_ref, far_ref))


def diffuse_and_read(
    coarse_ref, near_ref, far_ref, own_ref, cell_ref, field_ref, values_ref, one_ref, two_ref, coef_ref, *, width
):
    rows, channels, wide = coarse_ref.shape
    senders = values_ref.shape[0]
    total = rows + 2 * STEPS
    own = own_ref[...]
    coef_ref[STEPS : STEPS + rows, :] = widened([own], own, own, width)
    one_ref[STEPS : STEPS + rows] = coarse_ref[...]
    even = lax.axis_index("tile") % 2 == 0

    def read(before_ref, after_ref):
        for k in range(STEPS):
            one_ref[k] = read_edge(before_ref, k, width)
            one_ref[STEPS + rows + k] = read_edge(after_ref, k, width)
            coef_ref[k : k + 1, :] = read_coef(before_ref, k, width)
            coef_ref[STEPS + rows + k : STEPS + rows + k + 1, :] = read_coef(after_ref, k, width)

    pl.when(even)(lambda: read(far_ref, near_ref))
    pl.when(jnp.logical_not(even))(lambda: read(near_ref, far_ref))
    held, other = one_ref, two_ref
    for turn in range(1, STEPS + 1):
        for y in range(turn, total - turn):
            here = held[y]
            spread = held[y + 1] + held[y - 1] + pltpu.roll(here, 1, 1) + pltpu.roll(here, wide - 1, 1)
            other[y] = here + coef_ref[y : y + 1, :] * (spread - 4.0 * here)
        held, other = other, held
    final = held[STEPS : STEPS + rows]
    field_ref[...] = final[:, :, :width]
    left = jnp.concatenate(halves(final.reshape(rows * channels, wide)), 1)
    for s in range(0, senders, 2):
        cells = jnp.concatenate([cell_ref[s : s + 1, :], cell_ref[s + 1 : s + 2, :]], 1)
        y = cells // width
        right = one_hot(cells - y * width, wide)
        found = jnp.dot(left, jnp.concatenate([right, right], 0), preferred_element_type=F32)
        out = jnp.zeros((channels, 2 * LANES), F32)
        marks = jnp.broadcast_to(y, out.shape)
        for k in range(rows):
            out = jnp.where(marks == k, found[channels * k : channels * (k + 1)], out)
        values_ref[s] = out[:, :LANES]
        values_ref[s + 1] = out[:, LANES:]


def by_product(table_ref, slot_ref, weight_ref, columns, channels):
    count = table_ref.shape[0] // (2 * channels)
    total = 0.0
    for corner in range(CORNERS):
        slots = slot_ref[corner : corner + 1, columns]
        found = jnp.dot(table_ref[...], one_hot(slots % PLACES, PLACES), preferred_element_type=F32)
        marks = jnp.broadcast_to(slots // PLACES, (channels, slots.shape[1]))
        out = None
        for k in range(count):
            both = found[2 * channels * k : 2 * channels * (k + 1)]
            both = both[:channels] + both[channels:]
            out = both if out is None else jnp.where(marks == k, both, out)
        total = total + weight_ref[corner : corner + 1, columns] * out
    return total


def by_lanes(ret_ref, slot_ref, weight_ref, columns):
    blocks, channels, _ = ret_ref.shape
    group = 8
    totals = [0.0] * (channels // group)
    for corner in range(CORNERS):
        slots = slot_ref[corner : corner + 1, columns]
        weight = weight_ref[corner : corner + 1, columns]
        lanes = jnp.broadcast_to(slots % LANES, (group, LANES))
        block = jnp.broadcast_to(slots // LANES, (group, LANES))
        marks = [block == k for k in range(blocks)]
        for c in range(channels // group):
            out = None
            for k in range(blocks):
                found = jnp.take_along_axis(ret_ref[k, group * c : group * (c + 1), :], lanes, axis=1)
                out = found if out is None else jnp.where(marks[k], found, out)
            totals[c] = totals[c] + weight * out
    return jnp.concatenate(totals, 0)


def sum_from_slots(ret_ref, slot_ref, weight_ref, result_ref, table_ref, *, plan):
    blocks, channels, _ = ret_ref.shape
    group = PLACES // LANES

    @pl.when(pl.program_id(0) == 0)
    def _():
        for k in range(blocks // group):
            both = halves(jnp.concatenate([ret_ref[group * k + part] for part in range(group)], 1))
            table_ref[2 * channels * k : 2 * channels * (k + 1), :] = jnp.concatenate(both, 0)

    at = 0
    for product, single in plan:
        columns = slice(at, at + product * LANES)
        result_ref[:, columns] = by_product(table_ref, slot_ref, weight_ref, columns, channels)
        for k in range(product, product + single):
            columns = slice(at + k * LANES, at + (k + 1) * LANES)
            result_ref[:, columns] = by_lanes(ret_ref, slot_ref, weight_ref, columns)
        at += (product + single) * LANES


def plan_of(blocks):
    turns = max(t for t in (3, 2, 1) if blocks % t == 0)
    size = blocks // turns
    return [(size - size // 3, size // 3)] * turns


def chunk_of(fine, most):
    return max(c for c in range(LANES, most + 1, LANES) if fine % c == 0)


def call(kernel, ins, out, scratch=(), grid=(), in_specs=VMEM, out_specs=VMEM, memory=16):
    single = isinstance(in_specs, pl.BlockSpec)
    return pl.pallas_call(
        kernel,
        grid=grid,
        out_shape=out,
        in_specs=[in_specs] * len(ins) if single else in_specs,
        out_specs=[out_specs] * len(out) if isinstance(out, list) else out_specs,
        scratch_shapes=list(scratch),
        compiler_params=pltpu.CompilerParams(vmem_limit_bytes=memory << 20),
    )(*ins)


def body(increment, send_slots, tent_weight, coarse_cell, diffusivity):
    channels, fine = increment.shape
    slot_count = coarse_cell.shape[0]
    rows, width = diffusivity.shape
    tiles = lax.axis_size("tile")
    share = slot_count // tiles
    blocks = slot_count // LANES
    wide = 2 * LANES
    on_chip = [(i, i ^ 1) for i in range(tiles)]
    off_chip = [(i, (i + 2 * (i % 2) - 1) % tiles) for i in range(tiles)]
    shape = jax.ShapeDtypeStruct
    slots = send_slots.T
    cells = coarse_cell.reshape(blocks, LANES)
    chunk = chunk_of(fine, 2304)
    grid = (fine // chunk,)
    part = lambda n: pl.BlockSpec((n, chunk), lambda i: (0, i))
    whole = pl.BlockSpec((blocks, channels, LANES), lambda i: (0, 0, 0))

    sent = call(
        sum_to_slots,
        (increment, slots, tent_weight),
        shape((blocks, channels, LANES), F32),
        grid=grid,
        in_specs=[part(channels), part(CORNERS), part(CORNERS)],
        out_specs=whole,
        memory=56,
    )
    received = exchange(sent, tiles, share)
    edge = shape((EDGE, channels, LANES), F32)
    coarse, near, far = call(
        functools.partial(add_to_cells, width=width),
        (received, cells, diffusivity),
        [shape((rows, channels, wide), F32), edge, edge],
    )
    far = lax.ppermute(far, "tile", off_chip)
    near = lax.ppermute(near, "tile", on_chip)
    padded = pltpu.VMEM((rows + 2 * STEPS, channels, wide), F32)
    field, values = call(
        functools.partial(diffuse_and_read, width=width),
        (coarse, near, far, diffusivity, cells),
        [shape((rows, channels, width), F32), shape((blocks, channels, LANES), F32)],
        [padded, padded, pltpu.VMEM((rows + 2 * STEPS, wide), F32)],
    )
    returned = exchange(values, tiles, share)
    result = call(
        functools.partial(sum_from_slots, plan=plan_of(chunk // LANES)),
        (returned, slots, tent_weight),
        shape((channels, fine), F32),
        [pltpu.VMEM((2 * channels * slot_count // PLACES, PLACES), BF16)],
        grid=grid,
        in_specs=[whole, part(CORNERS), part(CORNERS)],
        out_specs=part(channels),
        memory=32,
    )
    return (result, field.transpose(1, 0, 2))


def exchange(blocks, tiles, share):
    count, channels, lanes = blocks.shape
    if share == lanes:
        return lax.all_to_all(blocks, "tile", split_axis=0, concat_axis=0, tiled=True)
    flat = blocks.transpose(1, 0, 2).reshape(channels, count * lanes)
    flat = lax.all_to_all(flat, "tile", split_axis=1, concat_axis=1, tiled=True)
    return flat.reshape(channels, count, lanes).transpose(1, 0, 2)


def solution(mesh):
    in_specs = (
        P(None, ("group", "tile")),
        P("tile", None),
        P(None, "tile"),
        P("tile"),
        P("tile", None),
    )
    out_specs = (P(None, ("group", "tile")), P(None, ("group", "tile"), None))
    return jax.shard_map(body, mesh=mesh, in_specs=in_specs, out_specs=out_specs, check_vma=False)
```

```python
import functools

import jax
import jax.numpy as jnp
from jax import lax
from jax.experimental import pallas as pl
from jax.experimental.pallas import tpu as pltpu
from jax.sharding import PartitionSpec as P

STEPS = 5
CORNERS = 4
LANES = 128
PLACES = 256
EDGE = STEPS + (STEPS + 1) // 2
BF16 = jnp.bfloat16
F32 = jnp.float32
VMEM = pl.BlockSpec(memory_space=pltpu.VMEM)


def halves(values):
    high = values.astype(BF16)
    return high, (values - high.astype(F32)).astype(BF16)


def one_hot(places, length):
    rows = lax.broadcasted_iota(jnp.int32, (length, places.shape[1]), 0)
    return jnp.where(rows == places, 1.0, 0.0).astype(BF16)


def masked(values, marks, count):
    marks = jnp.broadcast_to(marks, values.shape)
    zero = jnp.zeros((), values.dtype)
    return jnp.concatenate([jnp.where(marks == k, values, zero) for k in range(count)], 0)


def dot_last(left, right):
    return lax.dot_general(left, right, (((1,), (1,)), ((), ())), preferred_element_type=F32)


def sum_to_slots(inc_ref, slot_ref, weight_ref, sent_ref):
    channels = inc_ref.shape[0]
    count = sent_ref.shape[0] * LANES // PLACES
    inc = inc_ref[...]
    left, right = [], []
    for corner in range(CORNERS):
        slots = slot_ref[corner : corner + 1, :]
        parts = jnp.concatenate(halves(weight_ref[corner : corner + 1, :] * inc), 0)
        left.append(masked(parts, slots // PLACES, count))
        right.append(one_hot(slots % PLACES, PLACES))
    sums = dot_last(jnp.concatenate(left, 1), jnp.concatenate(right, 1))

    @pl.when(pl.program_id(0) == 0)
    def _():
        sent_ref[...] = jnp.zeros_like(sent_ref)

    for k in range(count):
        both = sums[2 * channels * k : 2 * channels * (k + 1)]
        both = both[:channels] + both[channels:]
        for part in range(PLACES // LANES):
            sent_ref[k * (PLACES // LANES) + part] += both[:, LANES * part : LANES * (part + 1)]


def wide_column(width):
    lanes = lax.broadcasted_iota(jnp.int32, (2 * LANES, 1), 0)
    extra = (2 * LANES - width) // 2
    return jnp.where(lanes < width, lanes, jnp.where(lanes < width + extra, lanes - width, lanes - 2 * LANES + width))


def place_edge(edge_ref, rows, coefs, width):
    half = width - LANES
    for k, row in enumerate(rows):
        edge_ref[k] = row[:, :LANES]
    ends = [row[:, LANES:width] for row in rows]
    for k in range(0, STEPS - 1, 2):
        edge_ref[STEPS + k // 2] = jnp.concatenate([ends[k], ends[k + 1]], 1)
    edge_ref[EDGE - 1] = jnp.concatenate([ends[-1], jnp.zeros_like(ends[-1])], 1)
    for k, coef in enumerate(coefs):
        for part in range(3):
            edge_ref[EDGE - 1, 3 * k + part : 3 * k + part + 1, half:] = coef[:, half * part : half * (part + 1)]


def read_edge(edge_ref, k, width):
    half = width - LANES
    start = edge_ref[k]
    end = edge_ref[STEPS + k // 2, :, half * (k % 2) : half * (k % 2) + half]
    return widened([start, end], start, end, width)


def read_coef(edge_ref, k, width):
    half = width - LANES
    parts = [edge_ref[EDGE - 1, 3 * k + part : 3 * k + part + 1, half:] for part in range(3)]
    return widened(parts, parts[0], parts[2], width)


def widened(parts, start, end, width):
    extra = (2 * LANES - width) // 2
    return jnp.concatenate(parts + [start[:, :extra], end[:, end.shape[1] - extra :]], 1)


def add_to_cells(rec_ref, cell_ref, coef_ref, coarse_ref, near_ref, far_ref, *, width):
    rows, channels, wide = coarse_ref.shape
    senders = rec_ref.shape[0]
    cells = jnp.concatenate([cell_ref[s : s + 1, :] for s in range(senders)], 1)
    values = jnp.concatenate([rec_ref[s] for s in range(senders)], 1)
    y = cells // width
    right = jnp.where(wide_column(width) == cells - y * width, 1.0, 0.0).astype(BF16)
    left = masked(jnp.concatenate(halves(values), 0), y, rows)
    sums = dot_last(left, right)
    full = []
    for k in range(rows):
        both = sums[2 * channels * k : 2 * channels * (k + 1)]
        both = both[:channels] + both[channels:]
        coarse_ref[k] = both
        full.append(both)
    coefs = [coef_ref[k : k + 1, :] for k in range(rows)]
    even = lax.axis_index("tile") % 2 == 0

    def place(head_ref, tail_ref):
        place_edge(head_ref, full[:STEPS], coefs[:STEPS], width)
        place_edge(tail_ref, full[rows - STEPS :], coefs[rows - STEPS :], width)

    pl.when(even)(lambda: place(far_ref, near_ref))
    pl.when(jnp.logical_not(even))(lambda: place(near_ref, far_ref))


def stepped(above, here, below, coef):
    wide = here.shape[-1]
    spread = below + above + pltpu.roll(here, 1, 1) + pltpu.roll(here, wide - 1, 1)
    return here + coef * (spread - 4.0 * here)


def kept_rows(turn, total):
    first, last = STEPS + turn, total - STEPS - turn
    return [first, first + 1, last - 2, last - 1]


def read_rows(final_rows, ys, cell_ref, values_ref, base, width):
    senders, channels, _ = values_ref.shape
    left = jnp.concatenate([jnp.concatenate(halves(row), 0) for row in final_rows], 0)
    for s in range(0, senders, 2):
        cells = jnp.concatenate([cell_ref[s : s + 1, :], cell_ref[s + 1 : s + 2, :]], 1)
        y = cells // width
        found = jnp.dot(left, one_hot(cells - y * width, left.shape[1]), preferred_element_type=F32)
        out = base(s)
        marks = jnp.broadcast_to(y, out.shape)
        for k, row in enumerate(ys):
            both = found[2 * channels * k : 2 * channels * (k + 1)]
            out = jnp.where(marks == row, both[:channels] + both[channels:], out)
        values_ref[s] = out[:, :LANES]
        values_ref[s + 1] = out[:, LANES:]


def diffuse_inner(coarse_ref, own_ref, cell_ref, kept_ref, inner_ref, values_ref, one_ref, two_ref, coef_ref, *, width):
    rows, channels, wide = coarse_ref.shape
    own = own_ref[...]
    coef_ref[...] = widened([own], own, own, width)
    held, other, last = coarse_ref, one_ref, two_ref
    for turn in range(1, STEPS + 1):
        for y in range(turn, rows - turn):
            other[y] = stepped(held[y - 1], held[y], held[y + 1], coef_ref[y : y + 1, :])
        if turn < STEPS:
            for place, y in enumerate(kept_rows(turn, rows + 2 * STEPS)):
                kept_ref[turn - 1, place] = other[y - STEPS]
        held, other, last = other, last, other
    ys = range(STEPS, rows - STEPS)
    for y in ys:
        inner_ref[y - STEPS] = held[y]
    nothing = lambda s: jnp.zeros((channels, 2 * LANES), F32)
    read_rows([held[y] for y in ys], ys, cell_ref, values_ref, nothing, width)


def diffuse_outer(
    coarse_ref, near_ref, far_ref, own_ref, cell_ref, kept_ref, inner_ref, part_ref,
    field_ref, values_ref, one_ref, two_ref, coef_ref, *, width
):
    rows, channels, wide = coarse_ref.shape
    total = rows + 2 * STEPS
    own = own_ref[...]
    coef_ref[STEPS : STEPS + rows, :] = widened([own], own, own, width)
    even = lax.axis_index("tile") % 2 == 0

    def read(before_ref, after_ref):
        for k in range(STEPS):
            one_ref[k] = read_edge(before_ref, k, width)
            one_ref[STEPS + rows + k] = read_edge(after_ref, k, width)
            coef_ref[k : k + 1, :] = read_coef(before_ref, k, width)
            coef_ref[STEPS + rows + k : STEPS + rows + k + 1, :] = read_coef(after_ref, k, width)

    pl.when(even)(lambda: read(far_ref, near_ref))
    pl.when(jnp.logical_not(even))(lambda: read(near_ref, far_ref))
    held, other = one_ref, two_ref
    for turn in range(1, STEPS + 1):

        def row(y):
            if turn == 1 and STEPS <= y < STEPS + rows:
                return coarse_ref[y - STEPS]
            kept = kept_rows(turn - 1, total) if turn > 1 else []
            return kept_ref[turn - 2, kept.index(y)] if y in kept else held[y]

        for start in (turn, total - STEPS - turn):
            for y in range(start, start + STEPS):
                other[y] = stepped(row(y - 1), row(y), row(y + 1), coef_ref[y : y + 1, :])
        held, other = other, held
    ys = list(range(STEPS)) + list(range(rows - STEPS, rows))
    for y in range(rows):
        source = held[y + STEPS] if y in ys else inner_ref[y - STEPS]
        field_ref[y] = source[:, :width]
    base = lambda s: jnp.concatenate([part_ref[s], part_ref[s + 1]], 1)
    read_rows([held[y + STEPS] for y in ys], ys, cell_ref, values_ref, base, width)


def by_product(table_ref, slot_ref, weight_ref, columns, channels):
    count = table_ref.shape[0] // (2 * channels)
    total = 0.0
    for corner in range(CORNERS):
        slots = slot_ref[corner : corner + 1, columns]
        found = jnp.dot(table_ref[...], one_hot(slots % PLACES, PLACES), preferred_element_type=F32)
        marks = jnp.broadcast_to(slots // PLACES, (channels, slots.shape[1]))
        out = None
        for k in range(count):
            both = found[2 * channels * k : 2 * channels * (k + 1)]
            both = both[:channels] + both[channels:]
            out = both if out is None else jnp.where(marks == k, both, out)
        total = total + weight_ref[corner : corner + 1, columns] * out
    return total


def by_lanes(ret_ref, slot_ref, weight_ref, columns):
    blocks, channels, _ = ret_ref.shape
    group = 8
    totals = [0.0] * (channels // group)
    for corner in range(CORNERS):
        slots = slot_ref[corner : corner + 1, columns]
        weight = weight_ref[corner : corner + 1, columns]
        lanes = jnp.broadcast_to(slots % LANES, (group, LANES))
        block = jnp.broadcast_to(slots // LANES, (group, LANES))
        marks = [block == k for k in range(blocks)]
        for c in range(channels // group):
            out = None
            for k in range(blocks):
                found = jnp.take_along_axis(ret_ref[k, group * c : group * (c + 1), :], lanes, axis=1)
                out = found if out is None else jnp.where(marks[k], found, out)
            totals[c] = totals[c] + weight * out
    return jnp.concatenate(totals, 0)


def sum_from_slots(ret_ref, slot_ref, weight_ref, result_ref, table_ref, *, plan):
    blocks, channels, _ = ret_ref.shape
    group = PLACES // LANES

    @pl.when(pl.program_id(0) == 0)
    def _():
        for k in range(blocks // group):
            both = halves(jnp.concatenate([ret_ref[group * k + part] for part in range(group)], 1))
            table_ref[2 * channels * k : 2 * channels * (k + 1), :] = jnp.concatenate(both, 0)

    at = 0
    for product, single in plan:
        columns = slice(at, at + product * LANES)
        result_ref[:, columns] = by_product(table_ref, slot_ref, weight_ref, columns, channels)
        for k in range(product, product + single):
            columns = slice(at + k * LANES, at + (k + 1) * LANES)
            result_ref[:, columns] = by_lanes(ret_ref, slot_ref, weight_ref, columns)
        at += (product + single) * LANES


def plan_of(blocks):
    turns = max(t for t in (3, 2, 1) if blocks % t == 0)
    size = blocks // turns
    return [(size - size // 3, size // 3)] * turns


def chunk_of(fine, most):
    return max(c for c in range(LANES, most + 1, LANES) if fine % c == 0)


def call(kernel, ins, out, scratch=(), grid=(), in_specs=VMEM, out_specs=VMEM, memory=16, cost=None):
    single = isinstance(in_specs, pl.BlockSpec)
    return pl.pallas_call(
        kernel,
        grid=grid,
        out_shape=out,
        in_specs=[in_specs] * len(ins) if single else in_specs,
        out_specs=[out_specs] * len(out) if isinstance(out, list) else out_specs,
        scratch_shapes=list(scratch),
        cost_estimate=cost,
        compiler_params=pltpu.CompilerParams(vmem_limit_bytes=memory << 20),
    )(*ins)


def body(increment, send_slots, tent_weight, coarse_cell, diffusivity):
    channels, fine = increment.shape
    slot_count = coarse_cell.shape[0]
    rows, width = diffusivity.shape
    tiles = lax.axis_size("tile")
    share = slot_count // tiles
    blocks = slot_count // LANES
    wide = 2 * LANES
    on_chip = [(i, i ^ 1) for i in range(tiles)]
    off_chip = [(i, (i + 2 * (i % 2) - 1) % tiles) for i in range(tiles)]
    shape = jax.ShapeDtypeStruct
    slots = send_slots.T
    cells = coarse_cell.reshape(blocks, LANES)
    chunk = chunk_of(fine, 2304)
    grid = (fine // chunk,)
    part = lambda n: pl.BlockSpec((n, chunk), lambda i: (0, i))
    whole = pl.BlockSpec((blocks, channels, LANES), lambda i: (0, 0, 0))

    sent = call(
        sum_to_slots,
        (increment, slots, tent_weight),
        shape((blocks, channels, LANES), F32),
        grid=grid,
        in_specs=[part(channels), part(CORNERS), part(CORNERS)],
        out_specs=whole,
        memory=56,
    )
    received = exchange(sent, tiles, share)
    edge = shape((EDGE, channels, LANES), F32)
    coarse, near, far = call(
        functools.partial(add_to_cells, width=width),
        (received, cells, diffusivity),
        [shape((rows, channels, wide), F32), edge, edge],
    )
    far = lax.ppermute(far, "tile", off_chip)
    near = lax.ppermute(near, "tile", on_chip)
    slot_blocks = shape((blocks, channels, LANES), F32)
    own = pltpu.VMEM((rows, channels, wide), F32)
    kept, inner, found = call(
        functools.partial(diffuse_inner, width=width),
        (coarse, diffusivity, cells),
        [shape((STEPS - 1, 4, channels, wide), F32), shape((rows - 2 * STEPS, channels, wide), F32), slot_blocks],
        [own, own, pltpu.VMEM((rows, wide), F32)],
        cost=pl.CostEstimate(flops=2 * slot_count * wide * wide * 2, bytes_accessed=8 << 20, transcendentals=0),
    )
    padded = pltpu.VMEM((rows + 2 * STEPS, channels, wide), F32)
    field, values = call(
        functools.partial(diffuse_outer, width=width),
        (coarse, near, far, diffusivity, cells, kept, inner, found),
        [shape((rows, channels, width), F32), slot_blocks],
        [padded, padded, pltpu.VMEM((rows + 2 * STEPS, wide), F32)],
    )
    returned = exchange(values, tiles, share)
    result = call(
        functools.partial(sum_from_slots, plan=plan_of(chunk // LANES)),
        (returned, slots, tent_weight),
        shape((channels, fine), F32),
        [pltpu.VMEM((2 * channels * slot_count // PLACES, PLACES), BF16)],
        grid=grid,
        in_specs=[whole, part(CORNERS), part(CORNERS)],
        out_specs=part(channels),
        memory=32,
    )
    return (result, field.transpose(1, 0, 2))


def exchange(blocks, tiles, share):
    count, channels, lanes = blocks.shape
    if share == lanes:
        return lax.all_to_all(blocks, "tile", split_axis=0, concat_axis=0, tiled=True)
    flat = blocks.transpose(1, 0, 2).reshape(channels, count * lanes)
    flat = lax.all_to_all(flat, "tile", split_axis=1, concat_axis=1, tiled=True)
    return flat.reshape(channels, count, lanes).transpose(1, 0, 2)


def solution(mesh):
    in_specs = (
        P(None, ("group", "tile")),
        P("tile", None),
        P(None, "tile"),
        P("tile"),
        P("tile", None),
    )
    out_specs = (P(None, ("group", "tile")), P(None, ("group", "tile"), None))
    return jax.shard_map(body, mesh=mesh, in_specs=in_specs, out_specs=out_specs, check_vma=False)
```

```python
import functools

import jax
import jax.numpy as jnp
from jax import lax
from jax.experimental import pallas as pl
from jax.experimental.pallas import tpu as pltpu
from jax.sharding import PartitionSpec as P

STEPS = 5
CORNERS = 4
LANES = 128
PLACES = 256
EDGE = STEPS + (STEPS + 1) // 2
BF16 = jnp.bfloat16
F32 = jnp.float32
VMEM = pl.BlockSpec(memory_space=pltpu.VMEM)


def halves(values):
    high = values.astype(BF16)
    return high, (values - high.astype(F32)).astype(BF16)


def one_hot(places, length):
    rows = lax.broadcasted_iota(jnp.int32, (length, places.shape[1]), 0)
    return jnp.where(rows == places, 1.0, 0.0).astype(BF16)


def masked(values, marks, wanted):
    marks = jnp.broadcast_to(marks, values.shape)
    zero = jnp.zeros((), values.dtype)
    return jnp.concatenate([jnp.where(marks == k, values, zero) for k in wanted], 0)


def dot_last(left, right):
    return lax.dot_general(left, right, (((1,), (1,)), ((), ())), preferred_element_type=F32)


def sum_to_slots(inc_ref, slot_ref, weight_ref, sent_ref):
    channels = inc_ref.shape[0]
    count = sent_ref.shape[0] * LANES // PLACES
    inc = inc_ref[...]
    left, right = [], []
    for corner in range(CORNERS):
        slots = slot_ref[corner : corner + 1, :]
        parts = jnp.concatenate(halves(weight_ref[corner : corner + 1, :] * inc), 0)
        left.append(masked(parts, slots // PLACES, range(count)))
        right.append(one_hot(slots % PLACES, PLACES))
    sums = dot_last(jnp.concatenate(left, 1), jnp.concatenate(right, 1))

    @pl.when(pl.program_id(0) == 0)
    def _():
        sent_ref[...] = jnp.zeros_like(sent_ref)

    for k in range(count):
        both = sums[2 * channels * k : 2 * channels * (k + 1)]
        both = both[:channels] + both[channels:]
        for part in range(PLACES // LANES):
            sent_ref[k * (PLACES // LANES) + part] += both[:, LANES * part : LANES * (part + 1)]


def wide_column(width):
    lanes = lax.broadcasted_iota(jnp.int32, (2 * LANES, 1), 0)
    extra = (2 * LANES - width) // 2
    return jnp.where(lanes < width, lanes, jnp.where(lanes < width + extra, lanes - width, lanes - 2 * LANES + width))


def place_edge(edge_ref, rows, coefs, width):
    half = width - LANES
    for k, row in enumerate(rows):
        edge_ref[k] = row[:, :LANES]
    ends = [row[:, LANES:width] for row in rows]
    for k in range(0, STEPS - 1, 2):
        edge_ref[STEPS + k // 2] = jnp.concatenate([ends[k], ends[k + 1]], 1)
    edge_ref[EDGE - 1] = jnp.concatenate([ends[-1], jnp.zeros_like(ends[-1])], 1)
    for k, coef in enumerate(coefs):
        for part in range(3):
            edge_ref[EDGE - 1, 3 * k + part : 3 * k + part + 1, half:] = coef[:, half * part : half * (part + 1)]


def read_edge(edge_ref, k, width):
    half = width - LANES
    start = edge_ref[k]
    end = edge_ref[STEPS + k // 2, :, half * (k % 2) : half * (k % 2) + half]
    return widened([start, end], start, end, width)


def read_coef(edge_ref, k, width):
    half = width - LANES
    parts = [edge_ref[EDGE - 1, 3 * k + part : 3 * k + part + 1, half:] for part in range(3)]
    return widened(parts, parts[0], parts[2], width)


def widened(parts, start, end, width):
    extra = (2 * LANES - width) // 2
    return jnp.concatenate(parts + [start[:, :extra], end[:, end.shape[1] - extra :]], 1)


def cell_sums(rec_ref, cell_ref, ys, width):
    senders, channels, _ = rec_ref.shape
    cells = jnp.concatenate([cell_ref[s : s + 1, :] for s in range(senders)], 1)
    values = jnp.concatenate([rec_ref[s] for s in range(senders)], 1)
    y = cells // width
    right = jnp.where(wide_column(width) == cells - y * width, 1.0, 0.0).astype(BF16)
    sums = dot_last(masked(jnp.concatenate(halves(values), 0), y, ys), right)
    full = []
    for k in range(len(ys)):
        both = sums[2 * channels * k : 2 * channels * (k + 1)]
        full.append(both[:channels] + both[channels:])
    return full


def edges_of(rows):
    return list(range(STEPS)) + list(range(rows - STEPS, rows))


def sum_edges(rec_ref, cell_ref, coef_ref, edges_ref, near_ref, far_ref, *, width):
    rows = coef_ref.shape[0]
    full = cell_sums(rec_ref, cell_ref, edges_of(rows), width)
    for k, row in enumerate(full):
        edges_ref[k] = row
    coefs = [coef_ref[k : k + 1, :] for k in range(rows)]
    even = lax.axis_index("tile") % 2 == 0

    def place(head_ref, tail_ref):
        place_edge(head_ref, full[:STEPS], coefs[:STEPS], width)
        place_edge(tail_ref, full[STEPS:], coefs[rows - STEPS :], width)

    pl.when(even)(lambda: place(far_ref, near_ref))
    pl.when(jnp.logical_not(even))(lambda: place(near_ref, far_ref))


def stepped(above, here, below, coef):
    wide = here.shape[-1]
    spread = below + above + pltpu.roll(here, 1, 1) + pltpu.roll(here, wide - 1, 1)
    return here + coef * (spread - 4.0 * here)


def kept_rows(turn, total):
    first, last = STEPS + turn, total - STEPS - turn
    return [first, first + 1, last - 2, last - 1]


def read_rows(final_rows, ys, cell_ref, values_ref, base, width):
    senders, channels, _ = values_ref.shape
    left = jnp.concatenate([jnp.concatenate(halves(row), 0) for row in final_rows], 0)
    for s in range(0, senders, 2):
        cells = jnp.concatenate([cell_ref[s : s + 1, :], cell_ref[s + 1 : s + 2, :]], 1)
        y = cells // width
        found = jnp.dot(left, one_hot(cells - y * width, left.shape[1]), preferred_element_type=F32)
        out = base(s)
        marks = jnp.broadcast_to(y, out.shape)
        for k, row in enumerate(ys):
            both = found[2 * channels * k : 2 * channels * (k + 1)]
            out = jnp.where(marks == row, both[:channels] + both[channels:], out)
        values_ref[s] = out[:, :LANES]
        values_ref[s + 1] = out[:, LANES:]


def diffuse_inner(
    rec_ref, edges_ref, own_ref, cell_ref, kept_ref, inner_ref, values_ref, start_ref, one_ref, two_ref, coef_ref, *, width
):
    rows, channels, wide = start_ref.shape
    own = own_ref[...]
    coef_ref[...] = widened([own], own, own, width)
    for k, y in enumerate(edges_of(rows)):
        start_ref[y] = edges_ref[k]
    ys = range(STEPS, rows - STEPS)
    for y, row in zip(ys, cell_sums(rec_ref, cell_ref, ys, width)):
        start_ref[y] = row
    held, other, last = start_ref, one_ref, two_ref
    for turn in range(1, STEPS + 1):
        for y in range(turn, rows - turn):
            other[y] = stepped(held[y - 1], held[y], held[y + 1], coef_ref[y : y + 1, :])
        if turn < STEPS:
            for place, y in enumerate(kept_rows(turn, rows + 2 * STEPS)):
                kept_ref[turn - 1, place] = other[y - STEPS]
        held, other, last = other, last, other
    for y in ys:
        inner_ref[y - STEPS] = held[y]
    nothing = lambda s: jnp.zeros((channels, 2 * LANES), F32)
    read_rows([held[y] for y in ys], ys, cell_ref, values_ref, nothing, width)


def diffuse_outer(
    edges_ref, near_ref, far_ref, own_ref, cell_ref, kept_ref, part_ref,
    outer_ref, values_ref, one_ref, two_ref, coef_ref, *, width
):
    rows = own_ref.shape[0]
    total = rows + 2 * STEPS
    own = own_ref[...]
    coef_ref[STEPS : STEPS + rows, :] = widened([own], own, own, width)
    even = lax.axis_index("tile") % 2 == 0

    def read(before_ref, after_ref):
        for k in range(STEPS):
            one_ref[k] = read_edge(before_ref, k, width)
            one_ref[STEPS + rows + k] = read_edge(after_ref, k, width)
            coef_ref[k : k + 1, :] = read_coef(before_ref, k, width)
            coef_ref[STEPS + rows + k : STEPS + rows + k + 1, :] = read_coef(after_ref, k, width)

    pl.when(even)(lambda: read(far_ref, near_ref))
    pl.when(jnp.logical_not(even))(lambda: read(near_ref, far_ref))
    ys = edges_of(rows)
    held, other = one_ref, two_ref
    for turn in range(1, STEPS + 1):

        def row(y):
            if turn == 1 and y - STEPS in ys:
                return edges_ref[ys.index(y - STEPS)]
            kept = kept_rows(turn - 1, total) if turn > 1 else []
            return kept_ref[turn - 2, kept.index(y)] if y in kept else held[y]

        for start in (turn, total - STEPS - turn):
            for y in range(start, start + STEPS):
                other[y] = stepped(row(y - 1), row(y), row(y + 1), coef_ref[y : y + 1, :])
        held, other = other, held
    final = [held[y + STEPS] for y in ys]
    for k, row in enumerate(final):
        outer_ref[k] = row
    base = lambda s: jnp.concatenate([part_ref[s], part_ref[s + 1]], 1)
    read_rows(final, ys, cell_ref, values_ref, base, width)


def join_rows(inner_ref, outer_ref, field_ref):
    rows, _, width = field_ref.shape
    ys = edges_of(rows)
    for y in range(rows):
        row = outer_ref[ys.index(y)] if y in ys else inner_ref[y - STEPS]
        field_ref[y] = row[:, :width]


def by_product(table_ref, slot_ref, weight_ref, columns, channels):
    count = table_ref.shape[0] // (2 * channels)
    total = 0.0
    for corner in range(CORNERS):
        slots = slot_ref[corner : corner + 1, columns]
        found = jnp.dot(table_ref[...], one_hot(slots % PLACES, PLACES), preferred_element_type=F32)
        marks = jnp.broadcast_to(slots // PLACES, (channels, slots.shape[1]))
        out = None
        for k in range(count):
            both = found[2 * channels * k : 2 * channels * (k + 1)]
            both = both[:channels] + both[channels:]
            out = both if out is None else jnp.where(marks == k, both, out)
        total = total + weight_ref[corner : corner + 1, columns] * out
    return total


def by_lanes(ret_ref, slot_ref, weight_ref, columns):
    blocks, channels, _ = ret_ref.shape
    group = 8
    totals = [0.0] * (channels // group)
    for corner in range(CORNERS):
        slots = slot_ref[corner : corner + 1, columns]
        weight = weight_ref[corner : corner + 1, columns]
        lanes = jnp.broadcast_to(slots % LANES, (group, LANES))
        block = jnp.broadcast_to(slots // LANES, (group, LANES))
        marks = [block == k for k in range(blocks)]
        for c in range(channels // group):
            out = None
            for k in range(blocks):
                found = jnp.take_along_axis(ret_ref[k, group * c : group * (c + 1), :], lanes, axis=1)
                out = found if out is None else jnp.where(marks[k], found, out)
            totals[c] = totals[c] + weight * out
    return jnp.concatenate(totals, 0)


def sum_from_slots(ret_ref, slot_ref, weight_ref, result_ref, table_ref, *, plan):
    blocks, channels, _ = ret_ref.shape
    group = PLACES // LANES

    @pl.when(pl.program_id(0) == 0)
    def _():
        for k in range(blocks // group):
            both = halves(jnp.concatenate([ret_ref[group * k + part] for part in range(group)], 1))
            table_ref[2 * channels * k : 2 * channels * (k + 1), :] = jnp.concatenate(both, 0)

    at = 0
    for product, single in plan:
        columns = slice(at, at + product * LANES)
        result_ref[:, columns] = by_product(table_ref, slot_ref, weight_ref, columns, channels)
        for k in range(product, product + single):
            columns = slice(at + k * LANES, at + (k + 1) * LANES)
            result_ref[:, columns] = by_lanes(ret_ref, slot_ref, weight_ref, columns)
        at += (product + single) * LANES


def plan_of(blocks):
    turns = max(t for t in (3, 2, 1) if blocks % t == 0)
    size = blocks // turns
    return [(size - size // 3, size // 3)] * turns


def chunk_of(fine, most):
    return max(c for c in range(LANES, most + 1, LANES) if fine % c == 0)


def call(kernel, ins, out, scratch=(), grid=(), in_specs=VMEM, out_specs=VMEM, memory=16, cost=None):
    single = isinstance(in_specs, pl.BlockSpec)
    return pl.pallas_call(
        kernel,
        grid=grid,
        out_shape=out,
        in_specs=[in_specs] * len(ins) if single else in_specs,
        out_specs=[out_specs] * len(out) if isinstance(out, list) else out_specs,
        scratch_shapes=list(scratch),
        cost_estimate=cost,
        compiler_params=pltpu.CompilerParams(vmem_limit_bytes=memory << 20),
    )(*ins)


def body(increment, send_slots, tent_weight, coarse_cell, diffusivity):
    channels, fine = increment.shape
    slot_count = coarse_cell.shape[0]
    rows, width = diffusivity.shape
    tiles = lax.axis_size("tile")
    share = slot_count // tiles
    blocks = slot_count // LANES
    wide = 2 * LANES
    on_chip = [(i, i ^ 1) for i in range(tiles)]
    off_chip = [(i, (i + 2 * (i % 2) - 1) % tiles) for i in range(tiles)]
    shape = jax.ShapeDtypeStruct
    slots = send_slots.T
    cells = coarse_cell.reshape(blocks, LANES)
    chunk = chunk_of(fine, 2304)
    grid = (fine // chunk,)
    part = lambda n: pl.BlockSpec((n, chunk), lambda i: (0, i))
    whole = pl.BlockSpec((blocks, channels, LANES), lambda i: (0, 0, 0))

    sent = call(
        sum_to_slots,
        (increment, slots, tent_weight),
        shape((blocks, channels, LANES), F32),
        grid=grid,
        in_specs=[part(channels), part(CORNERS), part(CORNERS)],
        out_specs=whole,
        memory=56,
    )
    received = exchange(sent, tiles, share)
    edge = shape((EDGE, channels, LANES), F32)
    slot_blocks = shape((blocks, channels, LANES), F32)
    edge_rows = shape((2 * STEPS, channels, wide), F32)
    edges, near, far = call(
        functools.partial(sum_edges, width=width), (received, cells, diffusivity), [edge_rows, edge, edge]
    )
    far = lax.ppermute(far, "tile", off_chip)
    near = lax.ppermute(near, "tile", on_chip)
    own = pltpu.VMEM((rows, channels, wide), F32)
    kept, inner, found = call(
        functools.partial(diffuse_inner, width=width),
        (received, edges, diffusivity, cells),
        [shape((STEPS - 1, 4, channels, wide), F32), shape((rows - 2 * STEPS, channels, wide), F32), slot_blocks],
        [own, own, own, pltpu.VMEM((rows, wide), F32)],
        cost=pl.CostEstimate(flops=4 * slot_count * wide * wide, bytes_accessed=8 << 20, transcendentals=0),
    )
    padded = pltpu.VMEM((rows + 2 * STEPS, channels, wide), F32)
    outer, values = call(
        functools.partial(diffuse_outer, width=width),
        (edges, near, far, diffusivity, cells, kept, found),
        [edge_rows, slot_blocks],
        [padded, padded, pltpu.VMEM((rows + 2 * STEPS, wide), F32)],
    )
    field = call(
        join_rows,
        (inner, outer),
        shape((rows, channels, width), F32),
        cost=pl.CostEstimate(flops=rows * channels * wide, bytes_accessed=4 << 20, transcendentals=0),
    )
    returned = exchange(values, tiles, share)
    field, tent_weight = lax.optimization_barrier((field, tent_weight))
    result = call(
        functools.partial(sum_from_slots, plan=plan_of(chunk // LANES)),
        (returned, slots, tent_weight),
        shape((channels, fine), F32),
        [pltpu.VMEM((2 * channels * slot_count // PLACES, PLACES), BF16)],
        grid=grid,
        in_specs=[whole, part(CORNERS), part(CORNERS)],
        out_specs=part(channels),
        memory=32,
    )
    return (result, field.transpose(1, 0, 2))


def exchange(blocks, tiles, share):
    count, channels, lanes = blocks.shape
    if share == lanes:
        return lax.all_to_all(blocks, "tile", split_axis=0, concat_axis=0, tiled=True)
    flat = blocks.transpose(1, 0, 2).reshape(channels, count * lanes)
    flat = lax.all_to_all(flat, "tile", split_axis=1, concat_axis=1, tiled=True)
    return flat.reshape(channels, count, lanes).transpose(1, 0, 2)


def solution(mesh):
    in_specs = (
        P(None, ("group", "tile")),
        P("tile", None),
        P(None, "tile"),
        P("tile"),
        P("tile", None),
    )
    out_specs = (P(None, ("group", "tile")), P(None, ("group", "tile"), None))
    return jax.shard_map(body, mesh=mesh, in_specs=in_specs, out_specs=out_specs, check_vma=False)
```

```python
import functools

import jax
import jax.numpy as jnp
from jax import lax
from jax.experimental import pallas as pl
from jax.experimental.pallas import tpu as pltpu
from jax.sharding import PartitionSpec as P

STEPS = 5
CORNERS = 4
LANES = 128
PLACES = 256
EDGE = STEPS + (STEPS + 1) // 2
BF16 = jnp.bfloat16
F32 = jnp.float32
VMEM = pl.BlockSpec(memory_space=pltpu.VMEM)


def halves(values):
    high = values.astype(BF16)
    return high, (values - high.astype(F32)).astype(BF16)


def one_hot(places, length):
    rows = lax.broadcasted_iota(jnp.int32, (length, places.shape[1]), 0)
    return jnp.where(rows == places, 1.0, 0.0).astype(BF16)


def masked(values, marks, wanted):
    marks = jnp.broadcast_to(marks, values.shape)
    zero = jnp.zeros((), values.dtype)
    return jnp.concatenate([jnp.where(marks == k, values, zero) for k in wanted], 0)


def dot_last(left, right):
    return lax.dot_general(left, right, (((1,), (1,)), ((), ())), preferred_element_type=F32)


def sum_to_slots(inc_ref, slot_ref, weight_ref, sent_ref):
    channels = inc_ref.shape[0]
    count = sent_ref.shape[0] * LANES // PLACES
    inc = inc_ref[...]
    left, right = [], []
    for corner in range(CORNERS):
        slots = slot_ref[corner : corner + 1, :]
        parts = jnp.concatenate(halves(weight_ref[corner : corner + 1, :] * inc), 0)
        left.append(masked(parts, slots // PLACES, range(count)))
        right.append(one_hot(slots % PLACES, PLACES))
    sums = dot_last(jnp.concatenate(left, 1), jnp.concatenate(right, 1))

    @pl.when(pl.program_id(0) == 0)
    def _():
        sent_ref[...] = jnp.zeros_like(sent_ref)

    for k in range(count):
        both = sums[2 * channels * k : 2 * channels * (k + 1)]
        both = both[:channels] + both[channels:]
        for part in range(PLACES // LANES):
            sent_ref[k * (PLACES // LANES) + part] += both[:, LANES * part : LANES * (part + 1)]


def column_at(lanes, width):
    half, extra = width // 2, (LANES - width // 2) // 2
    odd = lanes // LANES
    at = lanes % LANES
    at = jnp.where(at < half, at, jnp.where(at < half + extra, at - half, at - LANES + half))
    return 2 * at + odd


def lane_of(x):
    return LANES * (x % 2) + x // 2


def narrowed(row, width):
    half = width // 2
    return jnp.concatenate([row[:, :half], row[:, LANES : LANES + half]], 1)


def widened(row):
    half = row.shape[1] // 2
    extra = (LANES - half) // 2
    out = []
    for part in (row[:, :half], row[:, half:]):
        out += [part, part[:, :extra], part[:, half - extra :]]
    return jnp.concatenate(out, 1)


def spread_columns(plain, width):
    sides = [plain[:, :LANES], jnp.concatenate([plain[:, LANES:width], plain[:, : 2 * LANES - width]], 1)]
    out = []
    for odd in range(2):
        x = column_at(lax.broadcasted_iota(jnp.int32, sides[0].shape, 1) + odd * LANES, width)
        found = [jnp.take_along_axis(side, x % LANES, axis=1) for side in sides]
        out.append(jnp.where(x < LANES, found[0], found[1]))
    return jnp.concatenate(out, 1)


def place_edge(edge_ref, rows, coefs, width):
    half = width - LANES
    rows = [narrowed(row, width) for row in rows]
    for k, row in enumerate(rows):
        edge_ref[k] = row[:, :LANES]
    ends = [row[:, LANES:] for row in rows]
    for k in range(0, STEPS - 1, 2):
        edge_ref[STEPS + k // 2] = jnp.concatenate([ends[k], ends[k + 1]], 1)
    edge_ref[EDGE - 1] = jnp.concatenate([ends[-1], jnp.zeros_like(ends[-1])], 1)
    for k, coef in enumerate(coefs):
        coef = narrowed(coef, width)
        for part in range(3):
            edge_ref[EDGE - 1, 3 * k + part : 3 * k + part + 1, half:] = coef[:, half * part : half * (part + 1)]


def read_edge(edge_ref, k, width):
    half = width - LANES
    end = edge_ref[STEPS + k // 2, :, half * (k % 2) : half * (k % 2) + half]
    return widened(jnp.concatenate([edge_ref[k], end], 1))


def read_coef(edge_ref, k, width):
    half = width - LANES
    parts = [edge_ref[EDGE - 1, 3 * k + part : 3 * k + part + 1, half:] for part in range(3)]
    return widened(jnp.concatenate(parts, 1))


def cell_sums(rec_ref, cell_ref, ys, width):
    senders, channels, _ = rec_ref.shape
    cells = jnp.concatenate([cell_ref[s : s + 1, :] for s in range(senders)], 1)
    values = jnp.concatenate([rec_ref[s] for s in range(senders)], 1)
    y = cells // width
    columns = column_at(lax.broadcasted_iota(jnp.int32, (2 * LANES, 1), 0), width)
    right = jnp.where(columns == cells - y * width, 1.0, 0.0).astype(BF16)
    sums = dot_last(masked(jnp.concatenate(halves(values), 0), y, ys), right)
    full = []
    for k in range(len(ys)):
        both = sums[2 * channels * k : 2 * channels * (k + 1)]
        full.append(both[:channels] + both[channels:])
    return full


def edges_of(rows):
    return list(range(STEPS)) + list(range(rows - STEPS, rows))


def sum_edges(rec_ref, cell_ref, own_ref, edges_ref, near_ref, far_ref, coef_ref, plain_ref, *, width):
    rows = own_ref.shape[0]
    plain_ref[...] = jnp.zeros_like(plain_ref)
    plain_ref[:rows] = own_ref[...]
    for k in range(0, plain_ref.shape[0], 8):
        coef_ref[k : k + 8, :] = spread_columns(plain_ref[k : k + 8, :], width)
    full = cell_sums(rec_ref, cell_ref, edges_of(rows), width)
    for k, row in enumerate(full):
        edges_ref[k] = row
    coefs = [coef_ref[k : k + 1, :] for k in range(rows)]
    even = lax.axis_index("tile") % 2 == 0

    def place(head_ref, tail_ref):
        place_edge(head_ref, full[:STEPS], coefs[:STEPS], width)
        place_edge(tail_ref, full[STEPS:], coefs[rows - STEPS :], width)

    pl.when(even)(lambda: place(far_ref, near_ref))
    pl.when(jnp.logical_not(even))(lambda: place(near_ref, far_ref))


def stepped(above, here, below, coef):
    even, odd = here[:, :LANES], here[:, LANES:]
    sides = jnp.concatenate([pltpu.roll(odd, 1, 1) + odd, even + pltpu.roll(even, LANES - 1, 1)], 1)
    spread = below + above + sides
    return here + coef * (spread - 4.0 * here)


def kept_rows(turn, total):
    first, last = STEPS + turn, total - STEPS - turn
    return [first, first + 1, last - 2, last - 1]


def read_rows(final_rows, ys, cell_ref, values_ref, base, width):
    senders, channels, _ = values_ref.shape
    left = jnp.concatenate([jnp.concatenate(halves(row), 0) for row in final_rows], 0)
    for s in range(0, senders, 2):
        cells = jnp.concatenate([cell_ref[s : s + 1, :], cell_ref[s + 1 : s + 2, :]], 1)
        y = cells // width
        found = jnp.dot(left, one_hot(lane_of(cells - y * width), left.shape[1]), preferred_element_type=F32)
        out = base(s)
        marks = jnp.broadcast_to(y, out.shape)
        for k, row in enumerate(ys):
            both = found[2 * channels * k : 2 * channels * (k + 1)]
            out = jnp.where(marks == row, both[:channels] + both[channels:], out)
        values_ref[s] = out[:, :LANES]
        values_ref[s + 1] = out[:, LANES:]


def diffuse_inner(
    rec_ref, edges_ref, coef_ref, cell_ref, kept_ref, inner_ref, values_ref, start_ref, one_ref, two_ref, *, width
):
    rows, channels, wide = start_ref.shape
    for k, y in enumerate(edges_of(rows)):
        start_ref[y] = edges_ref[k]
    ys = range(STEPS, rows - STEPS)
    for y, row in zip(ys, cell_sums(rec_ref, cell_ref, ys, width)):
        start_ref[y] = row
    held, other, last = start_ref, one_ref, two_ref
    for turn in range(1, STEPS + 1):
        for y in range(turn, rows - turn):
            other[y] = stepped(held[y - 1], held[y], held[y + 1], coef_ref[y : y + 1, :])
        if turn < STEPS:
            for place, y in enumerate(kept_rows(turn, rows + 2 * STEPS)):
                kept_ref[turn - 1, place] = other[y - STEPS]
        held, other, last = other, last, other
    for y in ys:
        inner_ref[y - STEPS] = held[y]
    nothing = lambda s: jnp.zeros((channels, 2 * LANES), F32)
    read_rows([held[y] for y in ys], ys, cell_ref, values_ref, nothing, width)


def diffuse_outer(
    edges_ref, near_ref, far_ref, own_ref, cell_ref, kept_ref, part_ref,
    outer_ref, values_ref, one_ref, two_ref, coef_ref, *, width
):
    total = coef_ref.shape[0]
    rows = total - 2 * STEPS
    coef_ref[STEPS : STEPS + rows, :] = own_ref[:rows, :]
    even = lax.axis_index("tile") % 2 == 0

    def read(before_ref, after_ref):
        for k in range(STEPS):
            one_ref[k] = read_edge(before_ref, k, width)
            one_ref[STEPS + rows + k] = read_edge(after_ref, k, width)
            coef_ref[k : k + 1, :] = read_coef(before_ref, k, width)
            coef_ref[STEPS + rows + k : STEPS + rows + k + 1, :] = read_coef(after_ref, k, width)

    pl.when(even)(lambda: read(far_ref, near_ref))
    pl.when(jnp.logical_not(even))(lambda: read(near_ref, far_ref))
    ys = edges_of(rows)
    held, other = one_ref, two_ref
    for turn in range(1, STEPS + 1):

        def row(y):
            if turn == 1 and y - STEPS in ys:
                return edges_ref[ys.index(y - STEPS)]
            kept = kept_rows(turn - 1, total) if turn > 1 else []
            return kept_ref[turn - 2, kept.index(y)] if y in kept else held[y]

        for start in (turn, total - STEPS - turn):
            for y in range(start, start + STEPS):
                other[y] = stepped(row(y - 1), row(y), row(y + 1), coef_ref[y : y + 1, :])
        held, other = other, held
    final = [held[y + STEPS] for y in ys]
    for k, row in enumerate(final):
        outer_ref[k] = row
    base = lambda s: jnp.concatenate([part_ref[s], part_ref[s + 1]], 1)
    read_rows(final, ys, cell_ref, values_ref, base, width)


def join_rows(inner_ref, outer_ref, field_ref):
    rows, channels, width = field_ref.shape
    ys = edges_of(rows)
    group = 8
    lanes = lax.broadcasted_iota(jnp.int32, (group, LANES), 1)
    for y in range(rows):
        row_ref = outer_ref.at[ys.index(y)] if y in ys else inner_ref.at[y - STEPS]
        for c in range(0, channels, group):
            even, odd = row_ref[c : c + group, :LANES], row_ref[c : c + group, LANES:]
            for start in range(0, width, LANES):
                at = (start + lanes) // 2
                found = [jnp.take_along_axis(part, at, axis=1) for part in (even, odd)]
                size = min(LANES, width - start)
                out = jnp.where(lanes % 2 == 0, found[0], found[1])
                field_ref[y, c : c + group, start : start + size] = out[:, :size]


def by_product(table_ref, slot_ref, weight_ref, columns, channels):
    count = table_ref.shape[0] // (2 * channels)
    total = 0.0
    for corner in range(CORNERS):
        slots = slot_ref[corner : corner + 1, columns]
        found = jnp.dot(table_ref[...], one_hot(slots % PLACES, PLACES), preferred_element_type=F32)
        marks = jnp.broadcast_to(slots // PLACES, (channels, slots.shape[1]))
        out = None
        for k in range(count):
            both = found[2 * channels * k : 2 * channels * (k + 1)]
            both = both[:channels] + both[channels:]
            out = both if out is None else jnp.where(marks == k, both, out)
        total = total + weight_ref[corner : corner + 1, columns] * out
    return total


def by_lanes(ret_ref, slot_ref, weight_ref, columns):
    blocks, channels, _ = ret_ref.shape
    group = 8
    totals = [0.0] * (channels // group)
    for corner in range(CORNERS):
        slots = slot_ref[corner : corner + 1, columns]
        weight = weight_ref[corner : corner + 1, columns]
        lanes = jnp.broadcast_to(slots % LANES, (group, LANES))
        block = jnp.broadcast_to(slots // LANES, (group, LANES))
        marks = [block == k for k in range(blocks)]
        for c in range(channels // group):
            out = None
            for k in range(blocks):
                found = jnp.take_along_axis(ret_ref[k, group * c : group * (c + 1), :], lanes, axis=1)
                out = found if out is None else jnp.where(marks[k], found, out)
            totals[c] = totals[c] + weight * out
    return jnp.concatenate(totals, 0)


def sum_from_slots(ret_ref, slot_ref, weight_ref, result_ref, table_ref, *, plan):
    blocks, channels, _ = ret_ref.shape
    group = PLACES // LANES

    @pl.when(pl.program_id(0) == 0)
    def _():
        for k in range(blocks // group):
            both = halves(jnp.concatenate([ret_ref[group * k + part] for part in range(group)], 1))
            table_ref[2 * channels * k : 2 * channels * (k + 1), :] = jnp.concatenate(both, 0)

    at = 0
    for product, single in plan:
        columns = slice(at, at + product * LANES)
        result_ref[:, columns] = by_product(table_ref, slot_ref, weight_ref, columns, channels)
        for k in range(product, product + single):
            columns = slice(at + k * LANES, at + (k + 1) * LANES)
            result_ref[:, columns] = by_lanes(ret_ref, slot_ref, weight_ref, columns)
        at += (product + single) * LANES


def plan_of(blocks):
    turns = max(t for t in (3, 2, 1) if blocks % t == 0)
    size = blocks // turns
    return [(size - size // 3, size // 3)] * turns


def chunk_of(fine, most):
    return max(c for c in range(LANES, most + 1, LANES) if fine % c == 0)


def call(kernel, ins, out, scratch=(), grid=(), in_specs=VMEM, out_specs=VMEM, memory=16, cost=None):
    single = isinstance(in_specs, pl.BlockSpec)
    return pl.pallas_call(
        kernel,
        grid=grid,
        out_shape=out,
        in_specs=[in_specs] * len(ins) if single else in_specs,
        out_specs=[out_specs] * len(out) if isinstance(out, list) else out_specs,
        scratch_shapes=list(scratch),
        cost_estimate=cost,
        compiler_params=pltpu.CompilerParams(vmem_limit_bytes=memory << 20),
    )(*ins)


def body(increment, send_slots, tent_weight, coarse_cell, diffusivity):
    channels, fine = increment.shape
    slot_count = coarse_cell.shape[0]
    rows, width = diffusivity.shape
    tiles = lax.axis_size("tile")
    share = slot_count // tiles
    blocks = slot_count // LANES
    wide = 2 * LANES
    on_chip = [(i, i ^ 1) for i in range(tiles)]
    off_chip = [(i, (i + 2 * (i % 2) - 1) % tiles) for i in range(tiles)]
    shape = jax.ShapeDtypeStruct
    slots = send_slots.T
    cells = coarse_cell.reshape(blocks, LANES)
    chunk = chunk_of(fine, 2304)
    grid = (fine // chunk,)
    part = lambda n: pl.BlockSpec((n, chunk), lambda i: (0, i))
    whole = pl.BlockSpec((blocks, channels, LANES), lambda i: (0, 0, 0))

    sent = call(
        sum_to_slots,
        (increment, slots, tent_weight),
        shape((blocks, channels, LANES), F32),
        grid=grid,
        in_specs=[part(channels), part(CORNERS), part(CORNERS)],
        out_specs=whole,
        memory=56,
    )
    received = exchange(sent, tiles, share)
    edge = shape((EDGE, channels, LANES), F32)
    slot_blocks = shape((blocks, channels, LANES), F32)
    edge_rows = shape((2 * STEPS, channels, wide), F32)
    tall = -(-rows // 8) * 8
    edges, near, far, coef = call(
        functools.partial(sum_edges, width=width),
        (received, cells, diffusivity),
        [edge_rows, edge, edge, shape((tall, wide), F32)],
        [pltpu.VMEM((tall, width), F32)],
    )
    far = lax.ppermute(far, "tile", off_chip)
    near = lax.ppermute(near, "tile", on_chip)
    own = pltpu.VMEM((rows, channels, wide), F32)
    kept, inner, found = call(
        functools.partial(diffuse_inner, width=width),
        (received, edges, coef, cells),
        [shape((STEPS - 1, 4, channels, wide), F32), shape((rows - 2 * STEPS, channels, wide), F32), slot_blocks],
        [own, own, own],
        cost=pl.CostEstimate(flops=4 * slot_count * wide * wide, bytes_accessed=8 << 20, transcendentals=0),
    )
    padded = pltpu.VMEM((rows + 2 * STEPS, channels, wide), F32)
    outer, values = call(
        functools.partial(diffuse_outer, width=width),
        (edges, near, far, coef, cells, kept, found),
        [edge_rows, slot_blocks],
        [padded, padded, pltpu.VMEM((rows + 2 * STEPS, wide), F32)],
    )
    field = call(
        join_rows,
        (inner, outer),
        shape((rows, channels, width), F32),
        cost=pl.CostEstimate(flops=rows * channels * wide, bytes_accessed=4 << 20, transcendentals=0),
    )
    returned = exchange(values, tiles, share)
    field, tent_weight = lax.optimization_barrier((field, tent_weight))
    result = call(
        functools.partial(sum_from_slots, plan=plan_of(chunk // LANES)),
        (returned, slots, tent_weight),
        shape((channels, fine), F32),
        [pltpu.VMEM((2 * channels * slot_count // PLACES, PLACES), BF16)],
        grid=grid,
        in_specs=[whole, part(CORNERS), part(CORNERS)],
        out_specs=part(channels),
        memory=32,
    )
    return (result, field.transpose(1, 0, 2))


def exchange(blocks, tiles, share):
    count, channels, lanes = blocks.shape
    if share == lanes:
        return lax.all_to_all(blocks, "tile", split_axis=0, concat_axis=0, tiled=True)
    flat = blocks.transpose(1, 0, 2).reshape(channels, count * lanes)
    flat = lax.all_to_all(flat, "tile", split_axis=1, concat_axis=1, tiled=True)
    return flat.reshape(channels, count, lanes).transpose(1, 0, 2)


def solution(mesh):
    in_specs = (
        P(None, ("group", "tile")),
        P("tile", None),
        P(None, "tile"),
        P("tile"),
        P("tile", None),
    )
    out_specs = (P(None, ("group", "tile")), P(None, ("group", "tile"), None))
    return jax.shard_map(body, mesh=mesh, in_specs=in_specs, out_specs=out_specs, check_vma=False)
```

```python
import functools

import jax
import jax.numpy as jnp
from jax import lax
from jax.experimental import pallas as pl
from jax.experimental.pallas import tpu as pltpu
from jax.sharding import PartitionSpec as P

STEPS = 5
CORNERS = 4
LANES = 128
PLACES = 256
EDGE = STEPS + (STEPS + 1) // 2
BF16 = jnp.bfloat16
F32 = jnp.float32
VMEM = pl.BlockSpec(memory_space=pltpu.VMEM)


def halves(values):
    high = values.astype(BF16)
    return high, (values - high.astype(F32)).astype(BF16)


def one_hot(places, length):
    rows = lax.broadcasted_iota(jnp.int32, (length, places.shape[1]), 0)
    return jnp.where(rows == places, 1.0, 0.0).astype(BF16)


def masked(values, marks, wanted):
    marks = jnp.broadcast_to(marks, values.shape)
    zero = jnp.zeros((), values.dtype)
    return jnp.concatenate([jnp.where(marks == k, values, zero) for k in wanted], 0)


def dot_last(left, right):
    return lax.dot_general(left, right, (((1,), (1,)), ((), ())), preferred_element_type=F32)


def sum_to_slots(inc_ref, slot_ref, weight_ref, sent_ref):
    channels = inc_ref.shape[0]
    count = sent_ref.shape[0] * LANES // PLACES
    inc = inc_ref[...]
    left, right = [], []
    for corner in range(CORNERS):
        slots = slot_ref[corner : corner + 1, :]
        parts = jnp.concatenate(halves(weight_ref[corner : corner + 1, :] * inc), 0)
        left.append(masked(parts, slots // PLACES, range(count)))
        right.append(one_hot(slots % PLACES, PLACES))
    sums = dot_last(jnp.concatenate(left, 1), jnp.concatenate(right, 1))

    @pl.when(pl.program_id(0) == 0)
    def _():
        sent_ref[...] = jnp.zeros_like(sent_ref)

    for k in range(count):
        both = sums[2 * channels * k : 2 * channels * (k + 1)]
        both = both[:channels] + both[channels:]
        for part in range(PLACES // LANES):
            sent_ref[k * (PLACES // LANES) + part] += both[:, LANES * part : LANES * (part + 1)]


def wide_column(width):
    lanes = lax.broadcasted_iota(jnp.int32, (2 * LANES, 1), 0)
    extra = (2 * LANES - width) // 2
    return jnp.where(lanes < width, lanes, jnp.where(lanes < width + extra, lanes - width, lanes - 2 * LANES + width))


def place_edge(edge_ref, rows, coefs, width):
    half = width - LANES
    for k, row in enumerate(rows):
        edge_ref[k] = row[:, :LANES]
    ends = [row[:, LANES:width] for row in rows]
    for k in range(0, STEPS - 1, 2):
        edge_ref[STEPS + k // 2] = jnp.concatenate([ends[k], ends[k + 1]], 1)
    edge_ref[EDGE - 1] = jnp.concatenate([ends[-1], jnp.zeros_like(ends[-1])], 1)
    for k, coef in enumerate(coefs):
        for part in range(3):
            edge_ref[EDGE - 1, 3 * k + part : 3 * k + part + 1, half:] = coef[:, half * part : half * (part + 1)]


def read_edge(edge_ref, k, width):
    half = width - LANES
    start = edge_ref[k]
    end = edge_ref[STEPS + k // 2, :, half * (k % 2) : half * (k % 2) + half]
    return widened([start, end], start, end, width)


def read_coef(edge_ref, k, width):
    half = width - LANES
    parts = [edge_ref[EDGE - 1, 3 * k + part : 3 * k + part + 1, half:] for part in range(3)]
    return widened(parts, parts[0], parts[2], width)


def widened(parts, start, end, width):
    extra = (2 * LANES - width) // 2
    return jnp.concatenate(parts + [start[:, :extra], end[:, end.shape[1] - extra :]], 1)


def cell_sums(rec_ref, cell_ref, ys, width):
    senders, channels, _ = rec_ref.shape
    cells = jnp.concatenate([cell_ref[s : s + 1, :] for s in range(senders)], 1)
    values = jnp.concatenate([rec_ref[s] for s in range(senders)], 1)
    y = cells // width
    right = jnp.where(wide_column(width) == cells - y * width, 1.0, 0.0).astype(BF16)
    sums = dot_last(masked(jnp.concatenate(halves(values), 0), y, ys), right)
    full = []
    for k in range(len(ys)):
        both = sums[2 * channels * k : 2 * channels * (k + 1)]
        full.append(both[:channels] + both[channels:])
    return full


def edges_of(rows):
    return list(range(STEPS)) + list(range(rows - STEPS, rows))


def edge_starts(rows):
    even = lax.axis_index("tile") % 2 == 0
    return jnp.where(even, 0, rows - STEPS), jnp.where(even, rows - STEPS, 0)


def sum_far(rec_ref, cell_ref, coef_ref, far_rows_ref, far_ref, *, width):
    start, _ = edge_starts(coef_ref.shape[0])
    full = cell_sums(rec_ref, cell_ref, [start + k for k in range(STEPS)], width)
    for k, row in enumerate(full):
        far_rows_ref[k] = row
    place_edge(far_ref, full, [coef_ref[pl.ds(start + k, 1), :] for k in range(STEPS)], width)


def sum_rest(rec_ref, cell_ref, coef_ref, far_rows_ref, start_ref, near_ref, *, width):
    rows = coef_ref.shape[0]
    far, near = edge_starts(rows)
    ys = [near + k for k in range(STEPS)] + list(range(STEPS, rows - STEPS))
    full = cell_sums(rec_ref, cell_ref, ys, width)
    for y, row in zip(ys, full):
        start_ref[y] = row
    for k in range(STEPS):
        start_ref[far + k] = far_rows_ref[k]
    place_edge(near_ref, full[:STEPS], [coef_ref[pl.ds(near + k, 1), :] for k in range(STEPS)], width)


def stepped(above, here, below, coef):
    wide = here.shape[-1]
    spread = below + above + pltpu.roll(here, 1, 1) + pltpu.roll(here, wide - 1, 1)
    return here + coef * (spread - 4.0 * here)


def kept_rows(turn, total):
    first, last = STEPS + turn, total - STEPS - turn
    return [first, first + 1, last - 2, last - 1]


def read_rows(final_rows, ys, cell_ref, values_ref, base, width):
    senders, channels, _ = values_ref.shape
    left = jnp.concatenate([jnp.concatenate(halves(row), 0) for row in final_rows], 0)
    for s in range(0, senders, 2):
        cells = jnp.concatenate([cell_ref[s : s + 1, :], cell_ref[s + 1 : s + 2, :]], 1)
        y = cells // width
        found = jnp.dot(left, one_hot(cells - y * width, left.shape[1]), preferred_element_type=F32)
        out = base(s)
        marks = jnp.broadcast_to(y, out.shape)
        for k, row in enumerate(ys):
            both = found[2 * channels * k : 2 * channels * (k + 1)]
            out = jnp.where(marks == row, both[:channels] + both[channels:], out)
        values_ref[s] = out[:, :LANES]
        values_ref[s + 1] = out[:, LANES:]


def diffuse_inner(
    start_ref, own_ref, cell_ref, kept_ref, inner_ref, values_ref, one_ref, two_ref, coef_ref, *, width
):
    rows, channels, wide = start_ref.shape
    own = own_ref[...]
    coef_ref[...] = widened([own], own, own, width)
    ys = range(STEPS, rows - STEPS)
    held, other, last = start_ref, one_ref, two_ref
    for turn in range(1, STEPS + 1):
        for y in range(turn, rows - turn):
            other[y] = stepped(held[y - 1], held[y], held[y + 1], coef_ref[y : y + 1, :])
        if turn < STEPS:
            for place, y in enumerate(kept_rows(turn, rows + 2 * STEPS)):
                kept_ref[turn - 1, place] = other[y - STEPS]
        held, other, last = other, last, other
    for y in ys:
        inner_ref[y - STEPS] = held[y]
    nothing = lambda s: jnp.zeros((channels, 2 * LANES), F32)
    read_rows([held[y] for y in ys], ys, cell_ref, values_ref, nothing, width)


def diffuse_outer(
    start_ref, near_ref, far_ref, own_ref, cell_ref, kept_ref, part_ref,
    outer_ref, values_ref, one_ref, two_ref, coef_ref, *, width
):
    rows = own_ref.shape[0]
    total = rows + 2 * STEPS
    own = own_ref[...]
    coef_ref[STEPS : STEPS + rows, :] = widened([own], own, own, width)
    even = lax.axis_index("tile") % 2 == 0

    def read(before_ref, after_ref):
        for k in range(STEPS):
            one_ref[k] = read_edge(before_ref, k, width)
            one_ref[STEPS + rows + k] = read_edge(after_ref, k, width)
            coef_ref[k : k + 1, :] = read_coef(before_ref, k, width)
            coef_ref[STEPS + rows + k : STEPS + rows + k + 1, :] = read_coef(after_ref, k, width)

    pl.when(even)(lambda: read(far_ref, near_ref))
    pl.when(jnp.logical_not(even))(lambda: read(near_ref, far_ref))
    ys = edges_of(rows)
    held, other = one_ref, two_ref
    for turn in range(1, STEPS + 1):

        def row(y):
            if turn == 1 and y - STEPS in ys:
                return start_ref[y - STEPS]
            kept = kept_rows(turn - 1, total) if turn > 1 else []
            return kept_ref[turn - 2, kept.index(y)] if y in kept else held[y]

        for start in (turn, total - STEPS - turn):
            for y in range(start, start + STEPS):
                other[y] = stepped(row(y - 1), row(y), row(y + 1), coef_ref[y : y + 1, :])
        held, other = other, held
    final = [held[y + STEPS] for y in ys]
    for k, row in enumerate(final):
        outer_ref[k] = row
    base = lambda s: jnp.concatenate([part_ref[s], part_ref[s + 1]], 1)
    read_rows(final, ys, cell_ref, values_ref, base, width)


def by_product(table_ref, slot_ref, weight_ref, columns, channels):
    count = table_ref.shape[0] // (2 * channels)
    total = 0.0
    for corner in range(CORNERS):
        slots = slot_ref[corner : corner + 1, columns]
        found = jnp.dot(table_ref[...], one_hot(slots % PLACES, PLACES), preferred_element_type=F32)
        marks = jnp.broadcast_to(slots // PLACES, (channels, slots.shape[1]))
        out = None
        for k in range(count):
            both = found[2 * channels * k : 2 * channels * (k + 1)]
            both = both[:channels] + both[channels:]
            out = both if out is None else jnp.where(marks == k, both, out)
        total = total + weight_ref[corner : corner + 1, columns] * out
    return total


def by_lanes(ret_ref, slot_ref, weight_ref, columns):
    blocks, channels, _ = ret_ref.shape
    group = 8
    totals = [0.0] * (channels // group)
    for corner in range(CORNERS):
        slots = slot_ref[corner : corner + 1, columns]
        weight = weight_ref[corner : corner + 1, columns]
        lanes = jnp.broadcast_to(slots % LANES, (group, LANES))
        block = jnp.broadcast_to(slots // LANES, (group, LANES))
        marks = [block == k for k in range(blocks)]
        for c in range(channels // group):
            out = None
            for k in range(blocks):
                found = jnp.take_along_axis(ret_ref[k, group * c : group * (c + 1), :], lanes, axis=1)
                out = found if out is None else jnp.where(marks[k], found, out)
            totals[c] = totals[c] + weight * out
    return jnp.concatenate(totals, 0)


def sum_from_slots(
    ret_ref, slot_ref, weight_ref, inner_ref, outer_ref, result_ref, field_ref, table_ref, *, plan
):
    blocks, channels, _ = ret_ref.shape
    some, _, width = field_ref.shape
    inner = inner_ref.shape[0]
    for k in range(some):
        y = pl.program_id(0) * some + k
        edge = jnp.where(y < STEPS, y, y - inner)
        is_inner = (y >= STEPS) & (y < STEPS + inner)
        within = jnp.clip(y - STEPS, 0, inner - 1)
        row = jnp.where(is_inner, inner_ref[within], outer_ref[jnp.clip(edge, 0, 2 * STEPS - 1)])
        field_ref[k] = row[:, :width]
    group = PLACES // LANES

    @pl.when(pl.program_id(0) == 0)
    def _():
        for k in range(blocks // group):
            both = halves(jnp.concatenate([ret_ref[group * k + part] for part in range(group)], 1))
            table_ref[2 * channels * k : 2 * channels * (k + 1), :] = jnp.concatenate(both, 0)

    at = 0
    for product, single in plan:
        columns = slice(at, at + product * LANES)
        result_ref[:, columns] = by_product(table_ref, slot_ref, weight_ref, columns, channels)
        for k in range(product, product + single):
            columns = slice(at + k * LANES, at + (k + 1) * LANES)
            result_ref[:, columns] = by_lanes(ret_ref, slot_ref, weight_ref, columns)
        at += (product + single) * LANES


def plan_of(blocks):
    turns = max(t for t in (3, 2, 1) if blocks % t == 0)
    size = blocks // turns
    return [(size - size // 3, size // 3)] * turns


def chunk_of(fine, most):
    return max(c for c in range(LANES, most + 1, LANES) if fine % c == 0)


def call(kernel, ins, out, scratch=(), grid=(), in_specs=VMEM, out_specs=VMEM, memory=16, cost=None):
    single = isinstance(in_specs, pl.BlockSpec)
    return pl.pallas_call(
        kernel,
        grid=grid,
        out_shape=out,
        in_specs=[in_specs] * len(ins) if single else in_specs,
        out_specs=[out_specs] * len(out) if single and isinstance(out, list) else out_specs,
        scratch_shapes=list(scratch),
        cost_estimate=cost,
        compiler_params=pltpu.CompilerParams(vmem_limit_bytes=memory << 20),
    )(*ins)


def body(increment, send_slots, tent_weight, coarse_cell, diffusivity):
    channels, fine = increment.shape
    slot_count = coarse_cell.shape[0]
    rows, width = diffusivity.shape
    tiles = lax.axis_size("tile")
    share = slot_count // tiles
    blocks = slot_count // LANES
    wide = 2 * LANES
    on_chip = [(i, i ^ 1) for i in range(tiles)]
    off_chip = [(i, (i + 2 * (i % 2) - 1) % tiles) for i in range(tiles)]
    shape = jax.ShapeDtypeStruct
    slots = send_slots.T
    cells = coarse_cell.reshape(blocks, LANES)
    chunk = chunk_of(fine, 2304)
    grid = (fine // chunk,)
    part = lambda n: pl.BlockSpec((n, chunk), lambda i: (0, i))
    whole = pl.BlockSpec((blocks, channels, LANES), lambda i: (0, 0, 0))

    sent = call(
        sum_to_slots,
        (increment, slots, tent_weight),
        shape((blocks, channels, LANES), F32),
        grid=grid,
        in_specs=[part(channels), part(CORNERS), part(CORNERS)],
        out_specs=whole,
        memory=56,
    )
    received = exchange(sent, tiles, share)
    edge = shape((EDGE, channels, LANES), F32)
    slot_blocks = shape((blocks, channels, LANES), F32)
    edge_rows = shape((2 * STEPS, channels, wide), F32)
    far_rows, far = call(
        functools.partial(sum_far, width=width),
        (received, cells, diffusivity),
        [shape((STEPS, channels, wide), F32), edge],
    )
    far = lax.ppermute(far, "tile", off_chip)
    start, near = call(
        functools.partial(sum_rest, width=width),
        (received, cells, diffusivity, far_rows),
        [shape((rows, channels, wide), F32), edge],
        cost=pl.CostEstimate(flops=2 * slot_count * wide * wide, bytes_accessed=4 << 20, transcendentals=0),
    )
    near = lax.ppermute(near, "tile", on_chip)
    own = pltpu.VMEM((rows, channels, wide), F32)
    kept, inner, found = call(
        functools.partial(diffuse_inner, width=width),
        (start, diffusivity, cells),
        [shape((STEPS - 1, 4, channels, wide), F32), shape((rows - 2 * STEPS, channels, wide), F32), slot_blocks],
        [own, own, pltpu.VMEM((rows, wide), F32)],
        cost=pl.CostEstimate(flops=4 * slot_count * wide * wide, bytes_accessed=8 << 20, transcendentals=0),
    )
    padded = pltpu.VMEM((rows + 2 * STEPS, channels, wide), F32)
    outer, values = call(
        functools.partial(diffuse_outer, width=width),
        (start, near, far, diffusivity, cells, kept, found),
        [edge_rows, slot_blocks],
        [padded, padded, pltpu.VMEM((rows + 2 * STEPS, wide), F32)],
    )
    returned = exchange(values, tiles, share)
    turns = fine // chunk
    some = rows // turns if rows % turns == 0 else rows
    all_of = lambda count: pl.BlockSpec((count, channels, wide), lambda i: (0, 0, 0))
    result, field = call(
        functools.partial(sum_from_slots, plan=plan_of(chunk // LANES)),
        (returned, slots, tent_weight, inner, outer),
        [shape((channels, fine), F32), shape((rows, channels, width), F32)],
        [pltpu.VMEM((2 * channels * slot_count // PLACES, PLACES), BF16)],
        grid=grid,
        in_specs=[whole, part(CORNERS), part(CORNERS), all_of(rows - 2 * STEPS), all_of(2 * STEPS)],
        out_specs=[part(channels), pl.BlockSpec((some, channels, width), lambda i: (i, 0, 0))],
        memory=32,
    )
    return (result, field.transpose(1, 0, 2))


def exchange(blocks, tiles, share):
    count, channels, lanes = blocks.shape
    if share == lanes:
        return lax.all_to_all(blocks, "tile", split_axis=0, concat_axis=0, tiled=True)
    flat = blocks.transpose(1, 0, 2).reshape(channels, count * lanes)
    flat = lax.all_to_all(flat, "tile", split_axis=1, concat_axis=1, tiled=True)
    return flat.reshape(channels, count, lanes).transpose(1, 0, 2)


def solution(mesh):
    in_specs = (
        P(None, ("group", "tile")),
        P("tile", None),
        P(None, "tile"),
        P("tile"),
        P("tile", None),
    )
    out_specs = (P(None, ("group", "tile")), P(None, ("group", "tile"), None))
    return jax.shard_map(body, mesh=mesh, in_specs=in_specs, out_specs=out_specs, check_vma=False)
```

```python
import functools

import jax
import jax.numpy as jnp
from jax import lax
from jax.experimental import pallas as pl
from jax.experimental.pallas import tpu as pltpu
from jax.sharding import PartitionSpec as P

STEPS = 5
CORNERS = 4
LANES = 128
PLACES = 256
EDGE = STEPS + (STEPS + 1) // 2
BF16 = jnp.bfloat16
F32 = jnp.float32
VMEM = pl.BlockSpec(memory_space=pltpu.VMEM)


def halves(values):
    high = values.astype(BF16)
    return high, (values - high.astype(F32)).astype(BF16)


def one_hot(places, length):
    rows = lax.broadcasted_iota(jnp.int32, (length, places.shape[1]), 0)
    return jnp.where(rows == places, 1.0, 0.0).astype(BF16)


def masked(values, marks, wanted):
    marks = jnp.broadcast_to(marks, values.shape)
    zero = jnp.zeros((), values.dtype)
    return jnp.concatenate([jnp.where(marks == k, values, zero) for k in wanted], 0)


def dot_last(left, right):
    return lax.dot_general(left, right, (((1,), (1,)), ((), ())), preferred_element_type=F32)


def sum_to_slots(inc_ref, slot_ref, weight_ref, sent_ref):
    channels = inc_ref.shape[0]
    count = sent_ref.shape[0] * LANES // PLACES
    inc = inc_ref[...]
    left, right = [], []
    for corner in range(CORNERS):
        slots = slot_ref[corner : corner + 1, :]
        parts = jnp.concatenate(halves(weight_ref[corner : corner + 1, :] * inc), 0)
        left.append(masked(parts, slots // PLACES, range(count)))
        right.append(one_hot(slots % PLACES, PLACES))
    sums = dot_last(jnp.concatenate(left, 1), jnp.concatenate(right, 1))

    @pl.when(pl.program_id(0) == 0)
    def _():
        sent_ref[...] = jnp.zeros_like(sent_ref)

    for k in range(count):
        both = sums[2 * channels * k : 2 * channels * (k + 1)]
        both = both[:channels] + both[channels:]
        for part in range(PLACES // LANES):
            sent_ref[k * (PLACES // LANES) + part] += both[:, LANES * part : LANES * (part + 1)]


def wide_column(width):
    lanes = lax.broadcasted_iota(jnp.int32, (2 * LANES, 1), 0)
    extra = (2 * LANES - width) // 2
    return jnp.where(lanes < width, lanes, jnp.where(lanes < width + extra, lanes - width, lanes - 2 * LANES + width))


def place_edge(edge_ref, rows, coefs, width):
    half = width - LANES
    for k, row in enumerate(rows):
        edge_ref[k] = row[:, :LANES]
    ends = [row[:, LANES:width] for row in rows]
    for k in range(0, STEPS - 1, 2):
        edge_ref[STEPS + k // 2] = jnp.concatenate([ends[k], ends[k + 1]], 1)
    edge_ref[EDGE - 1] = jnp.concatenate([ends[-1], jnp.zeros_like(ends[-1])], 1)
    for k, coef in enumerate(coefs):
        for part in range(3):
            edge_ref[EDGE - 1, 3 * k + part : 3 * k + part + 1, half:] = coef[:, half * part : half * (part + 1)]


def read_edge(edge_ref, k, width):
    half = width - LANES
    start = edge_ref[k]
    end = edge_ref[STEPS + k // 2, :, half * (k % 2) : half * (k % 2) + half]
    return widened([start, end], start, end, width)


def read_coef(edge_ref, k, width):
    half = width - LANES
    parts = [edge_ref[EDGE - 1, 3 * k + part : 3 * k + part + 1, half:] for part in range(3)]
    return widened(parts, parts[0], parts[2], width)


def widened(parts, start, end, width):
    extra = (2 * LANES - width) // 2
    return jnp.concatenate(parts + [start[:, :extra], end[:, end.shape[1] - extra :]], 1)


def cell_sums(rec_ref, cell_ref, ys, width):
    senders, channels, _ = rec_ref.shape
    cells = jnp.concatenate([cell_ref[s : s + 1, :] for s in range(senders)], 1)
    values = jnp.concatenate([rec_ref[s] for s in range(senders)], 1)
    y = cells // width
    right = jnp.where(wide_column(width) == cells - y * width, 1.0, 0.0).astype(BF16)
    sums = dot_last(masked(jnp.concatenate(halves(values), 0), y, ys), right)
    full = []
    for k in range(len(ys)):
        both = sums[2 * channels * k : 2 * channels * (k + 1)]
        full.append(both[:channels] + both[channels:])
    return full


def edge_starts(rows):
    even = lax.axis_index("tile") % 2 == 0
    return jnp.where(even, 0, rows - STEPS), jnp.where(even, rows - STEPS, 0)


def sum_edges(rec_ref, cell_ref, coef_ref, edges_ref, far_ref, near_ref, *, width):
    starts = edge_starts(coef_ref.shape[0])
    ys = [start + k for start in starts for k in range(STEPS)]
    full = cell_sums(rec_ref, cell_ref, ys, width)
    for k, row in enumerate(full):
        edges_ref[k] = row
    for edge_ref, at in ((far_ref, 0), (near_ref, STEPS)):
        coefs = [coef_ref[pl.ds(y, 1), :] for y in ys[at : at + STEPS]]
        place_edge(edge_ref, full[at : at + STEPS], coefs, width)


def stepped(above, here, below, coef):
    wide = here.shape[-1]
    spread = below + above + pltpu.roll(here, 1, 1) + pltpu.roll(here, wide - 1, 1)
    return here + coef * (spread - 4.0 * here)


def kept_rows(turn, total):
    first, last = STEPS + turn, total - STEPS - turn
    return [first, first + 1, last - 2, last - 1]


def read_rows(final_rows, ys, cell_ref, values_ref, base, width):
    senders, channels, _ = values_ref.shape
    left = jnp.concatenate([jnp.concatenate(halves(row), 0) for row in final_rows], 0)
    for s in range(0, senders, 2):
        cells = jnp.concatenate([cell_ref[s : s + 1, :], cell_ref[s + 1 : s + 2, :]], 1)
        y = cells // width
        found = jnp.dot(left, one_hot(cells - y * width, left.shape[1]), preferred_element_type=F32)
        out = base(s)
        marks = jnp.broadcast_to(y, out.shape)
        for k, row in enumerate(ys):
            both = found[2 * channels * k : 2 * channels * (k + 1)]
            out = jnp.where(marks == row, both[:channels] + both[channels:], out)
        values_ref[s] = out[:, :LANES]
        values_ref[s + 1] = out[:, LANES:]


def inner_rows(start_ref, own_ref, kept_ref, one_ref, two_ref, coef_ref, width):
    rows = start_ref.shape[0]
    own = own_ref[...]
    coef_ref[...] = widened([own], own, own, width)
    held, other, last = start_ref, one_ref, two_ref
    for turn in range(1, STEPS + 1):
        for y in range(turn, rows - turn):
            other[y] = stepped(held[y - 1], held[y], held[y + 1], coef_ref[y : y + 1, :])
        if turn < STEPS:
            for place, y in enumerate(kept_rows(turn, rows + 2 * STEPS)):
                kept_ref[turn - 1, place] = other[y - STEPS]
        held, other, last = other, last, other
    return [held[y] for y in range(STEPS, rows - STEPS)]


def side_rows(start_ref, edge_ref, own_ref, kept_ref, one_ref, two_ref, coef_ref, width, first):
    rows = own_ref.shape[0]
    head = first == 0
    flip = lambda ahead, behind: jnp.where(head, ahead, behind)
    for k in range(STEPS):
        place = flip(k, STEPS - 1 - k)
        one_ref[place] = read_edge(edge_ref, k, width)
        coef_ref[pl.ds(place, 1), :] = read_coef(edge_ref, k, width)
        own = own_ref[pl.ds(flip(k, rows - 1 - k), 1), :]
        coef_ref[STEPS + k : STEPS + k + 1, :] = widened([own], own, own, width)
    held, other = one_ref, two_ref
    for turn in range(1, STEPS + 1):

        def row(u):
            if turn == 1 and u >= STEPS:
                return start_ref[flip(u - STEPS, rows - 1 - u + STEPS)]
            if u >= STEPS + turn - 1:
                k = u - STEPS - turn + 1
                return kept_ref[turn - 2, flip(k, 3 - k)]
            return held[u]

        for u in range(turn, turn + STEPS):
            other[u] = stepped(row(u - 1), row(u), row(u + 1), coef_ref[u : u + 1, :])
        held, other = other, held
    return [held[flip(STEPS + k, 2 * STEPS - 1 - k)] for k in range(STEPS)]


def diffuse_most(
    rec_ref, edges_ref, edge_ref, own_ref, cell_ref, start_ref, kept_ref, inner_ref, side_ref, values_ref,
    one_ref, two_ref, coef_ref, side_one_ref, side_two_ref, side_coef_ref, *, width
):
    rows, channels, _ = start_ref.shape
    far, first = edge_starts(rows)
    for k in range(STEPS):
        start_ref[far + k] = edges_ref[k]
        start_ref[first + k] = edges_ref[STEPS + k]
    within = range(STEPS, rows - STEPS)
    for y, row in zip(within, cell_sums(rec_ref, cell_ref, within, width)):
        start_ref[y] = row
    inner = inner_rows(start_ref, own_ref, kept_ref, one_ref, two_ref, coef_ref, width)
    side = side_rows(
        start_ref, edge_ref, own_ref, kept_ref, side_one_ref, side_two_ref, side_coef_ref, width, first
    )
    for k, row in enumerate(inner):
        inner_ref[k] = row
    for k, row in enumerate(side):
        side_ref[k] = row
    ys = list(range(STEPS, rows - STEPS)) + [first + k for k in range(STEPS)]
    nothing = lambda s: jnp.zeros((channels, 2 * LANES), F32)
    read_rows(inner + side, ys, cell_ref, values_ref, nothing, width)


def diffuse_last(
    kept_ref, part_ref, start_ref, edge_ref, own_ref, cell_ref, side_ref, values_ref, one_ref, two_ref, coef_ref, *, width
):
    first, _ = edge_starts(own_ref.shape[0])
    side = side_rows(start_ref, edge_ref, own_ref, kept_ref, one_ref, two_ref, coef_ref, width, first)
    for k, row in enumerate(side):
        side_ref[k] = row
    base = lambda s: jnp.concatenate([part_ref[s], part_ref[s + 1]], 1)
    read_rows(side, [first + k for k in range(STEPS)], cell_ref, values_ref, base, width)


def by_product(table_ref, slot_ref, weight_ref, columns, channels):
    count = table_ref.shape[0] // (2 * channels)
    total = 0.0
    for corner in range(CORNERS):
        slots = slot_ref[corner : corner + 1, columns]
        found = jnp.dot(table_ref[...], one_hot(slots % PLACES, PLACES), preferred_element_type=F32)
        marks = jnp.broadcast_to(slots // PLACES, (channels, slots.shape[1]))
        out = None
        for k in range(count):
            both = found[2 * channels * k : 2 * channels * (k + 1)]
            both = both[:channels] + both[channels:]
            out = both if out is None else jnp.where(marks == k, both, out)
        total = total + weight_ref[corner : corner + 1, columns] * out
    return total


def by_lanes(ret_ref, slot_ref, weight_ref, columns):
    blocks, channels, _ = ret_ref.shape
    group = 8
    totals = [0.0] * (channels // group)
    for corner in range(CORNERS):
        slots = slot_ref[corner : corner + 1, columns]
        weight = weight_ref[corner : corner + 1, columns]
        lanes = jnp.broadcast_to(slots % LANES, (group, LANES))
        block = jnp.broadcast_to(slots // LANES, (group, LANES))
        marks = [block == k for k in range(blocks)]
        for c in range(channels // group):
            out = None
            for k in range(blocks):
                found = jnp.take_along_axis(ret_ref[k, group * c : group * (c + 1), :], lanes, axis=1)
                out = found if out is None else jnp.where(marks[k], found, out)
            totals[c] = totals[c] + weight * out
    return jnp.concatenate(totals, 0)


def sum_from_slots(
    ret_ref, slot_ref, weight_ref, inner_ref, near_ref, far_ref, result_ref, field_ref, table_ref, *, plan
):
    blocks, channels, _ = ret_ref.shape
    some, _, width = field_ref.shape
    inner = inner_ref.shape[0]
    far, _ = edge_starts(inner + 2 * STEPS)
    for k in range(some):
        y = pl.program_id(0) * some + k
        at = jnp.clip(jnp.where(y < STEPS, y, y - STEPS - inner), 0, STEPS - 1)
        is_inner = (y >= STEPS) & (y < STEPS + inner)
        edge = jnp.where((y < STEPS) == (far == 0), far_ref[at], near_ref[at])
        row = jnp.where(is_inner, inner_ref[jnp.clip(y - STEPS, 0, inner - 1)], edge)
        field_ref[k] = row[:, :width]
    group = PLACES // LANES

    @pl.when(pl.program_id(0) == 0)
    def _():
        for k in range(blocks // group):
            both = halves(jnp.concatenate([ret_ref[group * k + part] for part in range(group)], 1))
            table_ref[2 * channels * k : 2 * channels * (k + 1), :] = jnp.concatenate(both, 0)

    at = 0
    for product, single in plan:
        columns = slice(at, at + product * LANES)
        result_ref[:, columns] = by_product(table_ref, slot_ref, weight_ref, columns, channels)
        for k in range(product, product + single):
            columns = slice(at + k * LANES, at + (k + 1) * LANES)
            result_ref[:, columns] = by_lanes(ret_ref, slot_ref, weight_ref, columns)
        at += (product + single) * LANES


def plan_of(blocks):
    turns = max(t for t in (3, 2, 1) if blocks % t == 0)
    size = blocks // turns
    return [(size - size // 3, size // 3)] * turns


def chunk_of(fine, most):
    return max(c for c in range(LANES, most + 1, LANES) if fine % c == 0)


def call(kernel, ins, out, scratch=(), grid=(), in_specs=VMEM, out_specs=VMEM, memory=16, cost=None):
    single = isinstance(in_specs, pl.BlockSpec)
    return pl.pallas_call(
        kernel,
        grid=grid,
        out_shape=out,
        in_specs=[in_specs] * len(ins) if single else in_specs,
        out_specs=[out_specs] * len(out) if single and isinstance(out, list) else out_specs,
        scratch_shapes=list(scratch),
        cost_estimate=cost,
        compiler_params=pltpu.CompilerParams(vmem_limit_bytes=memory << 20),
    )(*ins)


def body(increment, send_slots, tent_weight, coarse_cell, diffusivity):
    channels, fine = increment.shape
    slot_count = coarse_cell.shape[0]
    rows, width = diffusivity.shape
    tiles = lax.axis_size("tile")
    share = slot_count // tiles
    blocks = slot_count // LANES
    wide = 2 * LANES
    on_chip = [(i, i ^ 1) for i in range(tiles)]
    off_chip = [(i, (i + 2 * (i % 2) - 1) % tiles) for i in range(tiles)]
    shape = jax.ShapeDtypeStruct
    slots = send_slots.T
    cells = coarse_cell.reshape(blocks, LANES)
    chunk = chunk_of(fine, 2304)
    grid = (fine // chunk,)
    part = lambda n: pl.BlockSpec((n, chunk), lambda i: (0, i))
    whole = pl.BlockSpec((blocks, channels, LANES), lambda i: (0, 0, 0))

    sent = call(
        sum_to_slots,
        (increment, slots, tent_weight),
        shape((blocks, channels, LANES), F32),
        grid=grid,
        in_specs=[part(channels), part(CORNERS), part(CORNERS)],
        out_specs=whole,
        memory=56,
    )
    received = exchange(sent, tiles, share)
    edge = shape((EDGE, channels, LANES), F32)
    slot_blocks = shape((blocks, channels, LANES), F32)
    edges, far, near = call(
        functools.partial(sum_edges, width=width),
        (received, cells, diffusivity),
        [shape((2 * STEPS, channels, wide), F32), edge, edge],
    )
    far = lax.ppermute(far, "tile", off_chip)
    near = lax.ppermute(near, "tile", on_chip)
    own = pltpu.VMEM((rows, channels, wide), F32)
    ends = shape((STEPS, channels, wide), F32)
    side = pltpu.VMEM((2 * STEPS + 1, channels, wide), F32)
    side_scratch = [side, side, pltpu.VMEM((2 * STEPS, wide), F32)]
    start, kept, inner, near_last, found = call(
        functools.partial(diffuse_most, width=width),
        (received, edges, near, diffusivity, cells),
        [
            shape((rows, channels, wide), F32),
            shape((STEPS - 1, 4, channels, wide), F32),
            shape((rows - 2 * STEPS, channels, wide), F32),
            ends,
            slot_blocks,
        ],
        [own, own, pltpu.VMEM((rows, wide), F32)] + side_scratch,
        cost=pl.CostEstimate(flops=4 * slot_count * wide * wide, bytes_accessed=8 << 20, transcendentals=0),
    )
    far_last, values = call(
        functools.partial(diffuse_last, width=width),
        (kept, found, start, far, diffusivity, cells),
        [ends, slot_blocks],
        side_scratch,
    )
    returned = exchange(values, tiles, share)
    turns = fine // chunk
    some = rows // turns if rows % turns == 0 else rows
    all_of = lambda count: pl.BlockSpec((count, channels, wide), lambda i: (0, 0, 0))
    result, field = call(
        functools.partial(sum_from_slots, plan=plan_of(chunk // LANES)),
        (returned, slots, tent_weight, inner, near_last, far_last),
        [shape((channels, fine), F32), shape((rows, channels, width), F32)],
        [pltpu.VMEM((2 * channels * slot_count // PLACES, PLACES), BF16)],
        grid=grid,
        in_specs=[whole, part(CORNERS), part(CORNERS), all_of(rows - 2 * STEPS), all_of(STEPS), all_of(STEPS)],
        out_specs=[part(channels), pl.BlockSpec((some, channels, width), lambda i: (i, 0, 0))],
        memory=32,
    )
    return (result, field.transpose(1, 0, 2))


def exchange(blocks, tiles, share):
    count, channels, lanes = blocks.shape
    if share == lanes:
        return lax.all_to_all(blocks, "tile", split_axis=0, concat_axis=0, tiled=True)
    flat = blocks.transpose(1, 0, 2).reshape(channels, count * lanes)
    flat = lax.all_to_all(flat, "tile", split_axis=1, concat_axis=1, tiled=True)
    return flat.reshape(channels, count, lanes).transpose(1, 0, 2)


def solution(mesh):
    in_specs = (
        P(None, ("group", "tile")),
        P("tile", None),
        P(None, "tile"),
        P("tile"),
        P("tile", None),
    )
    out_specs = (P(None, ("group", "tile")), P(None, ("group", "tile"), None))
    return jax.shard_map(body, mesh=mesh, in_specs=in_specs, out_specs=out_specs, check_vma=False)
```

```python
import functools

import jax
import jax.numpy as jnp
from jax import lax
from jax.experimental import pallas as pl
from jax.experimental.pallas import tpu as pltpu
from jax.sharding import PartitionSpec as P

STEPS = 5
CORNERS = 4
LANES = 128
PLACES = 256
EDGE = STEPS + (STEPS + 1) // 2
BF16 = jnp.bfloat16
F32 = jnp.float32
VMEM = pl.BlockSpec(memory_space=pltpu.VMEM)


def halves(values):
    high = values.astype(BF16)
    return high, (values - high.astype(F32)).astype(BF16)


def one_hot(places, length):
    rows = lax.broadcasted_iota(jnp.int32, (length, places.shape[1]), 0)
    return jnp.where(rows == places, 1.0, 0.0).astype(BF16)


def masked(values, marks, wanted):
    marks = jnp.broadcast_to(marks, values.shape)
    zero = jnp.zeros((), values.dtype)
    return jnp.concatenate([jnp.where(marks == k, values, zero) for k in wanted], 0)


def dot_last(left, right):
    return lax.dot_general(left, right, (((1,), (1,)), ((), ())), preferred_element_type=F32)


def sum_to_slots(inc_ref, slot_ref, weight_ref, sent_ref):
    channels = inc_ref.shape[0]
    count = sent_ref.shape[0] * LANES // PLACES
    inc = inc_ref[...]
    left, right = [], []
    for corner in range(CORNERS):
        slots = slot_ref[corner : corner + 1, :]
        parts = jnp.concatenate(halves(weight_ref[corner : corner + 1, :] * inc), 0)
        left.append(masked(parts, slots // PLACES, range(count)))
        right.append(one_hot(slots % PLACES, PLACES))
    sums = dot_last(jnp.concatenate(left, 1), jnp.concatenate(right, 1))

    @pl.when(pl.program_id(0) == 0)
    def _():
        sent_ref[...] = jnp.zeros_like(sent_ref)

    for k in range(count):
        both = sums[2 * channels * k : 2 * channels * (k + 1)]
        both = both[:channels] + both[channels:]
        for part in range(PLACES // LANES):
            sent_ref[k * (PLACES // LANES) + part] += both[:, LANES * part : LANES * (part + 1)]


def wide_column(width):
    lanes = lax.broadcasted_iota(jnp.int32, (2 * LANES, 1), 0)
    extra = (2 * LANES - width) // 2
    return jnp.where(lanes < width, lanes, jnp.where(lanes < width + extra, lanes - width, lanes - 2 * LANES + width))


def place_edge(edge_ref, rows, coefs, width):
    half = width - LANES
    for k, row in enumerate(rows):
        edge_ref[k] = row[:, :LANES]
    ends = [row[:, LANES:width] for row in rows]
    for k in range(0, STEPS - 1, 2):
        edge_ref[STEPS + k // 2] = jnp.concatenate([ends[k], ends[k + 1]], 1)
    edge_ref[EDGE - 1] = jnp.concatenate([ends[-1], jnp.zeros_like(ends[-1])], 1)
    for k, coef in enumerate(coefs):
        for part in range(3):
            edge_ref[EDGE - 1, 3 * k + part : 3 * k + part + 1, half:] = coef[:, half * part : half * (part + 1)]


def read_edge(edge_ref, k, width):
    half = width - LANES
    start = edge_ref[k]
    end = edge_ref[STEPS + k // 2, :, half * (k % 2) : half * (k % 2) + half]
    return widened([start, end], start, end, width)


def read_coef(edge_ref, k, width):
    half = width - LANES
    parts = [edge_ref[EDGE - 1, 3 * k + part : 3 * k + part + 1, half:] for part in range(3)]
    return widened(parts, parts[0], parts[2], width)


def widened(parts, start, end, width):
    extra = (2 * LANES - width) // 2
    return jnp.concatenate(parts + [start[:, :extra], end[:, end.shape[1] - extra :]], 1)


def cell_sums(rec_ref, cell_ref, ys, width):
    senders, channels, _ = rec_ref.shape
    cells = jnp.concatenate([cell_ref[s : s + 1, :] for s in range(senders)], 1)
    values = jnp.concatenate([rec_ref[s] for s in range(senders)], 1)
    y = cells // width
    right = jnp.where(wide_column(width) == cells - y * width, 1.0, 0.0).astype(BF16)
    sums = dot_last(masked(jnp.concatenate(halves(values), 0), y, ys), right)
    full = []
    for k in range(len(ys)):
        both = sums[2 * channels * k : 2 * channels * (k + 1)]
        full.append(both[:channels] + both[channels:])
    return full


def edge_starts(rows):
    even = lax.axis_index("tile") % 2 == 0
    return jnp.where(even, 0, rows - STEPS), jnp.where(even, rows - STEPS, 0)


def sum_edges(rec_ref, cell_ref, coef_ref, edges_ref, far_ref, near_ref, *, width):
    starts = edge_starts(coef_ref.shape[0])
    ys = [start + k for start in starts for k in range(STEPS)]
    full = cell_sums(rec_ref, cell_ref, ys, width)
    for k, row in enumerate(full):
        edges_ref[k] = row
    for edge_ref, at in ((far_ref, 0), (near_ref, STEPS)):
        coefs = [coef_ref[pl.ds(y, 1), :] for y in ys[at : at + STEPS]]
        place_edge(edge_ref, full[at : at + STEPS], coefs, width)


def stepped(above, here, below, coef):
    wide = here.shape[-1]
    spread = below + above + pltpu.roll(here, 1, 1) + pltpu.roll(here, wide - 1, 1)
    return here + coef * (spread - 4.0 * here)


def kept_rows(turn, total):
    first, last = STEPS + turn, total - STEPS - turn
    return [first, first + 1, last - 2, last - 1]


def read_rows(final_rows, ys, cell_ref, values_ref, base, width):
    senders, channels, _ = values_ref.shape
    left = jnp.concatenate([jnp.concatenate(halves(row), 0) for row in final_rows], 0)
    for s in range(0, senders, 2):
        cells = jnp.concatenate([cell_ref[s : s + 1, :], cell_ref[s + 1 : s + 2, :]], 1)
        y = cells // width
        found = jnp.dot(left, one_hot(cells - y * width, left.shape[1]), preferred_element_type=F32)
        out = base(s)
        marks = jnp.broadcast_to(y, out.shape)
        for k, row in enumerate(ys):
            both = found[2 * channels * k : 2 * channels * (k + 1)]
            out = jnp.where(marks == row, both[:channels] + both[channels:], out)
        values_ref[s] = out[:, :LANES]
        values_ref[s + 1] = out[:, LANES:]


def inner_rows(start_ref, own_ref, kept_ref, one_ref, two_ref, coef_ref, width):
    rows = start_ref.shape[0]
    own = own_ref[...]
    coef_ref[...] = widened([own], own, own, width)
    held, other, last = start_ref, one_ref, two_ref
    for turn in range(1, STEPS + 1):
        for y in range(turn, rows - turn):
            other[y] = stepped(held[y - 1], held[y], held[y + 1], coef_ref[y : y + 1, :])
        if turn < STEPS:
            for place, y in enumerate(kept_rows(turn, rows + 2 * STEPS)):
                kept_ref[turn - 1, place] = other[y - STEPS]
        held, other, last = other, last, other
    return [held[y] for y in range(STEPS, rows - STEPS)]


def side_rows(start_ref, edge_ref, own_ref, kept_ref, one_ref, two_ref, coef_ref, width, first):
    rows = own_ref.shape[0]
    head = first == 0
    flip = lambda ahead, behind: jnp.where(head, ahead, behind)
    for k in range(STEPS):
        place = flip(k, STEPS - 1 - k)
        one_ref[place] = read_edge(edge_ref, k, width)
        coef_ref[pl.ds(place, 1), :] = read_coef(edge_ref, k, width)
        own = own_ref[pl.ds(flip(k, rows - 1 - k), 1), :]
        coef_ref[STEPS + k : STEPS + k + 1, :] = widened([own], own, own, width)
    held, other = one_ref, two_ref
    for turn in range(1, STEPS + 1):

        def row(u):
            if turn == 1 and u >= STEPS:
                return start_ref[flip(u - STEPS, rows - 1 - u + STEPS)]
            if u >= STEPS + turn - 1:
                k = u - STEPS - turn + 1
                return kept_ref[turn - 2, flip(k, 3 - k)]
            return held[u]

        for u in range(turn, turn + STEPS):
            other[u] = stepped(row(u - 1), row(u), row(u + 1), coef_ref[u : u + 1, :])
        held, other = other, held
    return [held[flip(STEPS + k, 2 * STEPS - 1 - k)] for k in range(STEPS)]


def diffuse_most(
    rec_ref, edges_ref, edge_ref, own_ref, cell_ref, start_ref, kept_ref, inner_ref, side_ref, values_ref,
    one_ref, two_ref, coef_ref, side_one_ref, side_two_ref, side_coef_ref, *, width
):
    rows, channels, _ = start_ref.shape
    far, first = edge_starts(rows)
    for k in range(STEPS):
        start_ref[far + k] = edges_ref[k]
        start_ref[first + k] = edges_ref[STEPS + k]
    within = range(STEPS, rows - STEPS)
    for y, row in zip(within, cell_sums(rec_ref, cell_ref, within, width)):
        start_ref[y] = row
    inner = inner_rows(start_ref, own_ref, kept_ref, one_ref, two_ref, coef_ref, width)
    side = side_rows(
        start_ref, edge_ref, own_ref, kept_ref, side_one_ref, side_two_ref, side_coef_ref, width, first
    )
    for k, row in enumerate(inner):
        inner_ref[k] = row
    for k, row in enumerate(side):
        side_ref[k] = row
    ys = list(range(STEPS, rows - STEPS)) + [first + k for k in range(STEPS)]
    nothing = lambda s: jnp.zeros((channels, 2 * LANES), F32)
    read_rows(inner + side, ys, cell_ref, values_ref, nothing, width)


def diffuse_last(
    kept_ref, part_ref, start_ref, edge_ref, own_ref, cell_ref, side_ref, values_ref, one_ref, two_ref, coef_ref, *, width
):
    first, _ = edge_starts(own_ref.shape[0])
    side = side_rows(start_ref, edge_ref, own_ref, kept_ref, one_ref, two_ref, coef_ref, width, first)
    for k, row in enumerate(side):
        side_ref[k] = row
    base = lambda s: jnp.concatenate([part_ref[s], part_ref[s + 1]], 1)
    read_rows(side, [first + k for k in range(STEPS)], cell_ref, values_ref, base, width)


def by_product(table_ref, slot_ref, weight_ref, columns, channels):
    count = table_ref.shape[0] // (2 * channels)
    total = 0.0
    for corner in range(CORNERS):
        slots = slot_ref[corner : corner + 1, columns]
        found = jnp.dot(table_ref[...], one_hot(slots % PLACES, PLACES), preferred_element_type=F32)
        marks = jnp.broadcast_to(slots // PLACES, (channels, slots.shape[1]))
        out = None
        for k in range(count):
            both = found[2 * channels * k : 2 * channels * (k + 1)]
            both = both[:channels] + both[channels:]
            out = both if out is None else jnp.where(marks == k, both, out)
        total = total + weight_ref[corner : corner + 1, columns] * out
    return total


def by_lanes(ret_ref, slot_ref, weight_ref, columns):
    blocks, channels, _ = ret_ref.shape
    group = 8
    totals = [0.0] * (channels // group)
    for corner in range(CORNERS):
        slots = slot_ref[corner : corner + 1, columns]
        weight = weight_ref[corner : corner + 1, columns]
        lanes = jnp.broadcast_to(slots % LANES, (group, LANES))
        block = jnp.broadcast_to(slots // LANES, (group, LANES))
        marks = [block == k for k in range(blocks)]
        for c in range(channels // group):
            out = None
            for k in range(blocks):
                found = jnp.take_along_axis(ret_ref[k, group * c : group * (c + 1), :], lanes, axis=1)
                out = found if out is None else jnp.where(marks[k], found, out)
            totals[c] = totals[c] + weight * out
    return jnp.concatenate(totals, 0)


def sum_from_slots(
    ret_ref, slot_ref, weight_ref, inner_ref, near_ref, far_ref, result_ref, field_ref, table_ref, *, plan
):
    blocks, channels, _ = ret_ref.shape
    some, _, width = field_ref.shape
    inner = inner_ref.shape[0]
    far, _ = edge_starts(inner + 2 * STEPS)
    for k in range(some):
        y = pl.program_id(0) * some + k
        at = jnp.clip(jnp.where(y < STEPS, y, y - STEPS - inner), 0, STEPS - 1)
        is_inner = (y >= STEPS) & (y < STEPS + inner)
        edge = jnp.where((y < STEPS) == (far == 0), far_ref[at], near_ref[at])
        row = jnp.where(is_inner, inner_ref[jnp.clip(y - STEPS, 0, inner - 1)], edge)
        field_ref[k] = row[:, :width]
    group = PLACES // LANES

    @pl.when(pl.program_id(0) == 0)
    def _():
        for k in range(blocks // group):
            both = halves(jnp.concatenate([ret_ref[group * k + part] for part in range(group)], 1))
            table_ref[2 * channels * k : 2 * channels * (k + 1), :] = jnp.concatenate(both, 0)

    at = 0
    for product, single in plan:
        columns = slice(at, at + product * LANES)
        result_ref[:, columns] = by_product(table_ref, slot_ref, weight_ref, columns, channels)
        for k in range(product, product + single):
            columns = slice(at + k * LANES, at + (k + 1) * LANES)
            result_ref[:, columns] = by_lanes(ret_ref, slot_ref, weight_ref, columns)
        at += (product + single) * LANES


def plan_of(blocks):
    return [(blocks - blocks // 3, blocks // 3)]


def chunk_of(fine, most):
    return max(c for c in range(LANES, most + 1, LANES) if fine % c == 0)


def call(kernel, ins, out, scratch=(), grid=(), in_specs=VMEM, out_specs=VMEM, memory=16, cost=None):
    single = isinstance(in_specs, pl.BlockSpec)
    return pl.pallas_call(
        kernel,
        grid=grid,
        out_shape=out,
        in_specs=[in_specs] * len(ins) if single else in_specs,
        out_specs=[out_specs] * len(out) if single and isinstance(out, list) else out_specs,
        scratch_shapes=list(scratch),
        cost_estimate=cost,
        compiler_params=pltpu.CompilerParams(vmem_limit_bytes=memory << 20),
    )(*ins)


def body(increment, send_slots, tent_weight, coarse_cell, diffusivity):
    channels, fine = increment.shape
    slot_count = coarse_cell.shape[0]
    rows, width = diffusivity.shape
    tiles = lax.axis_size("tile")
    share = slot_count // tiles
    blocks = slot_count // LANES
    wide = 2 * LANES
    on_chip = [(i, i ^ 1) for i in range(tiles)]
    off_chip = [(i, (i + 2 * (i % 2) - 1) % tiles) for i in range(tiles)]
    shape = jax.ShapeDtypeStruct
    slots = send_slots.T
    cells = coarse_cell.reshape(blocks, LANES)
    chunk = chunk_of(fine, 3456)
    part = lambda n: pl.BlockSpec((n, chunk), lambda i: (0, i))
    full = lambda n: pl.BlockSpec((n, fine), lambda i: (0, 0))
    whole = pl.BlockSpec((blocks, channels, LANES), lambda i: (0, 0, 0))

    sent = call(
        sum_to_slots,
        (increment, slots, tent_weight),
        shape((blocks, channels, LANES), F32),
        grid=(1,),
        in_specs=[full(channels), full(CORNERS), full(CORNERS)],
        out_specs=whole,
        memory=56,
    )
    received = exchange(sent, tiles, share)
    edge = shape((EDGE, channels, LANES), F32)
    slot_blocks = shape((blocks, channels, LANES), F32)
    edges, far, near = call(
        functools.partial(sum_edges, width=width),
        (received, cells, diffusivity),
        [shape((2 * STEPS, channels, wide), F32), edge, edge],
    )
    far = lax.ppermute(far, "tile", off_chip)
    near = lax.ppermute(near, "tile", on_chip)
    own = pltpu.VMEM((rows, channels, wide), F32)
    ends = shape((STEPS, channels, wide), F32)
    side = pltpu.VMEM((2 * STEPS + 1, channels, wide), F32)
    side_scratch = [side, side, pltpu.VMEM((2 * STEPS, wide), F32)]
    start, kept, inner, near_last, found = call(
        functools.partial(diffuse_most, width=width),
        (received, edges, near, diffusivity, cells),
        [
            shape((rows, channels, wide), F32),
            shape((STEPS - 1, 4, channels, wide), F32),
            shape((rows - 2 * STEPS, channels, wide), F32),
            ends,
            slot_blocks,
        ],
        [own, own, pltpu.VMEM((rows, wide), F32)] + side_scratch,
        cost=pl.CostEstimate(flops=4 * slot_count * wide * wide, bytes_accessed=8 << 20, transcendentals=0),
    )
    far_last, values = call(
        functools.partial(diffuse_last, width=width),
        (kept, found, start, far, diffusivity, cells),
        [ends, slot_blocks],
        side_scratch,
    )
    returned = exchange(values, tiles, share)
    turns = fine // chunk
    some = rows // turns if rows % turns == 0 else rows
    all_of = lambda count: pl.BlockSpec((count, channels, wide), lambda i: (0, 0, 0))
    result, field = call(
        functools.partial(sum_from_slots, plan=plan_of(chunk // LANES)),
        (returned, slots, tent_weight, inner, near_last, far_last),
        [shape((channels, fine), F32), shape((rows, channels, width), F32)],
        [pltpu.VMEM((2 * channels * slot_count // PLACES, PLACES), BF16)],
        grid=(turns,),
        in_specs=[whole, part(CORNERS), part(CORNERS), all_of(rows - 2 * STEPS), all_of(STEPS), all_of(STEPS)],
        out_specs=[part(channels), pl.BlockSpec((some, channels, width), lambda i: (i, 0, 0))],
        memory=32,
    )
    return (result, field.transpose(1, 0, 2))


def exchange(blocks, tiles, share):
    count, channels, lanes = blocks.shape
    if share == lanes:
        return lax.all_to_all(blocks, "tile", split_axis=0, concat_axis=0, tiled=True)
    flat = blocks.transpose(1, 0, 2).reshape(channels, count * lanes)
    flat = lax.all_to_all(flat, "tile", split_axis=1, concat_axis=1, tiled=True)
    return flat.reshape(channels, count, lanes).transpose(1, 0, 2)


def solution(mesh):
    in_specs = (
        P(None, ("group", "tile")),
        P("tile", None),
        P(None, "tile"),
        P("tile"),
        P("tile", None),
    )
    out_specs = (P(None, ("group", "tile")), P(None, ("group", "tile"), None))
    return jax.shard_map(body, mesh=mesh, in_specs=in_specs, out_specs=out_specs, check_vma=False)
```

```python
import functools

import jax
import jax.numpy as jnp
from jax import lax
from jax.experimental import pallas as pl
from jax.experimental.pallas import tpu as pltpu
from jax.sharding import PartitionSpec as P

STEPS = 5
CORNERS = 4
LANES = 128
PLACES = 256
EDGE = STEPS + (STEPS + 1) // 2
BF16 = jnp.bfloat16
F32 = jnp.float32
VMEM = pl.BlockSpec(memory_space=pltpu.VMEM)


def halves(values):
    high = values.astype(BF16)
    return high, (values - high.astype(F32)).astype(BF16)


def one_hot(places, length):
    rows = lax.broadcasted_iota(jnp.int32, (length, places.shape[1]), 0)
    return jnp.where(rows == places, 1.0, 0.0).astype(BF16)


def masked(values, marks, wanted):
    marks = jnp.broadcast_to(marks, values.shape)
    zero = jnp.zeros((), values.dtype)
    return jnp.concatenate([jnp.where(marks == k, values, zero) for k in wanted], 0)


def dot_last(left, right):
    return lax.dot_general(left, right, (((1,), (1,)), ((), ())), preferred_element_type=F32)


def sum_to_slots(inc_ref, slot_ref, weight_ref, sent_ref):
    channels = inc_ref.shape[0]
    count = sent_ref.shape[0] * LANES // PLACES
    inc = inc_ref[...]
    left, right = [], []
    for corner in range(CORNERS):
        slots = slot_ref[corner : corner + 1, :]
        parts = jnp.concatenate(halves(weight_ref[corner : corner + 1, :] * inc), 0)
        left.append(masked(parts, slots // PLACES, range(count)))
        right.append(one_hot(slots % PLACES, PLACES))
    sums = dot_last(jnp.concatenate(left, 1), jnp.concatenate(right, 1))

    @pl.when(pl.program_id(0) == 0)
    def _():
        sent_ref[...] = jnp.zeros_like(sent_ref)

    for k in range(count):
        both = sums[2 * channels * k : 2 * channels * (k + 1)]
        both = both[:channels] + both[channels:]
        for part in range(PLACES // LANES):
            sent_ref[k * (PLACES // LANES) + part] += both[:, LANES * part : LANES * (part + 1)]


def wide_column(width):
    lanes = lax.broadcasted_iota(jnp.int32, (2 * LANES, 1), 0)
    extra = (2 * LANES - width) // 2
    return jnp.where(lanes < width, lanes, jnp.where(lanes < width + extra, lanes - width, lanes - 2 * LANES + width))


def place_edge(edge_ref, rows, coefs, width):
    half = width - LANES
    for k, row in enumerate(rows):
        edge_ref[k] = row[:, :LANES]
    ends = [row[:, LANES:width] for row in rows]
    for k in range(0, STEPS - 1, 2):
        edge_ref[STEPS + k // 2] = jnp.concatenate([ends[k], ends[k + 1]], 1)
    edge_ref[EDGE - 1] = jnp.concatenate([ends[-1], jnp.zeros_like(ends[-1])], 1)
    for k, coef in enumerate(coefs):
        for part in range(3):
            edge_ref[EDGE - 1, 3 * k + part : 3 * k + part + 1, half:] = coef[:, half * part : half * (part + 1)]


def read_edge(edge_ref, k, width):
    half = width - LANES
    start = edge_ref[k]
    end = edge_ref[STEPS + k // 2, :, half * (k % 2) : half * (k % 2) + half]
    return widened([start, end], start, end, width)


def read_coef(edge_ref, k, width):
    half = width - LANES
    parts = [edge_ref[EDGE - 1, 3 * k + part : 3 * k + part + 1, half:] for part in range(3)]
    return widened(parts, parts[0], parts[2], width)


def widened(parts, start, end, width):
    extra = (2 * LANES - width) // 2
    return jnp.concatenate(parts + [start[:, :extra], end[:, end.shape[1] - extra :]], 1)


def cell_sums(rec_ref, cell_ref, ys, width):
    senders, channels, _ = rec_ref.shape
    cells = jnp.concatenate([cell_ref[s : s + 1, :] for s in range(senders)], 1)
    values = jnp.concatenate([rec_ref[s] for s in range(senders)], 1)
    y = cells // width
    right = jnp.where(wide_column(width) == cells - y * width, 1.0, 0.0).astype(BF16)
    sums = dot_last(masked(jnp.concatenate(halves(values), 0), y, ys), right)
    full = []
    for k in range(len(ys)):
        both = sums[2 * channels * k : 2 * channels * (k + 1)]
        full.append(both[:channels] + both[channels:])
    return full


def edge_starts(rows):
    even = lax.axis_index("tile") % 2 == 0
    return jnp.where(even, 0, rows - STEPS), jnp.where(even, rows - STEPS, 0)


def sum_edges(rec_ref, cell_ref, coef_ref, edges_ref, far_ref, near_ref, *, width):
    starts = edge_starts(coef_ref.shape[0])
    ys = [start + k for start in starts for k in range(STEPS)]
    full = cell_sums(rec_ref, cell_ref, ys, width)
    for k, row in enumerate(full):
        edges_ref[k] = row
    for edge_ref, at in ((far_ref, 0), (near_ref, STEPS)):
        coefs = [coef_ref[pl.ds(y, 1), :] for y in ys[at : at + STEPS]]
        place_edge(edge_ref, full[at : at + STEPS], coefs, width)


def stepped(above, here, below, coef):
    wide = here.shape[-1]
    spread = below + above + pltpu.roll(here, 1, 1) + pltpu.roll(here, wide - 1, 1)
    return here + coef * (spread - 4.0 * here)


def kept_rows(turn, total):
    first, last = STEPS + turn, total - STEPS - turn
    return [first, first + 1, last - 2, last - 1]


def read_by_lanes(rows_ref, ys, cell_ref, values_ref, part_ref, senders, width):
    channels = values_ref.shape[1]
    group = 8
    for s in senders:
        cells = jnp.broadcast_to(cell_ref[s : s + 1, :], (group, LANES))
        y = cells // width
        x = cells - y * width
        lanes = x % LANES
        marks = [[(y == row) & (x // LANES == part) for part in range(2)] for row in ys]
        for c in range(0, channels, group):
            out = part_ref[s, c : c + group, :]
            for k in range(len(ys)):
                for part in range(2):
                    side = rows_ref[k, c : c + group, LANES * part : LANES * (part + 1)]
                    out = jnp.where(marks[k][part], jnp.take_along_axis(side, lanes, axis=1), out)
            values_ref[s, c : c + group, :] = out


def read_rows(final_rows, ys, cell_ref, values_ref, base, width, senders=None):
    senders = values_ref.shape[0] if senders is None else senders
    channels = values_ref.shape[1]
    left = jnp.concatenate([jnp.concatenate(halves(row), 0) for row in final_rows], 0)
    for s in range(0, senders, 2):
        cells = jnp.concatenate([cell_ref[s : s + 1, :], cell_ref[s + 1 : s + 2, :]], 1)
        y = cells // width
        found = jnp.dot(left, one_hot(cells - y * width, left.shape[1]), preferred_element_type=F32)
        out = base(s)
        marks = jnp.broadcast_to(y, out.shape)
        for k, row in enumerate(ys):
            both = found[2 * channels * k : 2 * channels * (k + 1)]
            out = jnp.where(marks == row, both[:channels] + both[channels:], out)
        values_ref[s] = out[:, :LANES]
        values_ref[s + 1] = out[:, LANES:]


def inner_rows(start_ref, own_ref, kept_ref, one_ref, two_ref, coef_ref, width):
    rows = start_ref.shape[0]
    own = own_ref[...]
    coef_ref[...] = widened([own], own, own, width)
    held, other, last = start_ref, one_ref, two_ref
    for turn in range(1, STEPS + 1):
        for y in range(turn, rows - turn):
            other[y] = stepped(held[y - 1], held[y], held[y + 1], coef_ref[y : y + 1, :])
        if turn < STEPS:
            for place, y in enumerate(kept_rows(turn, rows + 2 * STEPS)):
                kept_ref[turn - 1, place] = other[y - STEPS]
        held, other, last = other, last, other
    return [held[y] for y in range(STEPS, rows - STEPS)]


def side_rows(start_ref, edge_ref, own_ref, kept_ref, one_ref, two_ref, coef_ref, width, first):
    rows = own_ref.shape[0]
    head = first == 0
    flip = lambda ahead, behind: jnp.where(head, ahead, behind)
    for k in range(STEPS):
        place = flip(k, STEPS - 1 - k)
        one_ref[place] = read_edge(edge_ref, k, width)
        coef_ref[pl.ds(place, 1), :] = read_coef(edge_ref, k, width)
        own = own_ref[pl.ds(flip(k, rows - 1 - k), 1), :]
        coef_ref[STEPS + k : STEPS + k + 1, :] = widened([own], own, own, width)
    held, other = one_ref, two_ref
    for turn in range(1, STEPS + 1):

        def row(u):
            if turn == 1 and u >= STEPS:
                return start_ref[flip(u - STEPS, rows - 1 - u + STEPS)]
            if u >= STEPS + turn - 1:
                k = u - STEPS - turn + 1
                return kept_ref[turn - 2, flip(k, 3 - k)]
            return held[u]

        for u in range(turn, turn + STEPS):
            other[u] = stepped(row(u - 1), row(u), row(u + 1), coef_ref[u : u + 1, :])
        held, other = other, held
    return [held[flip(STEPS + k, 2 * STEPS - 1 - k)] for k in range(STEPS)]


def diffuse_most(
    rec_ref, edges_ref, edge_ref, own_ref, cell_ref, start_ref, kept_ref, inner_ref, side_ref, values_ref,
    one_ref, two_ref, coef_ref, side_one_ref, side_two_ref, side_coef_ref, *, width
):
    rows, channels, _ = start_ref.shape
    far, first = edge_starts(rows)
    for k in range(STEPS):
        start_ref[far + k] = edges_ref[k]
        start_ref[first + k] = edges_ref[STEPS + k]
    within = range(STEPS, rows - STEPS)
    for y, row in zip(within, cell_sums(rec_ref, cell_ref, within, width)):
        start_ref[y] = row
    inner = inner_rows(start_ref, own_ref, kept_ref, one_ref, two_ref, coef_ref, width)
    side = side_rows(
        start_ref, edge_ref, own_ref, kept_ref, side_one_ref, side_two_ref, side_coef_ref, width, first
    )
    for k, row in enumerate(inner):
        inner_ref[k] = row
    for k, row in enumerate(side):
        side_ref[k] = row
    ys = list(range(STEPS, rows - STEPS)) + [first + k for k in range(STEPS)]
    nothing = lambda s: jnp.zeros((channels, 2 * LANES), F32)
    read_rows(inner + side, ys, cell_ref, values_ref, nothing, width)


def diffuse_last(
    kept_ref, part_ref, start_ref, edge_ref, own_ref, cell_ref, side_ref, values_ref, one_ref, two_ref, coef_ref, *, width
):
    first, _ = edge_starts(own_ref.shape[0])
    side = side_rows(start_ref, edge_ref, own_ref, kept_ref, one_ref, two_ref, coef_ref, width, first)
    for k, row in enumerate(side):
        side_ref[k] = row
    base = lambda s: jnp.concatenate([part_ref[s], part_ref[s + 1]], 1)
    ys = [first + k for k in range(STEPS)]
    senders = values_ref.shape[0]
    products = senders - 2 * (3 * senders // 16)
    read_rows(side, ys, cell_ref, values_ref, base, width, products)
    read_by_lanes(side_ref, ys, cell_ref, values_ref, part_ref, range(products, senders), width)


def by_product(table_ref, slot_ref, weight_ref, columns, channels):
    count = table_ref.shape[0] // (2 * channels)
    total = 0.0
    for corner in range(CORNERS):
        slots = slot_ref[corner : corner + 1, columns]
        found = jnp.dot(table_ref[...], one_hot(slots % PLACES, PLACES), preferred_element_type=F32)
        marks = jnp.broadcast_to(slots // PLACES, (channels, slots.shape[1]))
        out = None
        for k in range(count):
            both = found[2 * channels * k : 2 * channels * (k + 1)]
            both = both[:channels] + both[channels:]
            out = both if out is None else jnp.where(marks == k, both, out)
        total = total + weight_ref[corner : corner + 1, columns] * out
    return total


def by_lanes(ret_ref, slot_ref, weight_ref, columns):
    blocks, channels, _ = ret_ref.shape
    group = 8
    totals = [0.0] * (channels // group)
    for corner in range(CORNERS):
        slots = slot_ref[corner : corner + 1, columns]
        weight = weight_ref[corner : corner + 1, columns]
        lanes = jnp.broadcast_to(slots % LANES, (group, LANES))
        block = jnp.broadcast_to(slots // LANES, (group, LANES))
        marks = [block == k for k in range(blocks)]
        for c in range(channels // group):
            out = None
            for k in range(blocks):
                found = jnp.take_along_axis(ret_ref[k, group * c : group * (c + 1), :], lanes, axis=1)
                out = found if out is None else jnp.where(marks[k], found, out)
            totals[c] = totals[c] + weight * out
    return jnp.concatenate(totals, 0)


def sum_from_slots(
    ret_ref, slot_ref, weight_ref, inner_ref, near_ref, far_ref, result_ref, field_ref, table_ref, *, plan
):
    blocks, channels, _ = ret_ref.shape
    some, _, width = field_ref.shape
    inner = inner_ref.shape[0]
    far, _ = edge_starts(inner + 2 * STEPS)
    for k in range(some):
        y = pl.program_id(0) * some + k
        at = jnp.clip(jnp.where(y < STEPS, y, y - STEPS - inner), 0, STEPS - 1)
        is_inner = (y >= STEPS) & (y < STEPS + inner)
        edge = jnp.where((y < STEPS) == (far == 0), far_ref[at], near_ref[at])
        row = jnp.where(is_inner, inner_ref[jnp.clip(y - STEPS, 0, inner - 1)], edge)
        field_ref[k] = row[:, :width]
    group = PLACES // LANES

    @pl.when(pl.program_id(0) == 0)
    def _():
        for k in range(blocks // group):
            both = halves(jnp.concatenate([ret_ref[group * k + part] for part in range(group)], 1))
            table_ref[2 * channels * k : 2 * channels * (k + 1), :] = jnp.concatenate(both, 0)

    at = 0
    for product, single in plan:
        columns = slice(at, at + product * LANES)
        result_ref[:, columns] = by_product(table_ref, slot_ref, weight_ref, columns, channels)
        for k in range(product, product + single):
            columns = slice(at + k * LANES, at + (k + 1) * LANES)
            result_ref[:, columns] = by_lanes(ret_ref, slot_ref, weight_ref, columns)
        at += (product + single) * LANES


def plan_of(blocks):
    return [(blocks - blocks // 3, blocks // 3)]


def chunk_of(fine, most):
    return max(c for c in range(LANES, most + 1, LANES) if fine % c == 0)


def call(kernel, ins, out, scratch=(), grid=(), in_specs=VMEM, out_specs=VMEM, memory=16, cost=None):
    single = isinstance(in_specs, pl.BlockSpec)
    return pl.pallas_call(
        kernel,
        grid=grid,
        out_shape=out,
        in_specs=[in_specs] * len(ins) if single else in_specs,
        out_specs=[out_specs] * len(out) if single and isinstance(out, list) else out_specs,
        scratch_shapes=list(scratch),
        cost_estimate=cost,
        compiler_params=pltpu.CompilerParams(vmem_limit_bytes=memory << 20),
    )(*ins)


def body(increment, send_slots, tent_weight, coarse_cell, diffusivity):
    channels, fine = increment.shape
    slot_count = coarse_cell.shape[0]
    rows, width = diffusivity.shape
    tiles = lax.axis_size("tile")
    share = slot_count // tiles
    blocks = slot_count // LANES
    wide = 2 * LANES
    on_chip = [(i, i ^ 1) for i in range(tiles)]
    off_chip = [(i, (i + 2 * (i % 2) - 1) % tiles) for i in range(tiles)]
    shape = jax.ShapeDtypeStruct
    slots = send_slots.T
    cells = coarse_cell.reshape(blocks, LANES)
    chunk = chunk_of(fine, 3456)
    part = lambda n: pl.BlockSpec((n, chunk), lambda i: (0, i))
    full = lambda n: pl.BlockSpec((n, fine), lambda i: (0, 0))
    whole = pl.BlockSpec((blocks, channels, LANES), lambda i: (0, 0, 0))

    sent = call(
        sum_to_slots,
        (increment, slots, tent_weight),
        shape((blocks, channels, LANES), F32),
        grid=(1,),
        in_specs=[full(channels), full(CORNERS), full(CORNERS)],
        out_specs=whole,
        memory=56,
    )
    received = exchange(sent, tiles, share)
    edge = shape((EDGE, channels, LANES), F32)
    slot_blocks = shape((blocks, channels, LANES), F32)
    edges, far, near = call(
        functools.partial(sum_edges, width=width),
        (received, cells, diffusivity),
        [shape((2 * STEPS, channels, wide), F32), edge, edge],
    )
    far = lax.ppermute(far, "tile", off_chip)
    near = lax.ppermute(near, "tile", on_chip)
    own = pltpu.VMEM((rows, channels, wide), F32)
    ends = shape((STEPS, channels, wide), F32)
    side = pltpu.VMEM((2 * STEPS + 1, channels, wide), F32)
    side_scratch = [side, side, pltpu.VMEM((2 * STEPS, wide), F32)]
    start, kept, inner, near_last, found = call(
        functools.partial(diffuse_most, width=width),
        (received, edges, near, diffusivity, cells),
        [
            shape((rows, channels, wide), F32),
            shape((STEPS - 1, 4, channels, wide), F32),
            shape((rows - 2 * STEPS, channels, wide), F32),
            ends,
            slot_blocks,
        ],
        [own, own, pltpu.VMEM((rows, wide), F32)] + side_scratch,
        cost=pl.CostEstimate(flops=4 * slot_count * wide * wide, bytes_accessed=8 << 20, transcendentals=0),
    )
    far_last, values = call(
        functools.partial(diffuse_last, width=width),
        (kept, found, start, far, diffusivity, cells),
        [ends, slot_blocks],
        side_scratch,
    )
    returned = exchange(values, tiles, share)
    turns = fine // chunk
    some = rows // turns if rows % turns == 0 else rows
    all_of = lambda count: pl.BlockSpec((count, channels, wide), lambda i: (0, 0, 0))
    result, field = call(
        functools.partial(sum_from_slots, plan=plan_of(chunk // LANES)),
        (returned, slots, tent_weight, inner, near_last, far_last),
        [shape((channels, fine), F32), shape((rows, channels, width), F32)],
        [pltpu.VMEM((2 * channels * slot_count // PLACES, PLACES), BF16)],
        grid=(turns,),
        in_specs=[whole, part(CORNERS), part(CORNERS), all_of(rows - 2 * STEPS), all_of(STEPS), all_of(STEPS)],
        out_specs=[part(channels), pl.BlockSpec((some, channels, width), lambda i: (i, 0, 0))],
        memory=32,
    )
    return (result, field.transpose(1, 0, 2))


def exchange(blocks, tiles, share):
    count, channels, lanes = blocks.shape
    if share == lanes:
        return lax.all_to_all(blocks, "tile", split_axis=0, concat_axis=0, tiled=True)
    flat = blocks.transpose(1, 0, 2).reshape(channels, count * lanes)
    flat = lax.all_to_all(flat, "tile", split_axis=1, concat_axis=1, tiled=True)
    return flat.reshape(channels, count, lanes).transpose(1, 0, 2)


def solution(mesh):
    in_specs = (
        P(None, ("group", "tile")),
        P("tile", None),
        P(None, "tile"),
        P("tile"),
        P("tile", None),
    )
    out_specs = (P(None, ("group", "tile")), P(None, ("group", "tile"), None))
    return jax.shard_map(body, mesh=mesh, in_specs=in_specs, out_specs=out_specs, check_vma=False)
```

```python
import functools

import jax
import jax.numpy as jnp
from jax import lax
from jax.experimental import pallas as pl
from jax.experimental.pallas import tpu as pltpu
from jax.sharding import PartitionSpec as P

STEPS = 5
CORNERS = 4
LANES = 128
PLACES = 256
EDGE = STEPS + (STEPS + 1) // 2
BF16 = jnp.bfloat16
F32 = jnp.float32
VMEM = pl.BlockSpec(memory_space=pltpu.VMEM)


def halves(values):
    high = values.astype(BF16)
    return high, (values - high.astype(F32)).astype(BF16)


def one_hot(places, length):
    rows = lax.broadcasted_iota(jnp.int32, (length, places.shape[1]), 0)
    return jnp.where(rows == places, 1.0, 0.0).astype(BF16)


def masked(values, marks, wanted):
    marks = jnp.broadcast_to(marks, values.shape)
    zero = jnp.zeros((), values.dtype)
    return jnp.concatenate([jnp.where(marks == k, values, zero) for k in wanted], 0)


def dot_last(left, right):
    return lax.dot_general(left, right, (((1,), (1,)), ((), ())), preferred_element_type=F32)


def sum_to_slots(inc_ref, slot_ref, weight_ref, sent_ref):
    channels = inc_ref.shape[0]
    count = sent_ref.shape[0] * LANES // PLACES
    inc = inc_ref[...]
    left, right = [], []
    for corner in range(CORNERS):
        slots = slot_ref[corner : corner + 1, :]
        parts = jnp.concatenate(halves(weight_ref[corner : corner + 1, :] * inc), 0)
        left.append(masked(parts, slots // PLACES, range(count)))
        right.append(one_hot(slots % PLACES, PLACES))
    sums = dot_last(jnp.concatenate(left, 1), jnp.concatenate(right, 1))

    @pl.when(pl.program_id(0) == 0)
    def _():
        sent_ref[...] = jnp.zeros_like(sent_ref)

    for k in range(count):
        both = sums[2 * channels * k : 2 * channels * (k + 1)]
        both = both[:channels] + both[channels:]
        for part in range(PLACES // LANES):
            sent_ref[k * (PLACES // LANES) + part] += both[:, LANES * part : LANES * (part + 1)]


def wide_column(width):
    lanes = lax.broadcasted_iota(jnp.int32, (2 * LANES, 1), 0)
    extra = (2 * LANES - width) // 2
    return jnp.where(lanes < width, lanes, jnp.where(lanes < width + extra, lanes - width, lanes - 2 * LANES + width))


def place_edge(edge_ref, rows, coefs, width):
    half = width - LANES
    for k, row in enumerate(rows):
        edge_ref[k] = row[:, :LANES]
    ends = [row[:, LANES:width] for row in rows]
    for k in range(0, STEPS - 1, 2):
        edge_ref[STEPS + k // 2] = jnp.concatenate([ends[k], ends[k + 1]], 1)
    edge_ref[EDGE - 1] = jnp.concatenate([ends[-1], jnp.zeros_like(ends[-1])], 1)
    for k, coef in enumerate(coefs):
        for part in range(3):
            edge_ref[EDGE - 1, 3 * k + part : 3 * k + part + 1, half:] = coef[:, half * part : half * (part + 1)]


def read_edge(edge_ref, k, width):
    half = width - LANES
    start = edge_ref[k]
    end = edge_ref[STEPS + k // 2, :, half * (k % 2) : half * (k % 2) + half]
    return widened([start, end], start, end, width)


def read_coef(edge_ref, k, width):
    half = width - LANES
    parts = [edge_ref[EDGE - 1, 3 * k + part : 3 * k + part + 1, half:] for part in range(3)]
    return widened(parts, parts[0], parts[2], width)


def widened(parts, start, end, width):
    extra = (2 * LANES - width) // 2
    return jnp.concatenate(parts + [start[:, :extra], end[:, end.shape[1] - extra :]], 1)


def cell_sums(rec_ref, cell_ref, ys, width):
    senders, channels, _ = rec_ref.shape
    cells = jnp.concatenate([cell_ref[s : s + 1, :] for s in range(senders)], 1)
    values = jnp.concatenate([rec_ref[s] for s in range(senders)], 1)
    y = cells // width
    right = jnp.where(wide_column(width) == cells - y * width, 1.0, 0.0).astype(BF16)
    sums = dot_last(masked(jnp.concatenate(halves(values), 0), y, ys), right)
    full = []
    for k in range(len(ys)):
        both = sums[2 * channels * k : 2 * channels * (k + 1)]
        full.append(both[:channels] + both[channels:])
    return full


def edge_starts(rows):
    even = lax.axis_index("tile") % 2 == 0
    return jnp.where(even, 0, rows - STEPS), jnp.where(even, rows - STEPS, 0)


def sum_edges(rec_ref, cell_ref, coef_ref, edges_ref, far_ref, near_ref, *, width):
    starts = edge_starts(coef_ref.shape[0])
    ys = [start + k for start in starts for k in range(STEPS)]
    full = cell_sums(rec_ref, cell_ref, ys, width)
    for k, row in enumerate(full):
        edges_ref[k] = row
    for edge_ref, at in ((far_ref, 0), (near_ref, STEPS)):
        coefs = [coef_ref[pl.ds(y, 1), :] for y in ys[at : at + STEPS]]
        place_edge(edge_ref, full[at : at + STEPS], coefs, width)


def stepped(above, here, below, coef):
    wide = here.shape[-1]
    spread = below + above + pltpu.roll(here, 1, 1) + pltpu.roll(here, wide - 1, 1)
    return here + coef * (spread - 4.0 * here)


def kept_rows(turn, total):
    first, last = STEPS + turn, total - STEPS - turn
    return [first, first + 1, last - 2, last - 1]


def read_rows(final_rows, ys, cell_ref, values_ref, base, width):
    senders, channels, _ = values_ref.shape
    left = jnp.concatenate([jnp.concatenate(halves(row), 0) for row in final_rows], 0)
    for s in range(0, senders, 2):
        cells = jnp.concatenate([cell_ref[s : s + 1, :], cell_ref[s + 1 : s + 2, :]], 1)
        y = cells // width
        found = jnp.dot(left, one_hot(cells - y * width, left.shape[1]), preferred_element_type=F32)
        out = base(s)
        marks = jnp.broadcast_to(y, out.shape)
        for k, row in enumerate(ys):
            both = found[2 * channels * k : 2 * channels * (k + 1)]
            out = jnp.where(marks == row, both[:channels] + both[channels:], out)
        values_ref[s] = out[:, :LANES]
        values_ref[s + 1] = out[:, LANES:]


def inner_rows(start_ref, own_ref, kept_ref, one_ref, two_ref, coef_ref, width):
    rows = start_ref.shape[0]
    own = own_ref[...]
    coef_ref[...] = widened([own], own, own, width)
    held, other, last = start_ref, one_ref, two_ref
    for turn in range(1, STEPS + 1):
        for y in range(turn, rows - turn):
            other[y] = stepped(held[y - 1], held[y], held[y + 1], coef_ref[y : y + 1, :])
        if turn < STEPS:
            for place, y in enumerate(kept_rows(turn, rows + 2 * STEPS)):
                kept_ref[turn - 1, place] = other[y - STEPS]
        held, other, last = other, last, other
    return [held[y] for y in range(STEPS, rows - STEPS)]


def side_rows(start_ref, edge_ref, own_ref, kept_ref, one_ref, two_ref, coef_ref, width, first):
    rows = own_ref.shape[0]
    head = first == 0
    flip = lambda ahead, behind: jnp.where(head, ahead, behind)
    for k in range(STEPS):
        place = flip(k, STEPS - 1 - k)
        one_ref[place] = read_edge(edge_ref, k, width)
        coef_ref[pl.ds(place, 1), :] = read_coef(edge_ref, k, width)
        own = own_ref[pl.ds(flip(k, rows - 1 - k), 1), :]
        coef_ref[STEPS + k : STEPS + k + 1, :] = widened([own], own, own, width)
    held = {u: one_ref[u] for u in range(STEPS)}
    for turn in range(1, STEPS + 1):
        for u in (STEPS + turn - 1, STEPS + turn):
            k = u - STEPS - turn + 1
            inside = start_ref[flip(u - STEPS, rows - 1 - u + STEPS)] if turn == 1 else kept_ref[turn - 2, flip(k, 3 - k)]
            held[u] = inside
        ours = range(turn, turn + STEPS)
        held = {u: stepped(held[u - 1], held[u], held[u + 1], coef_ref[u : u + 1, :]) for u in ours}
    for u, row in held.items():
        two_ref[u] = row
    return [two_ref[flip(STEPS + k, 2 * STEPS - 1 - k)] for k in range(STEPS)]


def diffuse_most(
    rec_ref, edges_ref, edge_ref, own_ref, cell_ref, start_ref, kept_ref, inner_ref, side_ref, values_ref,
    one_ref, two_ref, coef_ref, side_one_ref, side_two_ref, side_coef_ref, *, width
):
    rows, channels, _ = start_ref.shape
    far, first = edge_starts(rows)
    for k in range(STEPS):
        start_ref[far + k] = edges_ref[k]
        start_ref[first + k] = edges_ref[STEPS + k]
    within = range(STEPS, rows - STEPS)
    for y, row in zip(within, cell_sums(rec_ref, cell_ref, within, width)):
        start_ref[y] = row
    inner = inner_rows(start_ref, own_ref, kept_ref, one_ref, two_ref, coef_ref, width)
    side = side_rows(
        start_ref, edge_ref, own_ref, kept_ref, side_one_ref, side_two_ref, side_coef_ref, width, first
    )
    for k, row in enumerate(inner):
        inner_ref[k] = row
    for k, row in enumerate(side):
        side_ref[k] = row
    ys = list(range(STEPS, rows - STEPS)) + [first + k for k in range(STEPS)]
    nothing = lambda s: jnp.zeros((channels, 2 * LANES), F32)
    read_rows(inner + side, ys, cell_ref, values_ref, nothing, width)


def diffuse_last(
    kept_ref, part_ref, start_ref, edge_ref, own_ref, cell_ref, side_ref, values_ref, one_ref, two_ref, coef_ref, *, width
):
    first, _ = edge_starts(own_ref.shape[0])
    side = side_rows(start_ref, edge_ref, own_ref, kept_ref, one_ref, two_ref, coef_ref, width, first)
    for k, row in enumerate(side):
        side_ref[k] = row
    base = lambda s: jnp.concatenate([part_ref[s], part_ref[s + 1]], 1)
    read_rows(side, [first + k for k in range(STEPS)], cell_ref, values_ref, base, width)


def by_product(table_ref, slot_ref, weight_ref, columns, channels):
    count = table_ref.shape[0] // (2 * channels)
    total = 0.0
    for corner in range(CORNERS):
        slots = slot_ref[corner : corner + 1, columns]
        found = jnp.dot(table_ref[...], one_hot(slots % PLACES, PLACES), preferred_element_type=F32)
        marks = jnp.broadcast_to(slots // PLACES, (channels, slots.shape[1]))
        out = None
        for k in range(count):
            both = found[2 * channels * k : 2 * channels * (k + 1)]
            both = both[:channels] + both[channels:]
            out = both if out is None else jnp.where(marks == k, both, out)
        total = total + weight_ref[corner : corner + 1, columns] * out
    return total


def by_lanes(ret_ref, slot_ref, weight_ref, columns):
    blocks, channels, _ = ret_ref.shape
    group = 8
    totals = [0.0] * (channels // group)
    for corner in range(CORNERS):
        slots = slot_ref[corner : corner + 1, columns]
        weight = weight_ref[corner : corner + 1, columns]
        lanes = jnp.broadcast_to(slots % LANES, (group, LANES))
        block = jnp.broadcast_to(slots // LANES, (group, LANES))
        marks = [block == k for k in range(blocks)]
        for c in range(channels // group):
            out = None
            for k in range(blocks):
                found = jnp.take_along_axis(ret_ref[k, group * c : group * (c + 1), :], lanes, axis=1)
                out = found if out is None else jnp.where(marks[k], found, out)
            totals[c] = totals[c] + weight * out
    return jnp.concatenate(totals, 0)


def sum_from_slots(
    ret_ref, slot_ref, weight_ref, inner_ref, near_ref, far_ref, result_ref, field_ref, table_ref, *, plan
):
    blocks, channels, _ = ret_ref.shape
    some, _, width = field_ref.shape
    inner = inner_ref.shape[0]
    far, _ = edge_starts(inner + 2 * STEPS)
    for k in range(some):
        y = pl.program_id(0) * some + k
        at = jnp.clip(jnp.where(y < STEPS, y, y - STEPS - inner), 0, STEPS - 1)
        is_inner = (y >= STEPS) & (y < STEPS + inner)
        edge = jnp.where((y < STEPS) == (far == 0), far_ref[at], near_ref[at])
        row = jnp.where(is_inner, inner_ref[jnp.clip(y - STEPS, 0, inner - 1)], edge)
        field_ref[k] = row[:, :width]
    group = PLACES // LANES

    @pl.when(pl.program_id(0) == 0)
    def _():
        for k in range(blocks // group):
            both = halves(jnp.concatenate([ret_ref[group * k + part] for part in range(group)], 1))
            table_ref[2 * channels * k : 2 * channels * (k + 1), :] = jnp.concatenate(both, 0)

    at = 0
    for product, single in plan:
        columns = slice(at, at + product * LANES)
        result_ref[:, columns] = by_product(table_ref, slot_ref, weight_ref, columns, channels)
        for k in range(product, product + single):
            columns = slice(at + k * LANES, at + (k + 1) * LANES)
            result_ref[:, columns] = by_lanes(ret_ref, slot_ref, weight_ref, columns)
        at += (product + single) * LANES


def plan_of(blocks):
    return [(blocks - blocks // 3, blocks // 3)]


def chunk_of(fine, most):
    return max(c for c in range(LANES, most + 1, LANES) if fine % c == 0)


def call(kernel, ins, out, scratch=(), grid=(), in_specs=VMEM, out_specs=VMEM, memory=16, cost=None):
    single = isinstance(in_specs, pl.BlockSpec)
    return pl.pallas_call(
        kernel,
        grid=grid,
        out_shape=out,
        in_specs=[in_specs] * len(ins) if single else in_specs,
        out_specs=[out_specs] * len(out) if single and isinstance(out, list) else out_specs,
        scratch_shapes=list(scratch),
        cost_estimate=cost,
        compiler_params=pltpu.CompilerParams(vmem_limit_bytes=memory << 20),
    )(*ins)


def body(increment, send_slots, tent_weight, coarse_cell, diffusivity):
    channels, fine = increment.shape
    slot_count = coarse_cell.shape[0]
    rows, width = diffusivity.shape
    tiles = lax.axis_size("tile")
    share = slot_count // tiles
    blocks = slot_count // LANES
    wide = 2 * LANES
    on_chip = [(i, i ^ 1) for i in range(tiles)]
    off_chip = [(i, (i + 2 * (i % 2) - 1) % tiles) for i in range(tiles)]
    shape = jax.ShapeDtypeStruct
    slots = send_slots.T
    cells = coarse_cell.reshape(blocks, LANES)
    chunk = chunk_of(fine, 3456)
    part = lambda n: pl.BlockSpec((n, chunk), lambda i: (0, i))
    full = lambda n: pl.BlockSpec((n, fine), lambda i: (0, 0))
    whole = pl.BlockSpec((blocks, channels, LANES), lambda i: (0, 0, 0))

    sent = call(
        sum_to_slots,
        (increment, slots, tent_weight),
        shape((blocks, channels, LANES), F32),
        grid=(1,),
        in_specs=[full(channels), full(CORNERS), full(CORNERS)],
        out_specs=whole,
        memory=56,
    )
    received = exchange(sent, tiles, share)
    edge = shape((EDGE, channels, LANES), F32)
    slot_blocks = shape((blocks, channels, LANES), F32)
    edges, far, near = call(
        functools.partial(sum_edges, width=width),
        (received, cells, diffusivity),
        [shape((2 * STEPS, channels, wide), F32), edge, edge],
    )
    far = lax.ppermute(far, "tile", off_chip)
    near = lax.ppermute(near, "tile", on_chip)
    own = pltpu.VMEM((rows, channels, wide), F32)
    ends = shape((STEPS, channels, wide), F32)
    side = pltpu.VMEM((2 * STEPS + 1, channels, wide), F32)
    side_scratch = [side, side, pltpu.VMEM((2 * STEPS, wide), F32)]
    start, kept, inner, near_last, found = call(
        functools.partial(diffuse_most, width=width),
        (received, edges, near, diffusivity, cells),
        [
            shape((rows, channels, wide), F32),
            shape((STEPS - 1, 4, channels, wide), F32),
            shape((rows - 2 * STEPS, channels, wide), F32),
            ends,
            slot_blocks,
        ],
        [own, own, pltpu.VMEM((rows, wide), F32)] + side_scratch,
        cost=pl.CostEstimate(flops=4 * slot_count * wide * wide, bytes_accessed=8 << 20, transcendentals=0),
    )
    far_last, values = call(
        functools.partial(diffuse_last, width=width),
        (kept, found, start, far, diffusivity, cells),
        [ends, slot_blocks],
        side_scratch,
    )
    returned = exchange(values, tiles, share)
    turns = fine // chunk
    some = rows // turns if rows % turns == 0 else rows
    all_of = lambda count: pl.BlockSpec((count, channels, wide), lambda i: (0, 0, 0))
    result, field = call(
        functools.partial(sum_from_slots, plan=plan_of(chunk // LANES)),
        (returned, slots, tent_weight, inner, near_last, far_last),
        [shape((channels, fine), F32), shape((rows, channels, width), F32)],
        [pltpu.VMEM((2 * channels * slot_count // PLACES, PLACES), BF16)],
        grid=(turns,),
        in_specs=[whole, part(CORNERS), part(CORNERS), all_of(rows - 2 * STEPS), all_of(STEPS), all_of(STEPS)],
        out_specs=[part(channels), pl.BlockSpec((some, channels, width), lambda i: (i, 0, 0))],
        memory=32,
    )
    return (result, field.transpose(1, 0, 2))


def exchange(blocks, tiles, share):
    count, channels, lanes = blocks.shape
    if share == lanes:
        return lax.all_to_all(blocks, "tile", split_axis=0, concat_axis=0, tiled=True)
    flat = blocks.transpose(1, 0, 2).reshape(channels, count * lanes)
    flat = lax.all_to_all(flat, "tile", split_axis=1, concat_axis=1, tiled=True)
    return flat.reshape(channels, count, lanes).transpose(1, 0, 2)


def solution(mesh):
    in_specs = (
        P(None, ("group", "tile")),
        P("tile", None),
        P(None, "tile"),
        P("tile"),
        P("tile", None),
    )
    out_specs = (P(None, ("group", "tile")), P(None, ("group", "tile"), None))
    return jax.shard_map(body, mesh=mesh, in_specs=in_specs, out_specs=out_specs, check_vma=False)
```

```python
import functools

import jax
import jax.numpy as jnp
from jax import lax
from jax.experimental import pallas as pl
from jax.experimental.pallas import tpu as pltpu
from jax.sharding import PartitionSpec as P

STEPS = 5
CORNERS = 4
LANES = 128
PLACES = 256
EDGE = STEPS + (STEPS + 1) // 2
BF16 = jnp.bfloat16
F32 = jnp.float32
VMEM = pl.BlockSpec(memory_space=pltpu.VMEM)


def halves(values):
    high = values.astype(BF16)
    return high, (values - high.astype(F32)).astype(BF16)


def one_hot(places, length):
    rows = lax.broadcasted_iota(jnp.int32, (length, places.shape[1]), 0)
    return jnp.where(rows == places, 1.0, 0.0).astype(BF16)


def masked(values, marks, wanted):
    marks = jnp.broadcast_to(marks, values.shape)
    zero = jnp.zeros((), values.dtype)
    return jnp.concatenate([jnp.where(marks == k, values, zero) for k in wanted], 0)


def dot_last(left, right):
    return lax.dot_general(left, right, (((1,), (1,)), ((), ())), preferred_element_type=F32)


def sum_to_slots(inc_ref, slot_ref, weight_ref, sent_ref):
    channels = inc_ref.shape[0]
    count = sent_ref.shape[0] * LANES // PLACES
    inc = inc_ref[...]
    left, right = [], []
    for corner in range(CORNERS):
        slots = slot_ref[corner : corner + 1, :]
        parts = jnp.concatenate(halves(weight_ref[corner : corner + 1, :] * inc), 0)
        left.append(masked(parts, slots // PLACES, range(count)))
        right.append(one_hot(slots % PLACES, PLACES))
    sums = dot_last(jnp.concatenate(left, 1), jnp.concatenate(right, 1))

    @pl.when(pl.program_id(0) == 0)
    def _():
        sent_ref[...] = jnp.zeros_like(sent_ref)

    for k in range(count):
        both = sums[2 * channels * k : 2 * channels * (k + 1)]
        both = both[:channels] + both[channels:]
        for part in range(PLACES // LANES):
            sent_ref[k * (PLACES // LANES) + part] += both[:, LANES * part : LANES * (part + 1)]


def wide_column(width):
    lanes = lax.broadcasted_iota(jnp.int32, (2 * LANES, 1), 0)
    extra = (2 * LANES - width) // 2
    return jnp.where(lanes < width, lanes, jnp.where(lanes < width + extra, lanes - width, lanes - 2 * LANES + width))


def place_edge(edge_ref, rows, coefs, width):
    half = width - LANES
    for k, row in enumerate(rows):
        edge_ref[k] = row[:, :LANES]
    ends = [row[:, LANES:width] for row in rows]
    for k in range(0, STEPS - 1, 2):
        edge_ref[STEPS + k // 2] = jnp.concatenate([ends[k], ends[k + 1]], 1)
    edge_ref[EDGE - 1] = jnp.concatenate([ends[-1], jnp.zeros_like(ends[-1])], 1)
    for k, coef in enumerate(coefs):
        for part in range(3):
            edge_ref[EDGE - 1, 3 * k + part : 3 * k + part + 1, half:] = coef[:, half * part : half * (part + 1)]


def read_edge(edge_ref, k, width):
    half = width - LANES
    start = edge_ref[k]
    end = edge_ref[STEPS + k // 2, :, half * (k % 2) : half * (k % 2) + half]
    return widened([start, end], start, end, width)


def read_coef(edge_ref, k, width):
    half = width - LANES
    parts = [edge_ref[EDGE - 1, 3 * k + part : 3 * k + part + 1, half:] for part in range(3)]
    return widened(parts, parts[0], parts[2], width)


def widened(parts, start, end, width):
    extra = (2 * LANES - width) // 2
    return jnp.concatenate(parts + [start[:, :extra], end[:, end.shape[1] - extra :]], 1)


def cell_sums(rec_ref, cell_ref, ys, width):
    senders, channels, _ = rec_ref.shape
    cells = jnp.concatenate([cell_ref[s : s + 1, :] for s in range(senders)], 1)
    values = jnp.concatenate([rec_ref[s] for s in range(senders)], 1)
    y = cells // width
    right = jnp.where(wide_column(width) == cells - y * width, 1.0, 0.0).astype(BF16)
    sums = dot_last(masked(jnp.concatenate(halves(values), 0), y, ys), right)
    full = []
    for k in range(len(ys)):
        both = sums[2 * channels * k : 2 * channels * (k + 1)]
        full.append(both[:channels] + both[channels:])
    return full


def edge_starts(rows):
    even = lax.axis_index("tile") % 2 == 0
    return jnp.where(even, 0, rows - STEPS), jnp.where(even, rows - STEPS, 0)


def sum_edges(rec_ref, cell_ref, coef_ref, edges_ref, far_ref, near_ref, *, width):
    starts = edge_starts(coef_ref.shape[0])
    ys = [start + k for start in starts for k in range(STEPS)]
    full = cell_sums(rec_ref, cell_ref, ys, width)
    for k, row in enumerate(full):
        edges_ref[k] = row
    for edge_ref, at in ((far_ref, 0), (near_ref, STEPS)):
        coefs = [coef_ref[pl.ds(y, 1), :] for y in ys[at : at + STEPS]]
        place_edge(edge_ref, full[at : at + STEPS], coefs, width)


def stepped(above, here, below, coef):
    wide = here.shape[-1]
    spread = below + above + pltpu.roll(here, 1, 1) + pltpu.roll(here, wide - 1, 1)
    return here + coef * (spread - 4.0 * here)


def kept_rows(turn, total):
    first, last = STEPS + turn, total - STEPS - turn
    return [first, first + 1, last - 2, last - 1]


def read_by_lanes(rows_ref, ys, cell_ref, values_ref, part_ref, senders, width):
    channels = values_ref.shape[1]
    group = 8
    for s in senders:
        cells = jnp.broadcast_to(cell_ref[s : s + 1, :], (group, LANES))
        y = cells // width
        x = cells - y * width
        lanes = x % LANES
        marks = [[(y == row) & (x // LANES == part) for part in range(2)] for row in ys]
        for c in range(0, channels, group):
            out = part_ref[s, c : c + group, :]
            for k in range(len(ys)):
                for part in range(2):
                    side = rows_ref[k, c : c + group, LANES * part : LANES * (part + 1)]
                    out = jnp.where(marks[k][part], jnp.take_along_axis(side, lanes, axis=1), out)
            values_ref[s, c : c + group, :] = out


def read_rows(final_rows, ys, cell_ref, values_ref, base, width, senders=None):
    senders = values_ref.shape[0] if senders is None else senders
    channels = values_ref.shape[1]
    left = jnp.concatenate([jnp.concatenate(halves(row), 0) for row in final_rows], 0)
    for s in range(0, senders, 2):
        cells = jnp.concatenate([cell_ref[s : s + 1, :], cell_ref[s + 1 : s + 2, :]], 1)
        y = cells // width
        found = jnp.dot(left, one_hot(cells - y * width, left.shape[1]), preferred_element_type=F32)
        out = base(s)
        marks = jnp.broadcast_to(y, out.shape)
        for k, row in enumerate(ys):
            both = found[2 * channels * k : 2 * channels * (k + 1)]
            out = jnp.where(marks == row, both[:channels] + both[channels:], out)
        values_ref[s] = out[:, :LANES]
        values_ref[s + 1] = out[:, LANES:]


def inner_rows(start_ref, own_ref, kept_ref, one_ref, two_ref, coef_ref, width):
    rows = start_ref.shape[0]
    own = own_ref[...]
    coef_ref[...] = widened([own], own, own, width)
    held, other, last = start_ref, one_ref, two_ref
    for turn in range(1, STEPS + 1):
        for y in range(turn, rows - turn):
            other[y] = stepped(held[y - 1], held[y], held[y + 1], coef_ref[y : y + 1, :])
        if turn < STEPS:
            for place, y in enumerate(kept_rows(turn, rows + 2 * STEPS)):
                kept_ref[turn - 1, place] = other[y - STEPS]
        held, other, last = other, last, other
    return [held[y] for y in range(STEPS, rows - STEPS)]


def side_rows(start_ref, edge_ref, own_ref, kept_ref, one_ref, two_ref, coef_ref, width, first):
    rows = own_ref.shape[0]
    head = first == 0
    flip = lambda ahead, behind: jnp.where(head, ahead, behind)
    for k in range(STEPS):
        place = flip(k, STEPS - 1 - k)
        one_ref[place] = read_edge(edge_ref, k, width)
        coef_ref[pl.ds(place, 1), :] = read_coef(edge_ref, k, width)
        own = own_ref[pl.ds(flip(k, rows - 1 - k), 1), :]
        coef_ref[STEPS + k : STEPS + k + 1, :] = widened([own], own, own, width)
    held = {u: one_ref[u] for u in range(STEPS)}
    for turn in range(1, STEPS + 1):
        for u in (STEPS + turn - 1, STEPS + turn):
            k = u - STEPS - turn + 1
            inside = start_ref[flip(u - STEPS, rows - 1 - u + STEPS)] if turn == 1 else kept_ref[turn - 2, flip(k, 3 - k)]
            held[u] = inside
        ours = range(turn, turn + STEPS)
        held = {u: stepped(held[u - 1], held[u], held[u + 1], coef_ref[u : u + 1, :]) for u in ours}
    for u, row in held.items():
        two_ref[u] = row
    return [two_ref[flip(STEPS + k, 2 * STEPS - 1 - k)] for k in range(STEPS)]


def diffuse_most(
    rec_ref, edges_ref, edge_ref, own_ref, cell_ref, start_ref, kept_ref, inner_ref, side_ref, values_ref,
    one_ref, two_ref, coef_ref, side_one_ref, side_two_ref, side_coef_ref, *, width
):
    rows, channels, _ = start_ref.shape
    far, first = edge_starts(rows)
    for k in range(STEPS):
        start_ref[far + k] = edges_ref[k]
        start_ref[first + k] = edges_ref[STEPS + k]
    within = range(STEPS, rows - STEPS)
    for y, row in zip(within, cell_sums(rec_ref, cell_ref, within, width)):
        start_ref[y] = row
    inner = inner_rows(start_ref, own_ref, kept_ref, one_ref, two_ref, coef_ref, width)
    side = side_rows(
        start_ref, edge_ref, own_ref, kept_ref, side_one_ref, side_two_ref, side_coef_ref, width, first
    )
    for k, row in enumerate(inner):
        inner_ref[k] = row
    for k, row in enumerate(side):
        side_ref[k] = row
    ys = list(range(STEPS, rows - STEPS)) + [first + k for k in range(STEPS)]
    nothing = lambda s: jnp.zeros((channels, 2 * LANES), F32)
    read_rows(inner + side, ys, cell_ref, values_ref, nothing, width)


def diffuse_last(
    kept_ref, part_ref, start_ref, edge_ref, own_ref, cell_ref, side_ref, values_ref, one_ref, two_ref, coef_ref, *, width
):
    first, _ = edge_starts(own_ref.shape[0])
    side = side_rows(start_ref, edge_ref, own_ref, kept_ref, one_ref, two_ref, coef_ref, width, first)
    for k, row in enumerate(side):
        side_ref[k] = row
    base = lambda s: jnp.concatenate([part_ref[s], part_ref[s + 1]], 1)
    ys = [first + k for k in range(STEPS)]
    senders = values_ref.shape[0]
    products = senders - 2 * (3 * senders // 16)
    read_rows(side, ys, cell_ref, values_ref, base, width, products)
    read_by_lanes(side_ref, ys, cell_ref, values_ref, part_ref, range(products, senders), width)


def by_product(table_ref, slot_ref, weight_ref, columns, channels):
    count = table_ref.shape[0] // (2 * channels)
    total = 0.0
    for corner in range(CORNERS):
        slots = slot_ref[corner : corner + 1, columns]
        found = jnp.dot(table_ref[...], one_hot(slots % PLACES, PLACES), preferred_element_type=F32)
        marks = jnp.broadcast_to(slots // PLACES, (channels, slots.shape[1]))
        out = None
        for k in range(count):
            both = found[2 * channels * k : 2 * channels * (k + 1)]
            both = both[:channels] + both[channels:]
            out = both if out is None else jnp.where(marks == k, both, out)
        total = total + weight_ref[corner : corner + 1, columns] * out
    return total


def by_lanes(ret_ref, slot_ref, weight_ref, columns):
    blocks, channels, _ = ret_ref.shape
    group = 8
    totals = [0.0] * (channels // group)
    for corner in range(CORNERS):
        slots = slot_ref[corner : corner + 1, columns]
        weight = weight_ref[corner : corner + 1, columns]
        lanes = jnp.broadcast_to(slots % LANES, (group, LANES))
        block = jnp.broadcast_to(slots // LANES, (group, LANES))
        marks = [block == k for k in range(blocks)]
        for c in range(channels // group):
            out = None
            for k in range(blocks):
                found = jnp.take_along_axis(ret_ref[k, group * c : group * (c + 1), :], lanes, axis=1)
                out = found if out is None else jnp.where(marks[k], found, out)
            totals[c] = totals[c] + weight * out
    return jnp.concatenate(totals, 0)


def sum_from_slots(
    ret_ref, slot_ref, weight_ref, inner_ref, near_ref, far_ref, result_ref, field_ref, table_ref, *, plan
):
    blocks, channels, _ = ret_ref.shape
    some, _, width = field_ref.shape
    inner = inner_ref.shape[0]
    far, _ = edge_starts(inner + 2 * STEPS)
    for k in range(some):
        y = pl.program_id(0) * some + k
        at = jnp.clip(jnp.where(y < STEPS, y, y - STEPS - inner), 0, STEPS - 1)
        is_inner = (y >= STEPS) & (y < STEPS + inner)
        edge = jnp.where((y < STEPS) == (far == 0), far_ref[at], near_ref[at])
        row = jnp.where(is_inner, inner_ref[jnp.clip(y - STEPS, 0, inner - 1)], edge)
        field_ref[k] = row[:, :width]
    group = PLACES // LANES

    @pl.when(pl.program_id(0) == 0)
    def _():
        for k in range(blocks // group):
            both = halves(jnp.concatenate([ret_ref[group * k + part] for part in range(group)], 1))
            table_ref[2 * channels * k : 2 * channels * (k + 1), :] = jnp.concatenate(both, 0)

    at = 0
    for product, single in plan:
        columns = slice(at, at + product * LANES)
        result_ref[:, columns] = by_product(table_ref, slot_ref, weight_ref, columns, channels)
        for k in range(product, product + single):
            columns = slice(at + k * LANES, at + (k + 1) * LANES)
            result_ref[:, columns] = by_lanes(ret_ref, slot_ref, weight_ref, columns)
        at += (product + single) * LANES


def plan_of(blocks):
    return [(blocks - blocks // 3, blocks // 3)]


def chunk_of(fine, most):
    return max(c for c in range(LANES, most + 1, LANES) if fine % c == 0)


def call(kernel, ins, out, scratch=(), grid=(), in_specs=VMEM, out_specs=VMEM, memory=16, cost=None):
    single = isinstance(in_specs, pl.BlockSpec)
    return pl.pallas_call(
        kernel,
        grid=grid,
        out_shape=out,
        in_specs=[in_specs] * len(ins) if single else in_specs,
        out_specs=[out_specs] * len(out) if single and isinstance(out, list) else out_specs,
        scratch_shapes=list(scratch),
        cost_estimate=cost,
        compiler_params=pltpu.CompilerParams(vmem_limit_bytes=memory << 20),
    )(*ins)


def body(increment, send_slots, tent_weight, coarse_cell, diffusivity):
    channels, fine = increment.shape
    slot_count = coarse_cell.shape[0]
    rows, width = diffusivity.shape
    tiles = lax.axis_size("tile")
    share = slot_count // tiles
    blocks = slot_count // LANES
    wide = 2 * LANES
    on_chip = [(i, i ^ 1) for i in range(tiles)]
    off_chip = [(i, (i + 2 * (i % 2) - 1) % tiles) for i in range(tiles)]
    shape = jax.ShapeDtypeStruct
    slots = send_slots.T
    cells = coarse_cell.reshape(blocks, LANES)
    chunk = chunk_of(fine, 3456)
    part = lambda n: pl.BlockSpec((n, chunk), lambda i: (0, i))
    full = lambda n: pl.BlockSpec((n, fine), lambda i: (0, 0))
    whole = pl.BlockSpec((blocks, channels, LANES), lambda i: (0, 0, 0))

    sent = call(
        sum_to_slots,
        (increment, slots, tent_weight),
        shape((blocks, channels, LANES), F32),
        grid=(1,),
        in_specs=[full(channels), full(CORNERS), full(CORNERS)],
        out_specs=whole,
        memory=56,
    )
    received = exchange(sent, tiles, share)
    edge = shape((EDGE, channels, LANES), F32)
    slot_blocks = shape((blocks, channels, LANES), F32)
    edges, far, near = call(
        functools.partial(sum_edges, width=width),
        (received, cells, diffusivity),
        [shape((2 * STEPS, channels, wide), F32), edge, edge],
    )
    far = lax.ppermute(far, "tile", off_chip)
    near = lax.ppermute(near, "tile", on_chip)
    own = pltpu.VMEM((rows, channels, wide), F32)
    ends = shape((STEPS, channels, wide), F32)
    side = pltpu.VMEM((2 * STEPS + 1, channels, wide), F32)
    side_scratch = [side, side, pltpu.VMEM((2 * STEPS, wide), F32)]
    start, kept, inner, near_last, found = call(
        functools.partial(diffuse_most, width=width),
        (received, edges, near, diffusivity, cells),
        [
            shape((rows, channels, wide), F32),
            shape((STEPS - 1, 4, channels, wide), F32),
            shape((rows - 2 * STEPS, channels, wide), F32),
            ends,
            slot_blocks,
        ],
        [own, own, pltpu.VMEM((rows, wide), F32)] + side_scratch,
        cost=pl.CostEstimate(flops=4 * slot_count * wide * wide, bytes_accessed=8 << 20, transcendentals=0),
    )
    far_last, values = call(
        functools.partial(diffuse_last, width=width),
        (kept, found, start, far, diffusivity, cells),
        [ends, slot_blocks],
        side_scratch,
    )
    returned = exchange(values, tiles, share)
    turns = fine // chunk
    some = rows // turns if rows % turns == 0 else rows
    all_of = lambda count: pl.BlockSpec((count, channels, wide), lambda i: (0, 0, 0))
    result, field = call(
        functools.partial(sum_from_slots, plan=plan_of(chunk // LANES)),
        (returned, slots, tent_weight, inner, near_last, far_last),
        [shape((channels, fine), F32), shape((rows, channels, width), F32)],
        [pltpu.VMEM((2 * channels * slot_count // PLACES, PLACES), BF16)],
        grid=(turns,),
        in_specs=[whole, part(CORNERS), part(CORNERS), all_of(rows - 2 * STEPS), all_of(STEPS), all_of(STEPS)],
        out_specs=[part(channels), pl.BlockSpec((some, channels, width), lambda i: (i, 0, 0))],
        memory=32,
    )
    return (result, field.transpose(1, 0, 2))


def exchange(blocks, tiles, share):
    count, channels, lanes = blocks.shape
    if share == lanes:
        return lax.all_to_all(blocks, "tile", split_axis=0, concat_axis=0, tiled=True)
    flat = blocks.transpose(1, 0, 2).reshape(channels, count * lanes)
    flat = lax.all_to_all(flat, "tile", split_axis=1, concat_axis=1, tiled=True)
    return flat.reshape(channels, count, lanes).transpose(1, 0, 2)


def solution(mesh):
    in_specs = (
        P(None, ("group", "tile")),
        P("tile", None),
        P(None, "tile"),
        P("tile"),
        P("tile", None),
    )
    out_specs = (P(None, ("group", "tile")), P(None, ("group", "tile"), None))
    return jax.shard_map(body, mesh=mesh, in_specs=in_specs, out_specs=out_specs, check_vma=False)
```

```python
import functools

import jax
import jax.numpy as jnp
from jax import lax
from jax.experimental import pallas as pl
from jax.experimental.pallas import tpu as pltpu
from jax.sharding import PartitionSpec as P

STEPS = 5
CORNERS = 4
LANES = 128
PLACES = 256
EDGE = STEPS + (STEPS + 1) // 2
BF16 = jnp.bfloat16
F32 = jnp.float32
VMEM = pl.BlockSpec(memory_space=pltpu.VMEM)


def halves(values):
    high = values.astype(BF16)
    return high, (values - high.astype(F32)).astype(BF16)


def one_hot(places, length):
    rows = lax.broadcasted_iota(jnp.int32, (length, places.shape[1]), 0)
    return jnp.where(rows == places, 1.0, 0.0).astype(BF16)


def masked(values, marks, wanted):
    marks = jnp.broadcast_to(marks, values.shape)
    zero = jnp.zeros((), values.dtype)
    return jnp.concatenate([jnp.where(marks == k, values, zero) for k in wanted], 0)


def dot_last(left, right):
    return lax.dot_general(left, right, (((1,), (1,)), ((), ())), preferred_element_type=F32)


def sum_to_slots(inc_ref, slot_ref, weight_ref, sent_ref):
    channels = inc_ref.shape[0]
    count = sent_ref.shape[0] * LANES // PLACES
    inc = inc_ref[...]
    left, right = [], []
    for corner in range(CORNERS):
        slots = slot_ref[corner : corner + 1, :]
        parts = jnp.concatenate(halves(weight_ref[corner : corner + 1, :] * inc), 0)
        left.append(masked(parts, slots // PLACES, range(count)))
        right.append(one_hot(slots % PLACES, PLACES))
    sums = dot_last(jnp.concatenate(left, 1), jnp.concatenate(right, 1))

    @pl.when(pl.program_id(0) == 0)
    def _():
        sent_ref[...] = jnp.zeros_like(sent_ref)

    for k in range(count):
        both = sums[2 * channels * k : 2 * channels * (k + 1)]
        both = both[:channels] + both[channels:]
        for part in range(PLACES // LANES):
            sent_ref[k * (PLACES // LANES) + part] += both[:, LANES * part : LANES * (part + 1)]


def wide_column(width):
    lanes = lax.broadcasted_iota(jnp.int32, (2 * LANES, 1), 0)
    extra = (2 * LANES - width) // 2
    return jnp.where(lanes < width, lanes, jnp.where(lanes < width + extra, lanes - width, lanes - 2 * LANES + width))


def place_edge(edge_ref, rows, coefs, width):
    half = width - LANES
    for k, row in enumerate(rows):
        edge_ref[k] = row[:, :LANES]
    ends = [row[:, LANES:width] for row in rows]
    for k in range(0, STEPS - 1, 2):
        edge_ref[STEPS + k // 2] = jnp.concatenate([ends[k], ends[k + 1]], 1)
    edge_ref[EDGE - 1] = jnp.concatenate([ends[-1], jnp.zeros_like(ends[-1])], 1)
    for k, coef in enumerate(coefs):
        for part in range(3):
            edge_ref[EDGE - 1, 3 * k + part : 3 * k + part + 1, half:] = coef[:, half * part : half * (part + 1)]


def read_edge(edge_ref, k, width):
    half = width - LANES
    start = edge_ref[k]
    end = edge_ref[STEPS + k // 2, :, half * (k % 2) : half * (k % 2) + half]
    return widened([start, end], start, end, width)


def read_coef(edge_ref, k, width):
    half = width - LANES
    parts = [edge_ref[EDGE - 1, 3 * k + part : 3 * k + part + 1, half:] for part in range(3)]
    return widened(parts, parts[0], parts[2], width)


def widened(parts, start, end, width):
    extra = (2 * LANES - width) // 2
    return jnp.concatenate(parts + [start[:, :extra], end[:, end.shape[1] - extra :]], 1)


def cell_sums(rec_ref, cell_ref, ys, width):
    senders, channels, _ = rec_ref.shape
    cells = jnp.concatenate([cell_ref[s : s + 1, :] for s in range(senders)], 1)
    values = jnp.concatenate([rec_ref[s] for s in range(senders)], 1)
    y = cells // width
    right = jnp.where(wide_column(width) == cells - y * width, 1.0, 0.0).astype(BF16)
    sums = dot_last(masked(jnp.concatenate(halves(values), 0), y, ys), right)
    full = []
    for k in range(len(ys)):
        both = sums[2 * channels * k : 2 * channels * (k + 1)]
        full.append(both[:channels] + both[channels:])
    return full


def edge_starts(rows):
    even = lax.axis_index("tile") % 2 == 0
    return jnp.where(even, 0, rows - STEPS), jnp.where(even, rows - STEPS, 0)


def sum_edges(rec_ref, cell_ref, coef_ref, edges_ref, far_ref, near_ref, *, width):
    starts = edge_starts(coef_ref.shape[0])
    ys = [start + k for start in starts for k in range(STEPS)]
    full = cell_sums(rec_ref, cell_ref, ys, width)
    for k, row in enumerate(full):
        edges_ref[k] = row
    for edge_ref, at in ((far_ref, 0), (near_ref, STEPS)):
        coefs = [coef_ref[pl.ds(y, 1), :] for y in ys[at : at + STEPS]]
        place_edge(edge_ref, full[at : at + STEPS], coefs, width)


def stepped(above, here, below, coef):
    wide = here.shape[-1]
    spread = below + above + pltpu.roll(here, 1, 1) + pltpu.roll(here, wide - 1, 1)
    return here + coef * (spread - 4.0 * here)


def kept_rows(turn, total):
    first, last = STEPS + turn, total - STEPS - turn
    return [first, first + 1, last - 2, last - 1]


def read_rows(final_rows, ys, cell_ref, values_ref, base, width):
    senders, channels, _ = values_ref.shape
    left = jnp.concatenate([jnp.concatenate(halves(row), 0) for row in final_rows], 0)
    for s in range(0, senders, 2):
        cells = jnp.concatenate([cell_ref[s : s + 1, :], cell_ref[s + 1 : s + 2, :]], 1)
        y = cells // width
        found = jnp.dot(left, one_hot(cells - y * width, left.shape[1]), preferred_element_type=F32)
        out = base(s)
        marks = jnp.broadcast_to(y, out.shape)
        for k, row in enumerate(ys):
            both = found[2 * channels * k : 2 * channels * (k + 1)]
            out = jnp.where(marks == row, both[:channels] + both[channels:], out)
        values_ref[s] = out[:, :LANES]
        values_ref[s + 1] = out[:, LANES:]


def inner_rows(start_ref, own_ref, kept_ref, one_ref, two_ref, coef_ref, width):
    rows = start_ref.shape[0]
    own = own_ref[...]
    coef_ref[...] = widened([own], own, own, width)
    held, other, last = start_ref, one_ref, two_ref
    for turn in range(1, STEPS + 1):
        for y in range(turn, rows - turn):
            other[y] = stepped(held[y - 1], held[y], held[y + 1], coef_ref[y : y + 1, :])
        if turn < STEPS:
            for place, y in enumerate(kept_rows(turn, rows + 2 * STEPS)):
                kept_ref[turn - 1, place] = other[y - STEPS]
        held, other, last = other, last, other
    return [held[y] for y in range(STEPS, rows - STEPS)]


def side_rows(start_ref, edge_ref, own_ref, kept_ref, one_ref, two_ref, coef_ref, width, first):
    rows = own_ref.shape[0]
    head = first == 0
    flip = lambda ahead, behind: jnp.where(head, ahead, behind)
    for k in range(STEPS):
        place = flip(k, STEPS - 1 - k)
        one_ref[place] = read_edge(edge_ref, k, width)
        coef_ref[pl.ds(place, 1), :] = read_coef(edge_ref, k, width)
        own = own_ref[pl.ds(flip(k, rows - 1 - k), 1), :]
        coef_ref[STEPS + k : STEPS + k + 1, :] = widened([own], own, own, width)
    held, other = one_ref, two_ref
    for turn in range(1, STEPS + 1):

        def row(u):
            if turn == 1 and u >= STEPS:
                return start_ref[flip(u - STEPS, rows - 1 - u + STEPS)]
            if u >= STEPS + turn - 1:
                k = u - STEPS - turn + 1
                return kept_ref[turn - 2, flip(k, 3 - k)]
            return held[u]

        for u in range(turn, turn + STEPS):
            other[u] = stepped(row(u - 1), row(u), row(u + 1), coef_ref[u : u + 1, :])
        held, other = other, held
    return [held[flip(STEPS + k, 2 * STEPS - 1 - k)] for k in range(STEPS)]


def diffuse_most(
    rec_ref, edges_ref, edge_ref, own_ref, cell_ref, start_ref, kept_ref, inner_ref, side_ref, values_ref,
    one_ref, two_ref, coef_ref, side_one_ref, side_two_ref, side_coef_ref, *, width
):
    rows, channels, _ = start_ref.shape
    far, first = edge_starts(rows)
    for k in range(STEPS):
        start_ref[far + k] = edges_ref[k]
        start_ref[first + k] = edges_ref[STEPS + k]
    within = range(STEPS, rows - STEPS)
    for y, row in zip(within, cell_sums(rec_ref, cell_ref, within, width)):
        start_ref[y] = row
    inner = inner_rows(start_ref, own_ref, kept_ref, one_ref, two_ref, coef_ref, width)
    side = side_rows(
        start_ref, edge_ref, own_ref, kept_ref, side_one_ref, side_two_ref, side_coef_ref, width, first
    )
    for k, row in enumerate(inner):
        inner_ref[k] = row
    for k, row in enumerate(side):
        side_ref[k] = row
    ys = list(range(STEPS, rows - STEPS)) + [first + k for k in range(STEPS)]
    nothing = lambda s: jnp.zeros((channels, 2 * LANES), F32)
    read_rows(inner + side, ys, cell_ref, values_ref, nothing, width)


def diffuse_last(
    kept_ref, part_ref, start_ref, edge_ref, own_ref, cell_ref, side_ref, values_ref, one_ref, two_ref, coef_ref, *, width
):
    first, _ = edge_starts(own_ref.shape[0])
    side = side_rows(start_ref, edge_ref, own_ref, kept_ref, one_ref, two_ref, coef_ref, width, first)
    for k, row in enumerate(side):
        side_ref[k] = row
    base = lambda s: jnp.concatenate([part_ref[s], part_ref[s + 1]], 1)
    read_rows(side, [first + k for k in range(STEPS)], cell_ref, values_ref, base, width)


def by_product(table_ref, slot_ref, weight_ref, columns, channels):
    count = table_ref.shape[0] // (2 * channels)
    total = 0.0
    for corner in range(CORNERS):
        slots = slot_ref[corner : corner + 1, columns]
        found = jnp.dot(table_ref[...], one_hot(slots % PLACES, PLACES), preferred_element_type=F32)
        marks = jnp.broadcast_to(slots // PLACES, (channels, slots.shape[1]))
        out = None
        for k in range(count):
            both = found[2 * channels * k : 2 * channels * (k + 1)]
            both = both[:channels] + both[channels:]
            out = both if out is None else jnp.where(marks == k, both, out)
        total = total + weight_ref[corner : corner + 1, columns] * out
    return total


def by_lanes(ret_ref, slot_ref, weight_ref, columns):
    blocks, channels, _ = ret_ref.shape
    group = 8
    totals = [0.0] * (channels // group)
    for corner in range(CORNERS):
        slots = slot_ref[corner : corner + 1, columns]
        weight = weight_ref[corner : corner + 1, columns]
        lanes = jnp.broadcast_to(slots % LANES, (group, LANES))
        block = jnp.broadcast_to(slots // LANES, (group, LANES))
        marks = [block == k for k in range(blocks)]
        for c in range(channels // group):
            out = None
            for k in range(blocks):
                found = jnp.take_along_axis(ret_ref[k, group * c : group * (c + 1), :], lanes, axis=1)
                out = found if out is None else jnp.where(marks[k], found, out)
            totals[c] = totals[c] + weight * out
    return jnp.concatenate(totals, 0)


def sum_from_slots(
    ret_ref, slot_ref, weight_ref, inner_ref, near_ref, far_ref, result_ref, field_ref, table_ref, *, plan
):
    blocks, channels, _ = ret_ref.shape
    some, _, width = field_ref.shape
    inner = inner_ref.shape[0]
    far, _ = edge_starts(inner + 2 * STEPS)
    for k in range(some):
        y = pl.program_id(0) * some + k
        at = jnp.clip(jnp.where(y < STEPS, y, y - STEPS - inner), 0, STEPS - 1)
        is_inner = (y >= STEPS) & (y < STEPS + inner)
        edge = jnp.where((y < STEPS) == (far == 0), far_ref[at], near_ref[at])
        row = jnp.where(is_inner, inner_ref[jnp.clip(y - STEPS, 0, inner - 1)], edge)
        field_ref[k] = row[:, :width]
    group = PLACES // LANES

    @pl.when(pl.program_id(0) == 0)
    def _():
        for k in range(blocks // group):
            both = halves(jnp.concatenate([ret_ref[group * k + part] for part in range(group)], 1))
            table_ref[2 * channels * k : 2 * channels * (k + 1), :] = jnp.concatenate(both, 0)

    at = 0
    for product, single in plan:
        for k in range(single):
            columns = slice(at + k * LANES, at + (k + 1) * LANES)
            result_ref[:, columns] = by_lanes(ret_ref, slot_ref, weight_ref, columns)
        columns = slice(at + single * LANES, at + (single + product) * LANES)
        result_ref[:, columns] = by_product(table_ref, slot_ref, weight_ref, columns, channels)
        at += (product + single) * LANES


def plan_of(blocks):
    return [(blocks - blocks // 3, blocks // 3)]


def chunk_of(fine, most):
    return max(c for c in range(LANES, most + 1, LANES) if fine % c == 0)


def call(kernel, ins, out, scratch=(), grid=(), in_specs=VMEM, out_specs=VMEM, memory=16, cost=None):
    single = isinstance(in_specs, pl.BlockSpec)
    return pl.pallas_call(
        kernel,
        grid=grid,
        out_shape=out,
        in_specs=[in_specs] * len(ins) if single else in_specs,
        out_specs=[out_specs] * len(out) if single and isinstance(out, list) else out_specs,
        scratch_shapes=list(scratch),
        cost_estimate=cost,
        compiler_params=pltpu.CompilerParams(vmem_limit_bytes=memory << 20),
    )(*ins)


def body(increment, send_slots, tent_weight, coarse_cell, diffusivity):
    channels, fine = increment.shape
    slot_count = coarse_cell.shape[0]
    rows, width = diffusivity.shape
    tiles = lax.axis_size("tile")
    share = slot_count // tiles
    blocks = slot_count // LANES
    wide = 2 * LANES
    on_chip = [(i, i ^ 1) for i in range(tiles)]
    off_chip = [(i, (i + 2 * (i % 2) - 1) % tiles) for i in range(tiles)]
    shape = jax.ShapeDtypeStruct
    slots = send_slots.T
    cells = coarse_cell.reshape(blocks, LANES)
    chunk = chunk_of(fine, 3456)
    part = lambda n: pl.BlockSpec((n, chunk), lambda i: (0, i))
    full = lambda n: pl.BlockSpec((n, fine), lambda i: (0, 0))
    whole = pl.BlockSpec((blocks, channels, LANES), lambda i: (0, 0, 0))

    sent = call(
        sum_to_slots,
        (increment, slots, tent_weight),
        shape((blocks, channels, LANES), F32),
        grid=(1,),
        in_specs=[full(channels), full(CORNERS), full(CORNERS)],
        out_specs=whole,
        memory=56,
    )
    received = exchange(sent, tiles, share)
    edge = shape((EDGE, channels, LANES), F32)
    slot_blocks = shape((blocks, channels, LANES), F32)
    edges, far, near = call(
        functools.partial(sum_edges, width=width),
        (received, cells, diffusivity),
        [shape((2 * STEPS, channels, wide), F32), edge, edge],
    )
    far = lax.ppermute(far, "tile", off_chip)
    near = lax.ppermute(near, "tile", on_chip)
    own = pltpu.VMEM((rows, channels, wide), F32)
    ends = shape((STEPS, channels, wide), F32)
    side = pltpu.VMEM((2 * STEPS + 1, channels, wide), F32)
    side_scratch = [side, side, pltpu.VMEM((2 * STEPS, wide), F32)]
    start, kept, inner, near_last, found = call(
        functools.partial(diffuse_most, width=width),
        (received, edges, near, diffusivity, cells),
        [
            shape((rows, channels, wide), F32),
            shape((STEPS - 1, 4, channels, wide), F32),
            shape((rows - 2 * STEPS, channels, wide), F32),
            ends,
            slot_blocks,
        ],
        [own, own, pltpu.VMEM((rows, wide), F32)] + side_scratch,
        cost=pl.CostEstimate(flops=4 * slot_count * wide * wide, bytes_accessed=8 << 20, transcendentals=0),
    )
    far_last, values = call(
        functools.partial(diffuse_last, width=width),
        (kept, found, start, far, diffusivity, cells),
        [ends, slot_blocks],
        side_scratch,
    )
    returned = exchange(values, tiles, share)
    turns = fine // chunk
    some = rows // turns if rows % turns == 0 else rows
    all_of = lambda count: pl.BlockSpec((count, channels, wide), lambda i: (0, 0, 0))
    result, field = call(
        functools.partial(sum_from_slots, plan=plan_of(chunk // LANES)),
        (returned, slots, tent_weight, inner, near_last, far_last),
        [shape((channels, fine), F32), shape((rows, channels, width), F32)],
        [pltpu.VMEM((2 * channels * slot_count // PLACES, PLACES), BF16)],
        grid=(turns,),
        in_specs=[whole, part(CORNERS), part(CORNERS), all_of(rows - 2 * STEPS), all_of(STEPS), all_of(STEPS)],
        out_specs=[part(channels), pl.BlockSpec((some, channels, width), lambda i: (i, 0, 0))],
        memory=32,
    )
    return (result, field.transpose(1, 0, 2))


def exchange(blocks, tiles, share):
    count, channels, lanes = blocks.shape
    if share == lanes:
        return lax.all_to_all(blocks, "tile", split_axis=0, concat_axis=0, tiled=True)
    flat = blocks.transpose(1, 0, 2).reshape(channels, count * lanes)
    flat = lax.all_to_all(flat, "tile", split_axis=1, concat_axis=1, tiled=True)
    return flat.reshape(channels, count, lanes).transpose(1, 0, 2)


def solution(mesh):
    in_specs = (
        P(None, ("group", "tile")),
        P("tile", None),
        P(None, "tile"),
        P("tile"),
        P("tile", None),
    )
    out_specs = (P(None, ("group", "tile")), P(None, ("group", "tile"), None))
    return jax.shard_map(body, mesh=mesh, in_specs=in_specs, out_specs=out_specs, check_vma=False)
```
